32 devices in a mesh: gx: 8 (over y, x, core), gy: 4 (over z).
Axes of the slice: x: 2, y: 2, z: 4, core: 2. Of those that a mesh axis runs over, the one named last changes fastest.
Arguments:
- density: float32 [256, 512, 256], P('gx', 'gy'), as said below
- reaction_rates: float32 [6], replicated, may hold values from 0.3 to 3
- state_changes: int32 [6, 3], replicated, may hold values from -2 to 2, as said below
- target_box: int32 [2, 3], replicated, may hold values from 0 to 512, as said below
- truncation: int32 [2], replicated, may hold values from 5 to 16
Outputs:
- occupancy: float32 [256, 512, 256], P('gx', 'gy')
- summary: float32 [2], replicated
The draws below stay inside these ranges and needn't reach their ends.
Inputs may be any that keep to these rules, and one draw needn't show every extreme that they name: density is positive. `state_changes`: each row is one reaction's change of the three counts; for each of the first two species, some reaction changes it by 2 and some by -2. For each species, target_box[0, d] < target_box[1, d], and target_box[1, d] is at most that species' number of counts; along the species with the most counts the box reaches the lattice's end.
All inputs are finite; a program needn't handle non-finite values.
Results may differ from the reference program's by a relative error of at most 0.0001.
Values sent between devices are 32-bit elements; how exact they have to be, the bound alone decides.
No kernel may reach another device: no remote copies, remote signals or barrier semaphores. Data moves between devices by JAX's collectives and lax.ppermute only.
A program may use at most 256 MiB of HBM per device.

```python
import math
import jax
import jax.numpy as jnp
from jax import lax

NZ = 256
STEPS = 4
REACTIONS = 6
NX = 256
NY = 512


def draw_density(key, part):
    key_first = jax.random.fold_in(key, 0)
    roughness = jnp.exp(jax.random.uniform(key_first, (NX, NY, NZ), jnp.float32, -0.7, 0.7))
    gradient = 1.0 + 2.0 * jnp.arange(NX, dtype=jnp.float32) / (NX - 1)
    return roughness * gradient[:, None, None]


def draw_state_changes(key, part):
    key_list = jax.random.split(key, 3)
    changes = jax.random.randint(key_list[0], (REACTIONS, 3), -2, 3)
    shuffled = jax.random.permutation(key_list[1], REACTIONS)
    direction = 2 * jax.random.randint(key_list[2], (), 0, 2) - 1
    changes = changes.at[shuffled[0], 0].set(2)
    changes = changes.at[shuffled[1], 0].set(-2)
    changes = changes.at[shuffled[2], 1].set(2)
    changes = changes.at[shuffled[3], 1].set(-2)
    changes = changes.at[shuffled[0], 1].set(direction)
    return changes.astype(jnp.int32)


def draw_target_box(key, part):
    key_list = jax.random.split(key, 6)
    extents = (NX, NY, NZ)
    longest = 0
    for axis_number in range(3):
        if extents[axis_number] > extents[longest]:
            longest = axis_number
    lower_bounds = [jax.random.randint(key_list[axis_number], (), 0, extents[axis_number] // 4) for axis_number in range(3)]
    upper_bounds = []
    for axis_number in range(3):
        if axis_number == longest:
            upper_bounds.append(jnp.array(extents[axis_number], jnp.int32))
        else:
            upper_bounds.append(jax.random.randint(key_list[3 + axis_number], (), extents[axis_number] // 2, extents[axis_number] + 1))
    return jnp.stack([jnp.stack(lower_bounds), jnp.stack(upper_bounds)]).astype(jnp.int32)


def setup_inputs(seed: int = 0) -> dict:
    splits = jax.random.split(jax.random.key(seed), 6)
    return {
        "density": draw_density(jax.random.fold_in(splits[5], 71), 0),
        "reaction_rates": jnp.clip(jnp.exp(jax.random.uniform(splits[1], (REACTIONS,), jnp.float32, math.log(0.3), math.log(3.0))), 0.3, 3.0),
        "state_changes": draw_state_changes(jax.random.fold_in(splits[5], 71), 0),
        "target_box": draw_target_box(jax.random.fold_in(splits[5], 71), 0),
        "truncation": jax.random.randint(splits[4], (2,), STEPS + 1, STEPS + 13).astype(jnp.int32),
    }


mean_jumps = 8.0
headroom = 1.05
series_length = 40


def propensity_factor(counts, reactant_order, extent):
    values = counts.astype(jnp.float32)
    linear = values / extent
    square = values * (values - 1.0) / (extent * extent)
    return jnp.where(reactant_order == 0, jnp.ones_like(values), jnp.where(reactant_order == 1, linear, square))


def box_indicator(counts, target_box, axis_number):
    return ((counts >= target_box[0, axis_number]) & (counts < target_box[1, axis_number])).astype(jnp.float32)


def outer_three(along_first, along_second, along_third):
    return along_first[:, None, None] * along_second[None, :, None] * along_third[None, None, :]


def jump_weights(truncation):
    table = [math.exp(-mean_jumps) * mean_jumps ** jump_index / math.factorial(jump_index) for jump_index in range(series_length)]
    weights = [jnp.float32(table[jump_index]) for jump_index in range(STEPS + 1)]
    tails = []
    for which in range(2):
        tail_weight = jnp.float32(0.0)
        for jump_index in range(STEPS + 1, series_length):
            taken = (jump_index <= truncation[which]).astype(jnp.float32)
            tail_weight = tail_weight + taken * jnp.float32(table[jump_index])
        tails.append(tail_weight)
    return weights, tails[0], tails[1]


def reference(density, reaction_rates, state_changes, target_box, truncation):
    extents = (NX, NY, NZ)
    reactant_orders = jnp.maximum(-state_changes, 0)
    count_grids = [jnp.arange(extent, dtype=jnp.int32) for extent in extents]
    inside = [box_indicator(count_grids[axis_number], target_box, axis_number) for axis_number in range(3)]
    box_mask = outer_three(inside[0], inside[1], inside[2])
    factors = [[propensity_factor(count_grids[axis_number], reactant_orders[reaction, axis_number], float(extents[axis_number])) for axis_number in range(3)] for reaction in range(REACTIONS)]
    corner = None
    for reaction in range(REACTIONS):
        corner_term = reaction_rates[reaction]
        for axis_number in range(3):
            last_count = jnp.full((1,), extents[axis_number] - 1, jnp.int32)
            corner_term = corner_term * propensity_factor(last_count, reactant_orders[reaction, axis_number], float(extents[axis_number]))[0]
        corner = corner_term if corner is None else corner + corner_term
    uniform_rate = headroom * corner

    def coefficient(reaction):
        return outer_three(reaction_rates[reaction] * factors[reaction][0], factors[reaction][1], factors[reaction][2])

    total_rate = coefficient(0)
    for reaction in range(1, REACTIONS):
        total_rate = total_rate + coefficient(reaction)

    def advance(current):
        scaled = current * (1.0 - box_mask) / uniform_rate
        advanced = current - total_rate * scaled
        for reaction in range(REACTIONS):
            flux_term = jnp.pad(scaled * coefficient(reaction), 2)
            start = [(2 - state_changes[reaction, axis_number]).astype(jnp.int32) for axis_number in range(3)]
            advanced = advanced + lax.dynamic_slice(flux_term, start, current.shape)
        return advanced

    weights, tail_density, tail_totals = jump_weights(truncation)
    mass_sums = [jnp.sum(density)]
    hit_sums = [jnp.sum(density * box_mask)]
    current = density
    accumulated = weights[0] * density
    for jump_index in range(1, STEPS + 1):
        current = advance(current)
        mass_sums.append(jnp.sum(current))
        hit_sums.append(jnp.sum(current * box_mask))
        accumulated = accumulated + weights[jump_index] * current
    occupancy = accumulated + tail_density * current
    reached = weights[0] * hit_sums[0]
    retained = weights[0] * mass_sums[0]
    for jump_index in range(1, STEPS + 1):
        reached = reached + weights[jump_index] * hit_sums[jump_index]
        retained = retained + weights[jump_index] * mass_sums[jump_index]
    cell_total = float(NX * NY * NZ)
    reached = (reached + tail_totals * hit_sums[STEPS]) / cell_total
    retained = (retained + tail_totals * mass_sums[STEPS]) / cell_total
    return occupancy, jnp.stack([reached, retained])
```

```python
import functools
import math

import jax
import jax.numpy as jnp
from jax import lax
from jax.experimental import pallas as pl
from jax.experimental.pallas import tpu as pltpu
from jax.sharding import PartitionSpec as P

STEPS = 4
REACTIONS = 6
HALO = 2 * STEPS
LANES = 128
ROWS = 16
PAD = 8

mean_jumps = 8.0
headroom = 1.05
series_length = 40

VMEM_LIMIT = 62 << 20


def largest_divisor(number, limit):
    return max(u for u in range(1, limit + 1) if number % u == 0)


def counts_factor(values, order, extent):
    linear = values * (1.0 / extent)
    square = values * (values - 1.0) * (1.0 / (extent * extent))
    return jnp.where(order == 0, 1.0, jnp.where(order == 1, linear, square))


def tables_kernel(
    dims, rates, changes, box, truncation, stay, weights, free, itab, ftab, plain
):
    block_first, block_second, extents, kernel_layers = dims
    rows = block_second + 2 * HALO
    plane = 2 * rows
    layers = block_first + 2 * HALO
    anchor_first = lax.axis_index("gx") * block_first - HALO
    anchor_second = lax.axis_index("gy") * block_second - HALO
    step = pl.program_id(0)

    def order(r, d):
        return jnp.maximum(-changes[r, d], 0)

    @pl.when(step == 0)
    def _():
        corner = jnp.float32(0.0)
        for r in range(REACTIONS):
            term = rates[r]
            for d in range(3):
                e = float(extents[d])
                s = order(r, d)
                term = term * jnp.where(
                    s == 0,
                    1.0,
                    jnp.where(s == 1, (e - 1.0) / e, (e - 1.0) * (e - 2.0) / (e * e)),
                )
            corner = corner + term
        inverse = 1.0 / jnp.full((rows, LANES), headroom * corner, jnp.float32)
        row = lax.broadcasted_iota(jnp.int32, (rows, LANES), 0) + anchor_second
        lane = lax.broadcasted_iota(jnp.int32, (rows, LANES), 1)
        real_row = (row >= 0) & (row < extents[1])
        box_row = (row >= box[0, 1]) & (row < box[1, 1])
        for h in range(2):
            third = 2 * lane + h
            box_here = box_row & (third >= box[0, 2]) & (third < box[1, 2])
            for v in range(3):
                at = pl.ds((v * 2 + h) * rows, rows)
                if v == 2:
                    free[at, :] = jnp.zeros((rows, LANES), jnp.float32)
                elif v == 1:
                    free[at, :] = jnp.where(real_row & ~box_here, 1.0, 0.0)
                else:
                    free[at, :] = jnp.where(real_row, 1.0, 0.0)

            def coefficient(r, carry):
                scale = inverse * rates[r]
                at = pl.ds(pl.multiple_of((r * 2 + h) * rows, 8), rows)
                s1 = order(r, 1)
                s2 = order(r, 2)
                plain[at, :] = (
                    scale
                    * counts_factor(row.astype(jnp.float32), s1, float(extents[1]))
                    * counts_factor(third.astype(jnp.float32), s2, float(extents[2]))
                )
                from_row = row - changes[r, 1]
                from_third = third - changes[r, 2]
                inside = (from_third >= 0) & (from_third < extents[2])
                moved = (
                    scale
                    * counts_factor(from_row.astype(jnp.float32), s1, float(extents[1]))
                    * counts_factor(from_third.astype(jnp.float32), s2, float(extents[2]))
                )
                weights[at, :] = jnp.where(inside, moved, 0.0)
                return carry

            lax.fori_loop(0, REACTIONS, coefficient, 0)
        for which in range(2):
            for r in range(REACTIONS):
                for h in range(2):
                    source = h - changes[r, 2]
                    parity = source & 1
                    turn = source >> 1
                    itab[which * 12 + r * 2 + h] = (
                        PAD
                        + ((turn + 1) * kernel_layers[which] - changes[r, 0]) * plane
                        + parity * rows
                        - changes[r, 1]
                    )

        def layer_scalars(i, carry):
            n0 = anchor_first + i
            real = (n0 >= 0) & (n0 < extents[0])
            in_box = (n0 >= box[0, 0]) & (n0 < box[1, 0])
            itab[24 + i] = jnp.where(real, jnp.where(in_box, 1, 0), 2)
            for r in range(REACTIONS):
                source = (n0 - changes[r, 0]).astype(jnp.float32)
                ftab[i * REACTIONS + r] = counts_factor(source, order(r, 0), float(extents[0]))
            return carry

        lax.fori_loop(0, layers, layer_scalars, 0)
        table = [
            math.exp(-mean_jumps) * mean_jumps**j / math.factorial(j) for j in range(series_length)
        ]
        tails = []
        for which in range(2):
            tail = jnp.float32(0.0)
            for j in range(STEPS + 1, series_length):
                tail = tail + jnp.where(j <= truncation[which], jnp.float32(table[j]), 0.0)
            tails.append(tail)
        base = layers * REACTIONS
        for j in range(STEPS):
            ftab[base + j] = jnp.float32(table[j])
        ftab[base + STEPS] = jnp.float32(table[STEPS]) + tails[0]
        ftab[base + STEPS + 1] = jnp.float32(table[STEPS]) + tails[1]

    chunk = stay.shape[0]

    def group(g, carry):
        row0 = pl.multiple_of(g * ROWS, ROWS)
        terms = [
            [plain[pl.ds((r * 2 + h) * rows + row0, ROWS), :] for h in range(2)]
            for r in range(REACTIONS)
        ]
        for i in range(chunk):
            n0 = anchor_first + step * chunk + i
            kind = itab[24 + step * chunk + i]
            firsts = [
                counts_factor(n0.astype(jnp.float32), order(r, 0), float(extents[0]))
                for r in range(REACTIONS)
            ]
            for h in range(2):
                total = terms[0][h] * firsts[0]
                for r in range(1, REACTIONS):
                    total = total + terms[r][h] * firsts[r]
                mask = free[pl.ds(pl.multiple_of(kind * plane + h * rows + row0, 8), ROWS), :]
                stay[i, h, pl.ds(row0, ROWS), :] = 1.0 - mask * total
        return carry

    lax.fori_loop(0, rows // ROWS, group, 0)


def split_product(values, matrix):
    high = values.astype(jnp.bfloat16)
    low = (values - high.astype(jnp.float32)).astype(jnp.bfloat16)
    return jnp.dot(high, matrix, preferred_element_type=jnp.float32) + jnp.dot(
        low, matrix, preferred_element_type=jnp.float32
    )


def parity_matrix(transposed):
    size = 2 * LANES
    third = lax.broadcasted_iota(jnp.int32, (size, size), 1 if transposed else 0)
    place = lax.broadcasted_iota(jnp.int32, (size, size), 0 if transposed else 1)
    return jnp.where(place == (third & 1) * LANES + (third >> 1), 1.0, 0.0).astype(jnp.bfloat16)


class Lattice:
    def __init__(self, layers, rows, which, itab, ftab, total_layers, weights, free, stay, p, acc, q):
        self.layers, self.rows, self.plane = layers, rows, 2 * rows
        self.which, self.itab, self.ftab = which, itab, ftab
        self.weights, self.free, self.stay = weights, free, stay
        self.p, self.acc, self.q = p, acc, q
        self.weight_base = total_layers * REACTIONS
        self.never = jnp.full((ROWS, LANES), itab[24], jnp.int32) < 0

    def moved(self, turn, row):
        return PAD + (turn + 1) * self.layers * self.plane + row

    def ingest(self, values, local, table_layer, row0, count):
        w0 = self.ftab[self.weight_base]
        kind = self.itab[24 + table_layer]
        for h in range(2):
            part = values[:, h * LANES : (h + 1) * LANES]
            at = pl.multiple_of(local * self.plane + h * self.rows + row0, 8)
            self.p[pl.ds(at, count), :] = part
            self.acc[pl.ds(at, count), :] = part * w0
            mask = self.free[
                pl.ds(pl.multiple_of(kind * self.plane + h * self.rows + row0, 8), count), :
            ]
            masked = part * mask
            self.q[0][pl.ds(pl.multiple_of(self.moved(0, at), 8), count), :] = masked
            self.q[0][pl.ds(pl.multiple_of(self.moved(-1, at), 8), count), :] = pltpu.roll(
                masked, 1, 1
            )
            self.q[0][pl.ds(pl.multiple_of(self.moved(1, at), 8), count), :] = pltpu.roll(
                masked, LANES - 1, 1
            )

    def arrivals(self, source, local0, u, row0, h, start, coefficients, firsts):
        total = start
        shift = local0 * self.plane + row0
        for r in range(REACTIONS):
            at = self.itab[self.which * 12 + r * 2 + h] + shift + u * self.plane
            total = total + source[pl.ds(at, ROWS), :] * coefficients[r][h] * firsts[r]
        return total

    def coefficients(self, row0):
        return [
            [
                self.weights[pl.ds(pl.multiple_of((r * 2 + h) * self.rows + row0, 8), ROWS), :]
                for h in range(2)
            ]
            for r in range(REACTIONS)
        ]

    def advance(self, k, unroll, blocks, block_start):
        source, target = self.q[(k - 1) % 2], self.q[k % 2]
        weight = self.ftab[self.weight_base + k]
        plane, rows = self.plane, self.rows

        def roll_block(before, u, h):
            at = pl.multiple_of(before + u * plane + h * rows, 8)
            values = target[pl.ds(pl.multiple_of(self.moved(0, at), 8), ROWS), :]
            return (pltpu.roll(values, 1, 1), pltpu.roll(values, LANES - 1, 1))

        def store_block(before, u, h, pair):
            at = pl.multiple_of(before + u * plane + h * rows, 8)
            target[pl.ds(pl.multiple_of(self.moved(-1, at), 8), ROWS), :] = pair[0]
            target[pl.ds(pl.multiple_of(self.moved(1, at), 8), ROWS), :] = pair[1]

        def group(g, before):
            row0 = pl.multiple_of(g * ROWS, ROWS)
            coefficients = self.coefficients(row0)

            def block(b, before):
                local0, table0 = block_start(b)
                rolled = [[roll_block(before, u, h) for h in range(2)] for u in range(unroll)]
                results = []
                for u in range(unroll):
                    kind = self.itab[24 + table0 + u]
                    firsts = [self.ftab[(table0 + u) * REACTIONS + r] for r in range(REACTIONS)]
                    for h in range(2):
                        at = pl.multiple_of((local0 + u) * plane + h * rows + row0, 8)
                        value = self.p[pl.ds(at, ROWS), :]
                        if u > 0:
                            value = jnp.where(self.never, rolled[u - 1][h][0], value)
                        value = value * self.stay[pl.ds(at, ROWS), :]
                        value = self.arrivals(
                            source, local0, u, row0, h, value, coefficients, firsts
                        )
                        mask = self.free[
                            pl.ds(pl.multiple_of(kind * plane + h * rows + row0, 8), ROWS), :
                        ]
                        total = self.acc[pl.ds(at, ROWS), :] + value * weight
                        results.append((at, value, value * mask, total))
                for at, value, masked, total in results:
                    self.p[pl.ds(at, ROWS), :] = value
                    self.acc[pl.ds(at, ROWS), :] = total
                    target[pl.ds(pl.multiple_of(self.moved(0, at), 8), ROWS), :] = masked
                for u in range(unroll):
                    for h in range(2):
                        store_block(before, u, h, rolled[u][h])
                return pl.multiple_of(local0 * plane + row0, 8)

            return lax.fori_loop(0, blocks, block, before)

        first = pl.multiple_of(block_start(0)[0] * plane, 8)
        last = lax.fori_loop(0, rows // ROWS, group, first)
        pairs = [[roll_block(last, u, h) for h in range(2)] for u in range(unroll)]
        for u in range(unroll):
            for h in range(2):
                store_block(last, u, h, pairs[u][h])

    def finish(self, unroll, blocks, block_start):
        source = self.q[(STEPS - 1) % 2]
        weight_density = self.ftab[self.weight_base + STEPS]
        weight_totals = self.ftab[self.weight_base + STEPS + 1]
        plane, rows = self.plane, self.rows

        def group(g, sums):
            row0 = pl.multiple_of(g * ROWS + HALO, 8)
            coefficients = self.coefficients(row0)

            def block(b, sums):
                mass, hit = sums
                local0, table0 = block_start(b)
                results = []
                for u in range(unroll):
                    kind = self.itab[24 + table0 + u]
                    firsts = [self.ftab[(table0 + u) * REACTIONS + r] for r in range(REACTIONS)]
                    for h in range(2):
                        at = pl.multiple_of((local0 + u) * plane + h * rows + row0, 8)
                        value = self.p[pl.ds(at, ROWS), :] * self.stay[pl.ds(at, ROWS), :]
                        value = self.arrivals(
                            source, local0, u, row0, h, value, coefficients, firsts
                        )
                        mask = self.free[
                            pl.ds(pl.multiple_of(kind * plane + h * rows + row0, 8), ROWS), :
                        ]
                        so_far = self.acc[pl.ds(at, ROWS), :]
                        totals = so_far + value * weight_totals
                        mass = mass + totals
                        hit = hit + totals * (1.0 - mask)
                        results.append((at, so_far + value * weight_density))
                for at, total in results:
                    self.acc[pl.ds(at, ROWS), :] = total
                return mass, hit

            return lax.fori_loop(0, blocks, block, sums)

        zero = jnp.zeros((ROWS, LANES), jnp.float32)
        return lax.fori_loop(0, (rows - 2 * HALO) // ROWS, group, (zero, zero))

    def restore(self, local, out, index, matrix):
        own = self.rows - 2 * HALO
        even = self.acc[pl.ds(pl.multiple_of(local * self.plane + HALO, 8), own), :]
        odd = self.acc[pl.ds(pl.multiple_of(local * self.plane + self.rows + HALO, 8), own), :]
        out[index] = split_product(jnp.concatenate([even, odd], axis=1), matrix)


def copy_all(copies):
    for copy in copies:
        copy.start()
    return copies


def wait_all(copies):
    for copy in copies:
        copy.wait()


def interior_kernel(
    dims,
    density, below, above, stay_all, weights, free, itab, ftab,
    occupancy, q_edges, p_edges, acc_edges, sums,
    p, acc, q0, q1, stay, block, staged, sem_in, sem_stay, sem_edges, sem_out,
):
    block_first, block_second, _, _ = dims
    rows = block_second + 2 * HALO
    plane = 2 * rows
    chunk = 8
    chunks = block_first // chunk
    lattice = Lattice(
        block_first, rows, 0, itab, ftab, block_first + 2 * HALO, weights, free, stay, p, acc, (q0, q1)
    )
    loads = copy_all(
        [
            pltpu.make_async_copy(
                density.at[pl.ds(c * chunk, chunk)], block.at[pl.ds(c * chunk, chunk)], sem_in.at[c]
            )
            for c in range(chunks)
        ]
    )
    stay_copy = pltpu.make_async_copy(
        stay_all.at[pl.ds(HALO * plane, block_first * plane)], stay, sem_stay
    )
    stay_copy.start()
    spread = parity_matrix(False)
    for c in range(chunks):
        loads[c].wait()

        def layer(i, carry):
            local = c * chunk + i
            for part, row0, count in (
                (below[local], 0, HALO),
                (block[local], HALO, block_second),
                (above[local], HALO + block_second, HALO),
            ):
                lattice.ingest(split_product(part, spread), local, local + HALO, row0, count)
            return carry

        lax.fori_loop(0, chunk, layer, 0)
    stay_copy.wait()

    edges = []

    def export(k):
        q = (q0, q1)[k % 2]
        for side in range(2):
            layer = 2 * k if side == 0 else block_first - 2 * k - 4
            for turn in (-1, 0, 1):
                edges.append(
                    pltpu.make_async_copy(
                        q.at[pl.ds(lattice.moved(turn, layer * plane), 4 * plane)],
                        q_edges.at[k, side, turn + 1],
                        sem_edges.at[(k * 2 + side) * 4 + turn + 1],
                    )
                )
                edges[-1].start()
            layer = 2 * k if side == 0 else block_first - 2 * k - 2
            edges.append(
                pltpu.make_async_copy(
                    p.at[pl.ds(layer * plane, 2 * plane)],
                    p_edges.at[k, side],
                    sem_edges.at[(k * 2 + side) * 4 + 3],
                )
            )
            edges[-1].start()

    export(0)
    for k in range(1, STEPS):
        low, high = 2 * k, block_first - 2 * k
        unroll = largest_divisor(high - low, 10)

        def block_start(b, low=low, unroll=unroll):
            return low + b * unroll, low + b * unroll + HALO

        lattice.advance(k, unroll, (high - low) // unroll, block_start)
        export(k)
    for side in range(2):
        layer = 0 if side == 0 else block_first - HALO
        edges.append(
            pltpu.make_async_copy(
                acc.at[pl.ds(layer * plane, HALO * plane)], acc_edges.at[side], sem_edges.at[32 + side]
            )
        )
        edges[-1].start()
    inner = block_first - 2 * HALO
    unroll = largest_divisor(inner, 8)
    mass, hit = lattice.finish(
        unroll, inner // unroll, lambda b: (HALO + b * unroll, 2 * HALO + b * unroll)
    )
    sums[pl.ds(0, ROWS), :] = mass
    sums[pl.ds(ROWS, ROWS), :] = hit
    gather = parity_matrix(True)

    def layer(i, carry):
        lattice.restore(HALO + i, staged, i, gather)
        return carry

    lax.fori_loop(0, inner, layer, 0)
    out = pltpu.make_async_copy(staged, occupancy.at[pl.ds(HALO, inner)], sem_out)
    out.start()
    out.wait()
    wait_all(edges)


def edges_kernel(
    dims, devices,
    halo_low, halo_high, corner_low, corner_high, stay_all, q_edges, p_edges, acc_edges, sums_in,
    weights, free, itab, ftab, occupancy_in,
    occupancy, row_out,
    p, acc, q0, q1, stay, staged, sem_q, sem_p, sem_other, sem_out,
):
    block_first, block_second, _, _ = dims
    rows = block_second + 2 * HALO
    plane = 2 * rows
    side_layers = 2 * HALO + 2
    right_table = block_first - 2
    lattice = Lattice(
        2 * side_layers, rows, 1, itab, ftab, block_first + 2 * HALO, weights, free, stay, p, acc,
        (q0, q1),
    )
    copies = []
    for side in range(2):
        table = 0 if side == 0 else right_table
        copies.append(
            pltpu.make_async_copy(
                stay_all.at[pl.ds(table * plane, side_layers * plane)],
                stay.at[pl.ds(side * side_layers * plane, side_layers * plane)],
                sem_other.at[side],
            )
        )
        layer = HALO if side == 0 else side_layers + 2
        copies.append(
            pltpu.make_async_copy(
                acc_edges.at[side], acc.at[pl.ds(layer * plane, HALO * plane)], sem_other.at[2 + side]
            )
        )
        for k in range(STEPS):
            layer = 2 * k + HALO if side == 0 else side_layers + 6 - 2 * k
            for turn in (-1, 0, 1):
                copies.append(
                    pltpu.make_async_copy(
                        q_edges.at[k, side, turn + 1],
                        (q0, q1)[k % 2].at[pl.ds(lattice.moved(turn, layer * plane), 4 * plane)],
                        sem_q.at[(k * 2 + side) * 3 + turn + 1],
                    )
                )
            layer = 2 * k + HALO if side == 0 else side_layers + 8 - 2 * k
            copies.append(
                pltpu.make_async_copy(
                    p_edges.at[k, side], p.at[pl.ds(layer * plane, 2 * plane)], sem_p.at[k * 2 + side]
                )
            )
    copy_all(copies)
    spread = parity_matrix(False)
    for side, main, corner in ((0, halo_low, corner_low), (1, halo_high, corner_high)):

        def layer(i, carry, side=side, main=main, corner=corner):
            local = i if side == 0 else side_layers + 10 + i
            table = i if side == 0 else block_first + HALO + i
            for part, row0, count in (
                (corner[i, pl.ds(0, HALO)], 0, HALO),
                (main[i], HALO, block_second),
                (corner[i, pl.ds(HALO, HALO)], HALO + block_second, HALO),
            ):
                lattice.ingest(split_product(part, spread), local, table, row0, count)
            return carry

        lax.fori_loop(0, HALO, layer, 0)
    wait_all(copies)

    def starts(k):
        def block_start(b):
            return (
                2 * k + b * (side_layers + 10 - 4 * k),
                2 * k + b * (block_first + HALO - 4 * k),
            )

        return block_start

    for k in range(1, STEPS):
        lattice.advance(k, HALO, 2, starts(k))
    mass, hit = lattice.finish(HALO, 2, starts(STEPS))
    gather = parity_matrix(True)
    outs = []
    for side in range(2):

        def layer(i, carry, side=side):
            local = HALO + i if side == 0 else side_layers + 2 + i
            lattice.restore(local, staged, side * HALO + i, gather)
            return carry

        lax.fori_loop(0, HALO, layer, 0)
        outs.append(
            pltpu.make_async_copy(
                staged.at[pl.ds(side * HALO, HALO)],
                occupancy.at[pl.ds(0 if side == 0 else block_first - HALO, HALO)],
                sem_out.at[side],
            )
        )
        outs[-1].start()
    mass = jnp.sum(mass + sums_in[pl.ds(0, ROWS), :])
    hit = jnp.sum(hit + sums_in[pl.ds(ROWS, ROWS), :])
    lane = lax.broadcasted_iota(jnp.int32, (devices, LANES), 1)
    row_out[...] = jnp.where(lane == 0, hit, jnp.where(lane == 1, mass, 0.0))
    wait_all(outs)


def body(density, reaction_rates, state_changes, target_box, truncation):
    block_first, block_second, species_third = density.shape
    extents = (
        block_first * lax.axis_size("gx"),
        block_second * lax.axis_size("gy"),
        species_third,
    )
    count_first, count_second = lax.axis_size("gx"), lax.axis_size("gy")
    devices = count_first * count_second
    rows = block_second + 2 * HALO
    plane = 2 * rows
    layers = block_first + 2 * HALO
    side_layers = 2 * HALO + 2
    dims = (block_first, block_second, extents, (block_first, 2 * side_layers))

    def to_next(x, axis, count):
        return lax.ppermute(x, axis, [(i, i + 1) for i in range(count - 1)])

    def to_previous(x, axis, count):
        return lax.ppermute(x, axis, [(i + 1, i) for i in range(count - 1)])

    below = to_next(density[:, -HALO:], "gy", count_second)
    above = to_previous(density[:, :HALO], "gy", count_second)
    halo_low = to_next(density[-HALO:], "gx", count_first)
    halo_high = to_previous(density[:HALO], "gx", count_first)
    corner_low = to_next(
        jnp.concatenate([below[-HALO:], above[-HALO:]], axis=1), "gx", count_first
    )
    corner_high = to_previous(
        jnp.concatenate([below[:HALO], above[:HALO]], axis=1), "gx", count_first
    )

    f32 = jnp.float32
    smem = pl.BlockSpec(memory_space=pltpu.SMEM)
    vmem = pl.BlockSpec(memory_space=pltpu.VMEM)
    hbm = pl.BlockSpec(memory_space=pl.ANY)
    params = pltpu.CompilerParams(vmem_limit_bytes=VMEM_LIMIT)
    chunk = largest_divisor(layers, 8)

    stay, weights, free, itab, ftab = pl.pallas_call(
        functools.partial(tables_kernel, dims),
        grid=(layers // chunk,),
        out_shape=(
            jax.ShapeDtypeStruct((layers, 2, rows, LANES), f32),
            jax.ShapeDtypeStruct((12 * rows, LANES), f32),
            jax.ShapeDtypeStruct((6 * rows, LANES), f32),
            jax.ShapeDtypeStruct((24 + layers,), jnp.int32),
            jax.ShapeDtypeStruct((layers * REACTIONS + 8,), f32),
        ),
        in_specs=[smem] * 4,
        out_specs=(
            pl.BlockSpec((chunk, 2, rows, LANES), lambda i: (i, 0, 0, 0)),
            pl.BlockSpec((12 * rows, LANES), lambda i: (0, 0)),
            pl.BlockSpec((6 * rows, LANES), lambda i: (0, 0)),
            smem,
            smem,
        ),
        scratch_shapes=[pltpu.VMEM((12 * rows, LANES), f32)],
        compiler_params=params,
        name="tables",
    )(reaction_rates, state_changes, target_box, truncation)
    stay = stay.reshape(layers * plane, LANES)

    def scratch(local_layers):
        return [
            pltpu.VMEM((local_layers * plane, LANES), f32),
            pltpu.VMEM((local_layers * plane, LANES), f32),
            pltpu.VMEM((3 * local_layers * plane + 2 * PAD, LANES), f32),
            pltpu.VMEM((3 * local_layers * plane + 2 * PAD, LANES), f32),
            pltpu.VMEM((local_layers * plane, LANES), f32),
        ]

    chunks = block_first // 8
    occupancy, q_edges, p_edges, acc_edges, sums = pl.pallas_call(
        functools.partial(interior_kernel, dims),
        out_shape=(
            jax.ShapeDtypeStruct(density.shape, f32),
            jax.ShapeDtypeStruct((STEPS, 2, 3, 4 * plane, LANES), f32),
            jax.ShapeDtypeStruct((STEPS, 2, 2 * plane, LANES), f32),
            jax.ShapeDtypeStruct((2, HALO * plane, LANES), f32),
            jax.ShapeDtypeStruct((2 * ROWS, LANES), f32),
        ),
        in_specs=[hbm, vmem, vmem, hbm, vmem, vmem, smem, smem],
        out_specs=(hbm, hbm, hbm, hbm, vmem),
        scratch_shapes=scratch(block_first)
        + [
            pltpu.VMEM((block_first, block_second, species_third), f32),
            pltpu.VMEM((block_first - 2 * HALO, block_second, species_third), f32),
            pltpu.SemaphoreType.DMA((chunks,)),
            pltpu.SemaphoreType.DMA,
            pltpu.SemaphoreType.DMA((34,)),
            pltpu.SemaphoreType.DMA,
        ],
        compiler_params=params,
        cost_estimate=pl.CostEstimate(flops=400_000_000, bytes_accessed=40_000_000, transcendentals=0),
        name="interior",
    )(density, below, above, stay, weights, free, itab, ftab)

    occupancy, row = pl.pallas_call(
        functools.partial(edges_kernel, dims, devices),
        out_shape=(
            jax.ShapeDtypeStruct(density.shape, f32),
            jax.ShapeDtypeStruct((devices, LANES), f32),
        ),
        in_specs=[vmem] * 4 + [hbm] * 4 + [vmem] * 3 + [smem] * 2 + [hbm],
        out_specs=(hbm, vmem),
        scratch_shapes=scratch(2 * side_layers)
        + [
            pltpu.VMEM((2 * HALO, block_second, species_third), f32),
            pltpu.SemaphoreType.DMA((24,)),
            pltpu.SemaphoreType.DMA((8,)),
            pltpu.SemaphoreType.DMA((4,)),
            pltpu.SemaphoreType.DMA((2,)),
        ],
        input_output_aliases={13: 0},
        compiler_params=params,
        name="edges",
    )(
        halo_low, halo_high, corner_low, corner_high, stay, q_edges, p_edges, acc_edges, sums,
        weights, free, itab, ftab, occupancy,
    )
    rows_in = lax.all_to_all(row, ("gx", "gy"), 0, 0, tiled=True)
    summary = jnp.sum(rows_in[:, :2], axis=0) * (1.0 / math.prod(extents))
    return occupancy, summary


def solution(mesh):
    placed = (P("gx", "gy", None), P(), P(), P(), P())
    return jax.shard_map(
        body, mesh=mesh, in_specs=placed, out_specs=(P("gx", "gy", None), P()), check_vma=False
    )
```

```python
import functools
import math

import jax
import jax.numpy as jnp
from jax import lax
from jax.experimental import pallas as pl
from jax.experimental.pallas import tpu as pltpu
from jax.sharding import PartitionSpec as P

STEPS = 4
REACTIONS = 6
HALO = 2 * STEPS
LANES = 128
ROWS = 16
PAD = 8
BODY_LAYERS = 14

mean_jumps = 8.0
headroom = 1.05
series_length = 40

VMEM_LIMIT = 62 << 20


KINDS = 24


def largest_divisor(number, limit):
    return max(u for u in range(1, limit + 1) if number % u == 0)


def counts_factor(values, order, extent):
    linear = values * (1.0 / extent)
    square = values * (values - 1.0) * (1.0 / (extent * extent))
    return jnp.where(order == 0, 1.0, jnp.where(order == 1, linear, square))


def tables_kernel(
    dims, rates, changes, box, truncation, stay, weights, free, itab, ftab, plain
):
    block_first, block_second, extents, kernel_layers = dims
    rows = block_second + 2 * HALO
    plane = 2 * rows
    layers = block_first + 2 * HALO
    anchor_first = lax.axis_index("gx") * block_first - HALO
    anchor_second = lax.axis_index("gy") * block_second - HALO
    step = pl.program_id(0)

    def order(r, d):
        return jnp.maximum(-changes[r, d], 0)

    @pl.when(step == 0)
    def _():
        corner = jnp.float32(0.0)
        for r in range(REACTIONS):
            term = rates[r]
            for d in range(3):
                e = float(extents[d])
                s = order(r, d)
                term = term * jnp.where(
                    s == 0,
                    1.0,
                    jnp.where(s == 1, (e - 1.0) / e, (e - 1.0) * (e - 2.0) / (e * e)),
                )
            corner = corner + term
        inverse = 1.0 / jnp.full((rows, LANES), headroom * corner, jnp.float32)
        row = lax.broadcasted_iota(jnp.int32, (rows, LANES), 0) + anchor_second
        lane = lax.broadcasted_iota(jnp.int32, (rows, LANES), 1)
        real_row = (row >= 0) & (row < extents[1])
        box_row = (row >= box[0, 1]) & (row < box[1, 1])
        for h in range(2):
            third = 2 * lane + h
            box_here = box_row & (third >= box[0, 2]) & (third < box[1, 2])
            for v in range(3):
                at = pl.ds((v * 2 + h) * rows, rows)
                if v == 2:
                    free[at, :] = jnp.zeros((rows, LANES), jnp.float32)
                elif v == 1:
                    free[at, :] = jnp.where(real_row & ~box_here, 1.0, 0.0)
                else:
                    free[at, :] = jnp.where(real_row, 1.0, 0.0)

            def coefficient(r, carry):
                scale = inverse * rates[r]
                at = pl.ds(pl.multiple_of((r * 2 + h) * rows, 8), rows)
                s1 = order(r, 1)
                s2 = order(r, 2)
                plain[at, :] = (
                    scale
                    * counts_factor(row.astype(jnp.float32), s1, float(extents[1]))
                    * counts_factor(third.astype(jnp.float32), s2, float(extents[2]))
                )
                from_row = row - changes[r, 1]
                from_third = third - changes[r, 2]
                inside = (from_third >= 0) & (from_third < extents[2])
                moved = (
                    scale
                    * counts_factor(from_row.astype(jnp.float32), s1, float(extents[1]))
                    * counts_factor(from_third.astype(jnp.float32), s2, float(extents[2]))
                )
                weights[at, :] = jnp.where(inside, moved, 0.0)
                return carry

            lax.fori_loop(0, REACTIONS, coefficient, 0)
        for which in range(2):
            for r in range(REACTIONS):
                for h in range(2):
                    source = h - changes[r, 2]
                    parity = source & 1
                    turn = source >> 1
                    itab[which * 12 + r * 2 + h] = (
                        PAD
                        + ((turn + 1) * kernel_layers[which] - changes[r, 0]) * plane
                        + parity * rows
                        - changes[r, 1]
                    )

        def layer_scalars(i, carry):
            n0 = anchor_first - 2 + i
            real = (n0 >= 0) & (n0 < extents[0])
            in_box = (n0 >= box[0, 0]) & (n0 < box[1, 0])
            itab[KINDS + i] = jnp.where(real, jnp.where(in_box, 1, 0), 2)
            for r in range(REACTIONS):
                source = (n0 - changes[r, 0]).astype(jnp.float32)
                ftab[i * REACTIONS + r] = counts_factor(source, order(r, 0), float(extents[0]))
            return carry

        lax.fori_loop(0, layers + 4, layer_scalars, 0)
        table = [
            math.exp(-mean_jumps) * mean_jumps**j / math.factorial(j) for j in range(series_length)
        ]
        tails = []
        for which in range(2):
            tail = jnp.float32(0.0)
            for j in range(STEPS + 1, series_length):
                tail = tail + jnp.where(j <= truncation[which], jnp.float32(table[j]), 0.0)
            tails.append(tail)
        base = (layers + 4) * REACTIONS
        for j in range(STEPS):
            ftab[base + j] = jnp.float32(table[j])
        ftab[base + STEPS] = jnp.float32(table[STEPS]) + tails[0]
        ftab[base + STEPS + 1] = jnp.float32(table[STEPS]) + tails[1]

    chunk = stay.shape[0]

    def group(g, carry):
        row0 = pl.multiple_of(g * ROWS, ROWS)
        terms = [
            [plain[pl.ds((r * 2 + h) * rows + row0, ROWS), :] for h in range(2)]
            for r in range(REACTIONS)
        ]
        for i in range(chunk):
            entry = step * chunk + i + 2
            kind = itab[KINDS + entry]
            firsts = [
                ftab[(entry + changes[r, 0]) * REACTIONS + r] for r in range(REACTIONS)
            ]
            for h in range(2):
                total = terms[0][h] * firsts[0]
                for r in range(1, REACTIONS):
                    total = total + terms[r][h] * firsts[r]
                mask = free[pl.ds(pl.multiple_of(kind * plane + h * rows + row0, 8), ROWS), :]
                stay[i, h, pl.ds(row0, ROWS), :] = 1.0 - mask * total
        return carry

    lax.fori_loop(0, rows // ROWS, group, 0)


def split_product(values, matrix):
    high = values.astype(jnp.bfloat16)
    low = (values - high.astype(jnp.float32)).astype(jnp.bfloat16)
    return jnp.dot(high, matrix, preferred_element_type=jnp.float32) + jnp.dot(
        low, matrix, preferred_element_type=jnp.float32
    )


def parity_matrix(transposed):
    size = 2 * LANES
    third = lax.broadcasted_iota(jnp.int32, (size, size), 1 if transposed else 0)
    place = lax.broadcasted_iota(jnp.int32, (size, size), 0 if transposed else 1)
    return jnp.where(place == (third & 1) * LANES + (third >> 1), 1.0, 0.0).astype(jnp.bfloat16)


class Segment:
    def __init__(self, count, own, table, source, target, totals):
        self.count, self.own, self.table = count, own, table
        self.source, self.target, self.totals = source, target, totals


class Lattice:
    def __init__(self, rows, which, itab, ftab, table_layers, weights, free, stay, p, acc, moved_layers):
        self.rows, self.plane = rows, 2 * rows
        self.which, self.itab, self.ftab = which, itab, ftab
        self.weights, self.free, self.stay = weights, free, stay
        self.p, self.acc, self.moved_layers = p, acc, moved_layers
        self.weight_base = (table_layers + 4) * REACTIONS
        self.never = jnp.full((ROWS, LANES), itab[KINDS], jnp.int32) < 0

    def moved(self, turn, row):
        return PAD + (turn + 1) * self.moved_layers * self.plane + row

    def kind(self, table):
        return self.itab[KINDS + 2 + table]

    def first(self, table, r):
        return self.ftab[(table + 2) * REACTIONS + r]

    def mask(self, kind, h, row0, count):
        at = pl.multiple_of(kind * self.plane + h * self.rows + row0, 8)
        return self.free[pl.ds(at, count), :]

    def ingest(self, q, values, local, table, target, totals):
        kind = self.kind(table)
        rows = self.rows
        for h in range(2):
            part = values[:, h * LANES : (h + 1) * LANES]
            at = pl.multiple_of(local * self.plane + h * rows, 8)
            self.p[pl.ds(at, rows), :] = part
            if totals is not None:
                at = pl.multiple_of(totals * self.plane + h * rows, 8)
                self.acc[pl.ds(at, rows), :] = part * self.ftab[self.weight_base]
            masked = part * self.mask(kind, h, 0, rows)
            at = target * self.plane + h * rows
            for turn in (0, -1, 1):
                lanes = masked if turn == 0 else pltpu.roll(masked, 1 if turn < 0 else LANES - 1, 1)
                q[pl.ds(pl.multiple_of(self.moved(turn, at), 8), rows), :] = lanes

    def coefficients(self, row0):
        return [
            [
                self.weights[pl.ds(pl.multiple_of((r * 2 + h) * self.rows + row0, 8), ROWS), :]
                for h in range(2)
            ]
            for r in range(REACTIONS)
        ]

    def places(self, segments, row0):
        found = []
        for segment in segments:
            own = segment.own * self.plane + row0
            target = segment.target * self.plane + row0
            totals = None if segment.totals is None else segment.totals * self.plane + row0
            shift = segment.source * self.plane + row0
            sources = [
                [self.itab[self.which * 12 + r * 2 + h] + shift for h in range(2)]
                for r in range(REACTIONS)
            ]
            for u in range(segment.count):
                found.append((segment, u, own, target, totals, sources))
        return found

    def value(self, source, place, h, coefficients, firsts, rolled=None):
        segment, u, own, _, _, sources = place
        at = pl.multiple_of(own + u * self.plane + h * self.rows, 8)
        value = self.p[pl.ds(at, ROWS), :]
        if rolled is not None:
            value = jnp.where(self.never, rolled, value)
        value = value * self.stay[pl.ds(at, ROWS), :]
        for r in range(REACTIONS):
            arriving = source[pl.ds(sources[r][h] + u * self.plane, ROWS), :]
            value = value + arriving * coefficients[r][h] * firsts[r]
        return at, value

    def advance(self, k, source, target, blocks, layout, has_totals=None):
        weight = self.ftab[self.weight_base + k]
        plane, rows = self.plane, self.rows
        counts = [segment.count for segment in layout(0)]
        size = sum(counts)
        offsets = [(s, u) for s, count in enumerate(counts) for u in range(count)]
        lag = min(5, size // 3)

        def center_row(before, index, h):
            s, u = offsets[index]
            return before[s] + u * plane + h * rows

        def roll_layer(before, index):
            pairs = []
            for h in range(2):
                at = self.moved(0, center_row(before, index, h))
                values = target[pl.ds(pl.multiple_of(at, 8), ROWS), :]
                pairs.append((pltpu.roll(values, 1, 1), pltpu.roll(values, LANES - 1, 1)))
            return pairs

        def store_layer(before, index, pairs):
            for h in range(2):
                row = center_row(before, index, h)
                for side, turn in enumerate((-1, 1)):
                    at = pl.multiple_of(self.moved(turn, row), 8)
                    target[pl.ds(at, ROWS), :] = pairs[h][side]

        def group(g, before):
            row0 = pl.multiple_of(g * ROWS, ROWS)
            coefficients = self.coefficients(row0)

            def block(b, before):
                places = self.places(layout(b), row0)
                rolled = [roll_layer(before, index) for index in range(size)]
                stored = 0
                for index, place in enumerate(places):
                    segment, u, own, target0, totals0, _ = place
                    table = segment.table + u
                    kind = self.kind(table)
                    firsts = [self.first(table, r) for r in range(REACTIONS)]
                    ready = -1
                    if index >= lag:
                        ready = ((index - lag + 1) * size + size - lag - 1) // (size - lag) - 1
                    for h in range(2):
                        at, value = self.value(
                            source, place, h, coefficients, firsts,
                            rolled[ready][1][h] if ready >= 0 else None,
                        )
                        self.p[pl.ds(at, ROWS), :] = value
                        masked = value * self.mask(kind, h, row0, ROWS)
                        row = target0 + u * plane + h * rows
                        target[pl.ds(pl.multiple_of(self.moved(0, row), 8), ROWS), :] = masked
                        if has_totals is None or has_totals[index]:
                            row = pl.multiple_of(totals0 + u * plane + h * rows, 8)
                            self.acc[pl.ds(row, ROWS), :] = (
                                self.acc[pl.ds(row, ROWS), :] + value * weight
                            )
                    while stored <= ready:
                        store_layer(before, stored, rolled[stored])
                        stored += 1
                while stored < size:
                    store_layer(before, stored, rolled[stored])
                    stored += 1
                return tuple(
                    pl.multiple_of(jnp.int32(segment.target * plane) + row0, 8)
                    for segment in layout(b)
                )

            return lax.fori_loop(0, blocks, block, before)

        before = tuple(jnp.int32(segment.target * plane) for segment in layout(jnp.int32(0)))
        last = lax.fori_loop(0, rows // ROWS, group, before)
        for index in range(size):
            store_layer(last, index, roll_layer(last, index))

    def finish(self, source, blocks, layout):
        weight_density = self.ftab[self.weight_base + STEPS]
        weight_totals = self.ftab[self.weight_base + STEPS + 1]

        def group(g, sums):
            row0 = pl.multiple_of(g * ROWS + HALO, 8)
            coefficients = self.coefficients(row0)

            def block(b, sums):
                mass, hit = sums
                for place in self.places(layout(b), row0):
                    segment, u, _, _, totals0, _ = place
                    table = segment.table + u
                    kind = self.kind(table)
                    firsts = [self.first(table, r) for r in range(REACTIONS)]
                    for h in range(2):
                        _, value = self.value(source, place, h, coefficients, firsts)
                        row = pl.multiple_of(totals0 + u * self.plane + h * self.rows, 8)
                        so_far = self.acc[pl.ds(row, ROWS), :]
                        totals = so_far + value * weight_totals
                        mass = mass + totals
                        hit = hit + totals * (1.0 - self.mask(kind, h, row0, ROWS))
                        self.acc[pl.ds(row, ROWS), :] = so_far + value * weight_density
                return mass, hit

            return lax.fori_loop(0, blocks, block, sums)

        zero = jnp.zeros((ROWS, LANES), jnp.float32)
        return lax.fori_loop(0, (self.rows - 2 * HALO) // ROWS, group, (zero, zero))

    def restore(self, local, out, index, matrix):
        own = self.rows - 2 * HALO
        even = self.acc[pl.ds(pl.multiple_of(local * self.plane + HALO, 8), own), :]
        odd = self.acc[pl.ds(pl.multiple_of(local * self.plane + self.rows + HALO, 8), own), :]
        out[index] = split_product(jnp.concatenate([even, odd], axis=1), matrix)


def copy_all(copies):
    for copy in copies:
        copy.start()
    return copies


def wait_all(copies):
    for copy in copies:
        copy.wait()


def in_groups(count, limit, function):
    size = largest_divisor(count, limit)

    def several(g, carry):
        for i in range(size):
            function(g * size + i)
        return carry

    lax.fori_loop(0, count // size, several, 0)


def sends_kernel(axis, dim, source, *refs):
    first, second, stage, sems = refs[-4:]
    odd = lax.axis_index(axis) & 1
    last = source.shape[dim] - HALO
    copies = []
    for i, start in enumerate(((1 - odd) * last, odd * last)):
        at = pl.ds(pl.multiple_of(start, HALO), HALO)
        piece = source.at[at] if dim == 0 else source.at[:, at]
        copies.append(pltpu.make_async_copy(piece, stage.at[i], sems.at[i]))
    copy_all(copies)
    outs = []
    for i, out in enumerate((first, second)):
        copies[i].wait()
        outs.append(pltpu.make_async_copy(stage.at[i], out, sems.at[2 + i]))
        outs[-1].start()
    wait_all(outs)


def corners_kernel(first_in, second_in, itab, first, second):
    odd = lax.axis_index("gx") & 1
    last = first_in.shape[0] - HALO
    swapped = (lax.axis_index("gy") & 1) == 0
    for out, start in ((first, (1 - odd) * last), (second, odd * last)):
        at = pl.ds(pl.multiple_of(start, HALO), HALO)
        low, high = first_in[at], second_in[at]
        out[:, pl.ds(0, HALO)] = jnp.where(swapped, high, low)
        out[:, pl.ds(HALO, HALO)] = jnp.where(swapped, low, high)


def interior_kernel(
    dims,
    density, first_side, second_side, stay_all, weights, free, itab, ftab,
    occupancy, q_edges, p_edges, acc_edges, sums,
    p, acc, q0, q1, stay, block, staged, sem_in, sem_stay, sem_edges, sem_out,
):
    block_first, block_second, _, _ = dims
    rows = block_second + 2 * HALO
    plane = 2 * rows
    chunk = 8
    chunks = block_first // chunk
    even = (lax.axis_index("gy") & 1) == 0
    lattice = Lattice(
        rows, 0, itab, ftab, block_first + 2 * HALO, weights, free, stay, p, acc, block_first
    )
    loads = copy_all(
        [
            pltpu.make_async_copy(
                density.at[pl.ds(c * chunk, chunk)], block.at[pl.ds(c * chunk, chunk)], sem_in.at[c]
            )
            for c in range(chunks)
        ]
    )
    stay_copy = pltpu.make_async_copy(
        stay_all.at[pl.ds(HALO * plane, block_first * plane)], stay, sem_stay
    )
    stay_copy.start()
    spread = parity_matrix(False)
    for c in range(chunks):
        loads[c].wait()

        def layer(i, c=c):
            local = c * chunk + i
            first, second = first_side[local], second_side[local]
            below = jnp.where(even, second, first)
            above = jnp.where(even, first, second)
            values = jnp.concatenate([below, block[local], above], axis=0)
            lattice.ingest(
                q0, split_product(values, spread), local, local + HALO, local, local
            )

        in_groups(chunk, 4, layer)
    stay_copy.wait()

    edges = []

    def export(k):
        q = (q0, q1)[k % 2]
        for side in range(2):
            layer = 2 * k if side == 0 else block_first - 2 * k - 4
            for turn in (-1, 0, 1):
                edges.append(
                    pltpu.make_async_copy(
                        q.at[pl.ds(lattice.moved(turn, layer * plane), 4 * plane)],
                        q_edges.at[k, side, turn + 1],
                        sem_edges.at[(k * 2 + side) * 4 + turn + 1],
                    )
                )
                edges[-1].start()
            layer = 2 * k if side == 0 else block_first - 2 * k - 2
            edges.append(
                pltpu.make_async_copy(
                    p.at[pl.ds(layer * plane, 2 * plane)],
                    p_edges.at[k, side],
                    sem_edges.at[(k * 2 + side) * 4 + 3],
                )
            )
            edges[-1].start()

    def layout_of(low, unroll):
        def layout(b):
            local = low + b * unroll
            return [Segment(unroll, local, local + HALO, local, local, local)]

        return layout

    export(0)
    for k in range(1, STEPS):
        low, high = 2 * k, block_first - 2 * k
        unroll = largest_divisor(high - low, BODY_LAYERS)
        lattice.advance(
            k, (q0, q1)[(k - 1) % 2], (q0, q1)[k % 2], (high - low) // unroll, layout_of(low, unroll)
        )
        export(k)
    for side in range(2):
        layer = 0 if side == 0 else block_first - HALO
        edges.append(
            pltpu.make_async_copy(
                acc.at[pl.ds(layer * plane, HALO * plane)], acc_edges.at[side], sem_edges.at[32 + side]
            )
        )
        edges[-1].start()
    inner = block_first - 2 * HALO
    unroll = largest_divisor(inner, 8)
    mass, hit = lattice.finish((q0, q1)[(STEPS - 1) % 2], inner // unroll, layout_of(HALO, unroll))
    sums[pl.ds(0, ROWS), :] = mass
    sums[pl.ds(ROWS, ROWS), :] = hit
    gather = parity_matrix(True)
    in_groups(inner, 4, lambda i: lattice.restore(HALO + i, staged, i, gather))
    out = pltpu.make_async_copy(staged, occupancy.at[pl.ds(HALO, inner)], sem_out)
    out.start()
    out.wait()
    wait_all(edges)


SIDE = 2 * HALO + 2
SIDE_MOVED = HALO + 4


def edges_kernel(
    dims, devices,
    first_halo, second_halo, first_corner, second_corner, stay_all, q_edges, p_edges, acc_edges, sums_in,
    weights, free, itab, ftab, occupancy_in,
    occupancy, row_out,
    p, acc, q0, q1, q2, q3, stay, staged, sem_q, sem_p, sem_other, sem_out,
):
    block_first, block_second, _, _ = dims
    rows = block_second + 2 * HALO
    plane = 2 * rows
    q = (q0, q1, q2, q3)
    right_table = block_first - 2
    lattice = Lattice(
        rows, 1, itab, ftab, block_first + 2 * HALO, weights, free, stay, p, acc, 2 * SIDE_MOVED
    )
    early, imports = [], []
    p_imports = [[] for _ in range(STEPS)]
    for side in range(2):
        first = 2
        early.append(
            pltpu.make_async_copy(
                stay_all.at[pl.ds(((0, right_table)[side] + first) * plane, (SIDE - 4) * plane)],
                stay.at[pl.ds((side * SIDE + first) * plane, (SIDE - 4) * plane)],
                sem_other.at[side],
            )
        )
        early.append(
            pltpu.make_async_copy(
                acc_edges.at[side],
                acc.at[pl.ds(side * HALO * plane, HALO * plane)],
                sem_other.at[2 + side],
            )
        )
        for k in range(STEPS):
            layer = 2 * k + HALO if side == 0 else SIDE + 8 - 2 * k
            p_imports[k].append(
                pltpu.make_async_copy(
                    p_edges.at[k, side], p.at[pl.ds(layer * plane, 2 * plane)], sem_p.at[k * 2 + side]
                )
            )
    for k in range(STEPS):
        imports.append([])
        for side in range(2):
            layer = HALO if side == 0 else SIDE_MOVED
            for turn in (-1, 0, 1):
                imports[k].append(
                    pltpu.make_async_copy(
                        q_edges.at[k, side, turn + 1],
                        q[k].at[pl.ds(lattice.moved(turn, layer * plane), 4 * plane)],
                        sem_q.at[(k * 2 + side) * 3 + turn + 1],
                    )
                )
    copy_all(imports[0])
    copy_all(early)
    copy_all(p_imports[0])
    for k in range(1, STEPS):
        copy_all(imports[k] + p_imports[k])
    spread = parity_matrix(False)
    even = (lax.axis_index("gx") & 1) == 0
    for side in range(2):

        def layer(i, side=side):
            take_first = even if side == 1 else ~even
            corner = jnp.where(take_first, first_corner[i], second_corner[i])
            main = jnp.where(take_first, first_halo[i], second_halo[i])
            values = jnp.concatenate([corner[:HALO], main, corner[HALO:]], axis=0)
            lattice.ingest(
                q0,
                split_product(values, spread),
                i if side == 0 else SIDE + 10 + i,
                i if side == 0 else block_first + HALO + i,
                i if side == 0 else SIDE_MOVED + 4 + i,
                None,
            )

        in_groups(HALO, 4, layer)
    wait_all(early)

    def layout_of(k):
        def layout(b):
            return [
                Segment(HALO, 2 * k, 2 * k, 2, 0, 2 * k - HALO),
                Segment(
                    HALO, SIDE + 10 - 2 * k, block_first + HALO - 2 * k,
                    SIDE_MOVED + 2, SIDE_MOVED + 4, 2 * HALO - 2 * k,
                ),
            ]

        return layout

    for k in range(1, STEPS):
        wait_all(imports[k - 1] + p_imports[k - 1])
        own = [u >= HALO - 2 * k for u in range(HALO)] + [u < 2 * k for u in range(HALO)]
        lattice.advance(k, q[k - 1], q[k], 1, layout_of(k), own)
    wait_all(imports[STEPS - 1] + p_imports[STEPS - 1])
    mass, hit = lattice.finish(q[STEPS - 1], 1, layout_of(STEPS))
    gather = parity_matrix(True)
    outs = []
    for side in range(2):
        in_groups(
            HALO,
            4,
            lambda i, side=side: lattice.restore(side * HALO + i, staged, side * HALO + i, gather),
        )
        outs.append(
            pltpu.make_async_copy(
                staged.at[pl.ds(side * HALO, HALO)],
                occupancy.at[pl.ds(0 if side == 0 else block_first - HALO, HALO)],
                sem_out.at[side],
            )
        )
        outs[-1].start()
    mass = jnp.sum(mass + sums_in[pl.ds(0, ROWS), :])
    hit = jnp.sum(hit + sums_in[pl.ds(ROWS, ROWS), :])
    lane = lax.broadcasted_iota(jnp.int32, (devices, LANES), 1)
    row_out[...] = jnp.where(lane == 0, hit, jnp.where(lane == 1, mass, 0.0))
    wait_all(outs)


def body(density, reaction_rates, state_changes, target_box, truncation):
    block_first, block_second, species_third = density.shape
    extents = (
        block_first * lax.axis_size("gx"),
        block_second * lax.axis_size("gy"),
        species_third,
    )
    count_first, count_second = lax.axis_size("gx"), lax.axis_size("gy")
    devices = count_first * count_second
    rows = block_second + 2 * HALO
    plane = 2 * rows
    layers = block_first + 2 * HALO
    dims = (block_first, block_second, extents, (block_first, 2 * SIDE_MOVED))

    def exchange(pieces, axis, count):
        received = []
        for start, piece in enumerate(pieces):
            pairs = [(i, i + 1) for i in range(start, count - 1, 2)]
            received.append(lax.ppermute(piece, axis, pairs + [(j, i) for i, j in pairs]))
        return received

    f32 = jnp.float32
    smem = pl.BlockSpec(memory_space=pltpu.SMEM)
    vmem = pl.BlockSpec(memory_space=pltpu.VMEM)
    hbm = pl.BlockSpec(memory_space=pl.ANY)
    params = pltpu.CompilerParams(vmem_limit_bytes=VMEM_LIMIT)
    chunk = largest_divisor(layers, 8)

    def sends(axis, dim, *after):
        shape = tuple(HALO if d == dim else size for d, size in enumerate(density.shape))
        return pl.pallas_call(
            functools.partial(sends_kernel, axis, dim),
            out_shape=(jax.ShapeDtypeStruct(shape, f32),) * 2,
            in_specs=[hbm] * (1 + len(after)),
            out_specs=(hbm, hbm),
            scratch_shapes=[pltpu.VMEM((2,) + shape, f32), pltpu.SemaphoreType.DMA((4,))],
            compiler_params=params,
            name="sends",
        )(density, *after)

    side_sends = sends("gy", 1)
    first_side, second_side = exchange(side_sends, "gy", count_second)
    first_halo, second_halo = exchange(sends("gx", 0, side_sends[0]), "gx", count_first)

    stay, weights, free, itab, ftab = pl.pallas_call(
        functools.partial(tables_kernel, dims),
        grid=(layers // chunk,),
        out_shape=(
            jax.ShapeDtypeStruct((layers, 2, rows, LANES), f32),
            jax.ShapeDtypeStruct((12 * rows, LANES), f32),
            jax.ShapeDtypeStruct((6 * rows, LANES), f32),
            jax.ShapeDtypeStruct((KINDS + layers + 4,), jnp.int32),
            jax.ShapeDtypeStruct(((layers + 4) * REACTIONS + 8,), f32),
        ),
        in_specs=[smem] * 4,
        out_specs=(
            pl.BlockSpec((chunk, 2, rows, LANES), lambda i: (i, 0, 0, 0)),
            pl.BlockSpec((12 * rows, LANES), lambda i: (0, 0)),
            pl.BlockSpec((6 * rows, LANES), lambda i: (0, 0)),
            smem,
            smem,
        ),
        scratch_shapes=[pltpu.VMEM((12 * rows, LANES), f32)],
        compiler_params=params,
        name="tables",
    )(reaction_rates, state_changes, target_box, truncation)
    stay = stay.reshape(layers * plane, LANES)

    corner = jax.ShapeDtypeStruct((HALO, 2 * HALO, species_third), f32)
    corner_sends = pl.pallas_call(
        corners_kernel,
        out_shape=(corner, corner),
        in_specs=[vmem, vmem, smem],
        out_specs=(vmem, vmem),
        compiler_params=params,
        name="corners",
    )(first_side, second_side, itab)
    first_corner, second_corner = exchange(corner_sends, "gx", count_first)

    def scratch(own, totals, moved, steps):
        return (
            [pltpu.VMEM((own * plane, LANES), f32), pltpu.VMEM((totals * plane, LANES), f32)]
            + [pltpu.VMEM((3 * moved * plane + 2 * PAD, LANES), f32) for _ in range(steps)]
            + [pltpu.VMEM((own * plane, LANES), f32)]
        )

    chunks = block_first // 8
    occupancy, q_edges, p_edges, acc_edges, sums = pl.pallas_call(
        functools.partial(interior_kernel, dims),
        out_shape=(
            jax.ShapeDtypeStruct(density.shape, f32),
            jax.ShapeDtypeStruct((STEPS, 2, 3, 4 * plane, LANES), f32),
            jax.ShapeDtypeStruct((STEPS, 2, 2 * plane, LANES), f32),
            jax.ShapeDtypeStruct((2, HALO * plane, LANES), f32),
            jax.ShapeDtypeStruct((2 * ROWS, LANES), f32),
        ),
        in_specs=[hbm, vmem, vmem, hbm, vmem, vmem, smem, smem],
        out_specs=(hbm, hbm, hbm, hbm, vmem),
        scratch_shapes=scratch(block_first, block_first, block_first, 2)
        + [
            pltpu.VMEM((block_first, block_second, species_third), f32),
            pltpu.VMEM((block_first - 2 * HALO, block_second, species_third), f32),
            pltpu.SemaphoreType.DMA((chunks,)),
            pltpu.SemaphoreType.DMA,
            pltpu.SemaphoreType.DMA((34,)),
            pltpu.SemaphoreType.DMA,
        ],
        compiler_params=params,
        cost_estimate=pl.CostEstimate(flops=400_000_000, bytes_accessed=40_000_000, transcendentals=0),
        name="interior",
    )(density, first_side, second_side, stay, weights, free, itab, ftab)

    occupancy, row = pl.pallas_call(
        functools.partial(edges_kernel, dims, devices),
        out_shape=(
            jax.ShapeDtypeStruct(density.shape, f32),
            jax.ShapeDtypeStruct((devices, LANES), f32),
        ),
        in_specs=[vmem] * 4 + [hbm] * 4 + [vmem] * 3 + [smem] * 2 + [hbm],
        out_specs=(hbm, vmem),
        scratch_shapes=scratch(2 * SIDE, 2 * HALO, 2 * SIDE_MOVED, STEPS)
        + [
            pltpu.VMEM((2 * HALO, block_second, species_third), f32),
            pltpu.SemaphoreType.DMA((24,)),
            pltpu.SemaphoreType.DMA((8,)),
            pltpu.SemaphoreType.DMA((4,)),
            pltpu.SemaphoreType.DMA((2,)),
        ],
        input_output_aliases={13: 0},
        compiler_params=params,
        name="edges",
    )(
        first_halo, second_halo, first_corner, second_corner, stay, q_edges, p_edges, acc_edges, sums,
        weights, free, itab, ftab, occupancy,
    )
    rows_in = lax.all_to_all(row, ("gx", "gy"), 0, 0, tiled=True)
    summary = jnp.sum(rows_in[:, :2], axis=0) * (1.0 / math.prod(extents))
    return occupancy, summary


def solution(mesh):
    placed = (P("gx", "gy", None), P(), P(), P(), P())
    return jax.shard_map(
        body, mesh=mesh, in_specs=placed, out_specs=(P("gx", "gy", None), P()), check_vma=False
    )
```

```python
import functools
import math

import jax
import jax.numpy as jnp
from jax import lax
from jax.experimental import pallas as pl
from jax.experimental.pallas import tpu as pltpu
from jax.sharding import PartitionSpec as P

STEPS = 4
REACTIONS = 6
HALO = 2 * STEPS
LANES = 128
ROWS = 16
PAD = 8
BODY_LAYERS = 14

mean_jumps = 8.0
headroom = 1.05
series_length = 40

VMEM_LIMIT = 62 << 20


ABOVE = 2


def largest_divisor(number, limit):
    return max(u for u in range(1, limit + 1) if number % u == 0)


def counts_factor(values, order, extent):
    linear = values * (1.0 / extent)
    square = values * (values - 1.0) * (1.0 / (extent * extent))
    return jnp.where(order == 0, 1.0, jnp.where(order == 1, linear, square))


def tables_kernel(
    dims, rates, changes, box, truncation,
    stay, weights, free, offsets, series, firsts, kinds,
    staged, sem_stay,
):
    block_first, block_second, extents, kernel_layers = dims
    rows = block_second + 2 * HALO
    plane = 2 * rows
    layers = block_first + 2 * HALO
    anchor_first = lax.axis_index("gx") * block_first - HALO
    anchor_second = lax.axis_index("gy") * block_second - HALO

    def order(r, d):
        return jnp.maximum(-changes[d, r], 0)

    def by_reaction(index, value, copies=1):
        found = jnp.zeros(index.shape, jnp.float32)
        for r in range(REACTIONS):
            here = index == r
            for c in range(1, copies):
                here = here | (index == r + c * REACTIONS)
            found = jnp.where(here, value(r), found)
        return found

    def orders_by_reaction(index, d, copies):
        return by_reaction(index, lambda r: order(r, d).astype(jnp.float32), copies)

    corner = jnp.float32(0.0)
    for r in range(REACTIONS):
        term = rates[r]
        for d in range(3):
            e = float(extents[d])
            s = order(r, d)
            term = term * jnp.where(
                s == 0, 1.0, jnp.where(s == 1, (e - 1.0) / e, (e - 1.0) * (e - 2.0) / (e * e))
            )
        corner = corner + term
    inverse = 1.0 / jnp.full((rows, LANES), headroom * corner, jnp.float32)
    row = lax.broadcasted_iota(jnp.int32, (rows, LANES), 0) + anchor_second
    lane = lax.broadcasted_iota(jnp.int32, (rows, LANES), 1)
    real_row = (row >= 0) & (row < extents[1])
    box_row = (row >= box[0, 1]) & (row < box[1, 1])
    for h in range(2):
        third = 2 * lane + h
        box_here = box_row & (third >= box[0, 2]) & (third < box[1, 2])
        free[pl.ds(h * rows, rows), :] = jnp.where(real_row, 1.0, 0.0)
        free[pl.ds(plane + h * rows, rows), :] = jnp.where(real_row & ~box_here, 1.0, 0.0)
        free[pl.ds(2 * plane + h * rows, rows), :] = jnp.zeros((rows, LANES), jnp.float32)

    copies = 3
    split_lane = lax.broadcasted_iota(jnp.int32, (1, LANES), 1)
    first_order = orders_by_reaction(split_lane, 0, copies)
    along_rows = jnp.where(
        lane < copies * REACTIONS,
        counts_factor(
            row.astype(jnp.float32),
            orders_by_reaction(split_lane, 1, copies),
            float(extents[1]),
        )
        * by_reaction(split_lane, lambda r: rates[r], copies)
        * inverse,
        0.0,
    )
    term = lax.broadcasted_iota(jnp.int32, (LANES, 2 * LANES), 0)
    place = lax.broadcasted_iota(jnp.int32, (LANES, 2 * LANES), 1)
    third = 2 * (place & (LANES - 1)) + (place >> 7)
    along_third = counts_factor(
        third.astype(jnp.float32),
        orders_by_reaction(term[:, :LANES], 2, copies)[:, :1],
        float(extents[2]),
    )
    high = along_third.astype(jnp.bfloat16).astype(jnp.float32)
    low = along_third - high
    is_low = (term >= REACTIONS) & (term < 2 * REACTIONS)
    along_third = jnp.where(
        term < copies * REACTIONS, jnp.where(is_low, low, high), 0.0
    ).astype(jnp.bfloat16)

    stay_copies = []
    chunk = largest_divisor(layers, 8)

    def stay_layer(i):
        n0 = anchor_first + i
        real = (n0 >= 0) & (n0 < extents[0])
        in_box = (n0 >= box[0, 0]) & (n0 < box[1, 0])
        kind = jnp.where(real, jnp.where(in_box, 1, 0), 2)
        along_first = counts_factor(
            jnp.full((1, LANES), n0, jnp.int32).astype(jnp.float32), first_order, float(extents[0])
        )
        whole = along_rows * along_first
        upper = whole.astype(jnp.bfloat16).astype(jnp.float32)
        split = jnp.where(lane < 2 * REACTIONS, upper, whole - upper).astype(jnp.bfloat16)
        total = jnp.dot(split, along_third, preferred_element_type=jnp.float32)
        for h in range(2):
            mask = free[pl.ds(pl.multiple_of(kind * plane + h * rows, 8), rows), :]
            at = pl.multiple_of(i * plane + h * rows, 8)
            staged[pl.ds(at, rows), :] = 1.0 - mask * total[:, h * LANES : (h + 1) * LANES]

    for c in range(layers // chunk):
        in_groups(chunk, 4, lambda i, c=c: stay_layer(c * chunk + i))
        at = pl.ds(c * chunk * plane, chunk * plane)
        stay_copies.append(pltpu.make_async_copy(staged.at[at], stay.at[at], sem_stay.at[c]))
        stay_copies[-1].start()

    for h in range(2):
        third = 2 * lane + h

        def coefficient(r, carry, h=h, third=third):
            from_row = row - changes[1, r]
            from_third = third - changes[2, r]
            moved = (
                inverse
                * rates[r]
                * counts_factor(from_row.astype(jnp.float32), order(r, 1), float(extents[1]))
                * counts_factor(from_third.astype(jnp.float32), order(r, 2), float(extents[2]))
            )
            inside = (from_third >= 0) & (from_third < extents[2])
            at = pl.ds(pl.multiple_of((r * 2 + h) * rows, 8), rows)
            weights[at, :] = jnp.where(inside, moved, 0.0)
            return carry

        lax.fori_loop(0, REACTIONS, coefficient, 0)
    for which in range(2):
        for r in range(REACTIONS):
            for h in range(2):
                source = h - changes[2, r]
                offsets[which * 12 + r * 2 + h] = (
                    PAD
                    + (((source >> 1) + 1) * kernel_layers[which] - changes[0, r]) * plane
                    + (source & 1) * rows
                    - changes[1, r]
                )
    n0 = lax.broadcasted_iota(jnp.int32, firsts.shape, 0) + (anchor_first - ABOVE)
    reaction = lax.broadcasted_iota(jnp.int32, firsts.shape, 1)
    change = by_reaction(reaction, lambda r: changes[0, r].astype(jnp.float32))
    firsts[...] = counts_factor(
        n0.astype(jnp.float32) - change, orders_by_reaction(reaction, 0, 1), float(extents[0])
    )
    real = (n0 >= 0) & (n0 < extents[0])
    in_box = (n0 >= box[0, 0]) & (n0 < box[1, 0])
    kinds[...] = jnp.where(real, jnp.where(in_box, 1, 0), 2)
    table = [
        math.exp(-mean_jumps) * mean_jumps**j / math.factorial(j) for j in range(series_length)
    ]
    for j in range(STEPS):
        series[j] = jnp.float32(table[j])
    for which in range(2):
        tail = jnp.float32(0.0)
        for j in range(STEPS + 1, series_length):
            tail = tail + jnp.where(j <= truncation[which], jnp.float32(table[j]), 0.0)
        series[STEPS + which] = jnp.float32(table[STEPS]) + tail
    wait_all(stay_copies)


def split_product(values, matrix):
    high = values.astype(jnp.bfloat16)
    low = (values - high.astype(jnp.float32)).astype(jnp.bfloat16)
    return jnp.dot(high, matrix, preferred_element_type=jnp.float32) + jnp.dot(
        low, matrix, preferred_element_type=jnp.float32
    )


def parity_matrix(transposed):
    size = 2 * LANES
    third = lax.broadcasted_iota(jnp.int32, (size, size), 1 if transposed else 0)
    place = lax.broadcasted_iota(jnp.int32, (size, size), 0 if transposed else 1)
    return jnp.where(place == (third & 1) * LANES + (third >> 1), 1.0, 0.0).astype(jnp.bfloat16)


class Segment:
    def __init__(self, count, own, table, source, target, totals):
        self.count, self.own, self.table = count, own, table
        self.source, self.target, self.totals = source, target, totals


class Lattice:
    def __init__(self, rows, which, tables, weights, free, stay, p, acc, moved_layers):
        self.rows, self.plane = rows, 2 * rows
        self.which = which
        self.offsets, self.series, self.firsts, self.kinds = tables
        self.weights, self.free, self.stay = weights, free, stay
        self.p, self.acc, self.moved_layers = p, acc, moved_layers
        self.never = jnp.full((ROWS, LANES), self.kinds[0, 0], jnp.int32) < 0

    def moved(self, turn, row):
        return PAD + (turn + 1) * self.moved_layers * self.plane + row

    def kind(self, table):
        return self.kinds[ABOVE + table, 0]

    def first(self, table, r):
        return self.firsts[ABOVE + table, r]

    def mask(self, kind, h, row0, count):
        at = pl.multiple_of(kind * self.plane + h * self.rows + row0, 8)
        return self.free[pl.ds(at, count), :]

    def ingest(self, q, values, local, table, target, totals):
        kind = self.kind(table)
        rows = self.rows
        for h in range(2):
            part = values[:, h * LANES : (h + 1) * LANES]
            at = pl.multiple_of(local * self.plane + h * rows, 8)
            self.p[pl.ds(at, rows), :] = part
            if totals is not None:
                at = pl.multiple_of(totals * self.plane + h * rows, 8)
                self.acc[pl.ds(at, rows), :] = part * self.series[0]
            masked = part * self.mask(kind, h, 0, rows)
            at = target * self.plane + h * rows
            for turn in (0, -1, 1):
                lanes = masked if turn == 0 else pltpu.roll(masked, 1 if turn < 0 else LANES - 1, 1)
                q[pl.ds(pl.multiple_of(self.moved(turn, at), 8), rows), :] = lanes

    def coefficients(self, row0):
        return [
            [
                self.weights[pl.ds(pl.multiple_of((r * 2 + h) * self.rows + row0, 8), ROWS), :]
                for h in range(2)
            ]
            for r in range(REACTIONS)
        ]

    def places(self, segments, row0):
        found = []
        for segment in segments:
            own = segment.own * self.plane + row0
            target = segment.target * self.plane + row0
            totals = None if segment.totals is None else segment.totals * self.plane + row0
            shift = segment.source * self.plane + row0
            sources = [
                [self.offsets[self.which * 12 + r * 2 + h] + shift for h in range(2)]
                for r in range(REACTIONS)
            ]
            for u in range(segment.count):
                found.append((segment, u, own, target, totals, sources))
        return found

    def value(self, source, place, h, coefficients, firsts, rolled=None):
        segment, u, own, _, _, sources = place
        at = pl.multiple_of(own + u * self.plane + h * self.rows, 8)
        value = self.p[pl.ds(at, ROWS), :]
        if rolled is not None:
            value = jnp.where(self.never, rolled, value)
        value = value * self.stay[pl.ds(at, ROWS), :]
        terms = [value]
        for r in range(REACTIONS):
            arriving = source[pl.ds(sources[r][h] + u * self.plane, ROWS), :]
            terms.append(arriving * coefficients[r][h] * firsts[r])
        while len(terms) > 1:
            pairs = [terms[i : i + 2] for i in range(0, len(terms), 2)]
            terms = [pair[0] + pair[1] if len(pair) == 2 else pair[0] for pair in pairs]
        return at, terms[0]

    def advance(self, k, source, target, blocks, layout, totals_by_layer=None):
        weight = self.series[k]
        plane, rows = self.plane, self.rows
        counts = [segment.count for segment in layout(0)]
        size = sum(counts)
        offsets = [(s, u) for s, count in enumerate(counts) for u in range(count)]
        lag = min(6, size // 2)

        def center_row(before, index, h):
            s, u = offsets[index]
            return before[s] + u * plane + h * rows

        def roll_layer(before, index):
            pairs = []
            for h in range(2):
                at = self.moved(0, center_row(before, index, h))
                values = target[pl.ds(pl.multiple_of(at, 8), ROWS), :]
                pairs.append((pltpu.roll(values, 1, 1), pltpu.roll(values, LANES - 1, 1)))
            return pairs

        def store_layer(before, index, pairs):
            for h in range(2):
                row = center_row(before, index, h)
                for side, turn in enumerate((-1, 1)):
                    at = pl.multiple_of(self.moved(turn, row), 8)
                    target[pl.ds(at, ROWS), :] = pairs[h][side]

        def group(g, before):
            row0 = pl.multiple_of(g * ROWS, ROWS)
            coefficients = self.coefficients(row0)

            def block(b, before):
                places = self.places(layout(b), row0)
                rolled = [roll_layer(before, index) for index in range(size)]
                stored = 0
                for index, place in enumerate(places):
                    segment, u, own, target0, totals0, _ = place
                    table = segment.table + u
                    kind = self.kind(table)
                    firsts = [self.first(table, r) for r in range(REACTIONS)]
                    ready = -1
                    if index >= lag:
                        ready = ((index - lag + 1) * size + size - lag - 1) // (size - lag) - 1
                    for h in range(2):
                        at, value = self.value(
                            source, place, h, coefficients, firsts,
                            rolled[ready][1][1] if ready >= 0 and h == 1 else None,
                        )
                        self.p[pl.ds(at, ROWS), :] = value
                        masked = value * self.mask(kind, h, row0, ROWS)
                        row = target0 + u * plane + h * rows
                        target[pl.ds(pl.multiple_of(self.moved(0, row), 8), ROWS), :] = masked
                        if totals_by_layer is None or totals_by_layer[index]:
                            at = pl.ds(pl.multiple_of(totals0 + u * plane + h * rows, 8), ROWS)
                            total = value * weight
                            if totals_by_layer is None or totals_by_layer[index] == "add":
                                total = total + self.acc[at, :]
                            self.acc[at, :] = total
                    while stored <= ready:
                        store_layer(before, stored, rolled[stored])
                        stored += 1
                while stored < size:
                    store_layer(before, stored, rolled[stored])
                    stored += 1
                return tuple(
                    pl.multiple_of(jnp.int32(segment.target * plane) + row0, 8)
                    for segment in layout(b)
                )

            return lax.fori_loop(0, blocks, block, before)

        before = tuple(jnp.int32(segment.target * plane) for segment in layout(jnp.int32(0)))
        last = lax.fori_loop(0, rows // ROWS, group, before)
        for index in range(size):
            store_layer(last, index, roll_layer(last, index))

    def finish(self, source, blocks, layout, more=None, fresh=None):
        weight_density = self.series[STEPS]
        weight_totals = self.series[STEPS + 1]

        def group(g, sums):
            row0 = pl.multiple_of(g * ROWS + HALO, 8)
            coefficients = self.coefficients(row0)

            def block(b, sums):
                mass, hit = sums
                for index, place in enumerate(self.places(layout(b), row0)):
                    segment, u, _, _, totals0, _ = place
                    table = segment.table + u
                    kind = self.kind(table)
                    firsts = [self.first(table, r) for r in range(REACTIONS)]
                    for h in range(2):
                        _, value = self.value(source, place, h, coefficients, firsts)
                        row = pl.multiple_of(totals0 + u * self.plane + h * self.rows, 8)
                        so_far = (self.acc if more is None else more)[pl.ds(row, ROWS), :]
                        if more is not None and not fresh[index]:
                            so_far = so_far + self.acc[pl.ds(row, ROWS), :]
                        totals = so_far + value * weight_totals
                        mass = mass + totals
                        hit = hit + totals * (1.0 - self.mask(kind, h, row0, ROWS))
                        self.acc[pl.ds(row, ROWS), :] = so_far + value * weight_density
                return mass, hit

            return lax.fori_loop(0, blocks, block, sums)

        zero = jnp.zeros((ROWS, LANES), jnp.float32)
        return lax.fori_loop(0, (self.rows - 2 * HALO) // ROWS, group, (zero, zero))

    def restore(self, local, out, index, matrix):
        own = self.rows - 2 * HALO
        even = self.acc[pl.ds(pl.multiple_of(local * self.plane + HALO, 8), own), :]
        odd = self.acc[pl.ds(pl.multiple_of(local * self.plane + self.rows + HALO, 8), own), :]
        out[index] = split_product(jnp.concatenate([even, odd], axis=1), matrix)


def copy_all(copies):
    for copy in copies:
        copy.start()
    return copies


def wait_all(copies):
    for copy in copies:
        copy.wait()


def in_groups(count, limit, function):
    size = largest_divisor(count, limit)

    def several(g, carry):
        for i in range(size):
            function(g * size + i)
        return carry

    lax.fori_loop(0, count // size, several, 0)


def start_sends(axis, dim, source, stage, sems):
    odd = lax.axis_index(axis) & 1
    last = source.shape[dim] - HALO
    copies = []
    for i, start in enumerate(((1 - odd) * last, odd * last)):
        at = pl.ds(pl.multiple_of(start, HALO), HALO)
        piece = source.at[at] if dim == 0 else source.at[:, at]
        copies.append(pltpu.make_async_copy(piece, stage.at[i], sems.at[i]))
    return copy_all(copies)


def finish_sends(loads, stage, outs, sems):
    stores = []
    for i, out in enumerate(outs):
        loads[i].wait()
        stores.append(pltpu.make_async_copy(stage.at[i], out, sems.at[2 + i]))
        stores[-1].start()
    return stores


def sends_kernel(axis, dim, source, *refs):
    first, second, stage, sems = refs[-4:]
    loads = start_sends(axis, dim, source, stage, sems)
    wait_all(finish_sends(loads, stage, (first, second), sems))


def corners_kernel(first_in, second_in, offsets, first, second):
    odd = lax.axis_index("gx") & 1
    last = first_in.shape[0] - HALO
    swapped = (lax.axis_index("gy") & 1) == 0
    for out, start in ((first, (1 - odd) * last), (second, odd * last)):
        at = pl.ds(pl.multiple_of(start, HALO), HALO)
        low, high = first_in[at], second_in[at]
        out[:, pl.ds(0, HALO)] = jnp.where(swapped, high, low)
        out[:, pl.ds(HALO, HALO)] = jnp.where(swapped, low, high)


def interior_kernel(
    dims,
    density, first_side, second_side, stay_all, weights, free, offsets, series, firsts, kinds,
    occupancy, q_edges, p_edges, acc_edges, sums,
    p, acc, q0, q1, stay, block, staged, sem_in, sem_stay, sem_edges, sem_out,
):
    block_first, block_second, _, _ = dims
    rows = block_second + 2 * HALO
    plane = 2 * rows
    chunk = 8
    chunks = block_first // chunk
    even = (lax.axis_index("gy") & 1) == 0
    lattice = Lattice(
        rows, 0, (offsets, series, firsts, kinds), weights, free, stay, p, acc, block_first
    )
    loads = copy_all(
        [
            pltpu.make_async_copy(
                density.at[pl.ds(c * chunk, chunk)], block.at[pl.ds(c * chunk, chunk)], sem_in.at[c]
            )
            for c in range(chunks)
        ]
    )
    stay_copy = pltpu.make_async_copy(
        stay_all.at[pl.ds(HALO * plane, block_first * plane)], stay, sem_stay
    )
    stay_copy.start()
    spread = parity_matrix(False)
    for c in range(chunks):
        loads[c].wait()

        def layer(i, c=c):
            local = c * chunk + i
            first, second = first_side[local], second_side[local]
            below = jnp.where(even, second, first)
            above = jnp.where(even, first, second)
            values = jnp.concatenate([below, block[local], above], axis=0)
            lattice.ingest(
                q0, split_product(values, spread), local, local + HALO, local, local
            )

        in_groups(chunk, 4, layer)
    stay_copy.wait()

    edges = []

    def export(k):
        q = (q0, q1)[k % 2]
        for side in range(2):
            layer = 2 * k if side == 0 else block_first - 2 * k - 4
            for turn in (-1, 0, 1):
                edges.append(
                    pltpu.make_async_copy(
                        q.at[pl.ds(lattice.moved(turn, layer * plane), 4 * plane)],
                        q_edges.at[k, side, turn + 1],
                        sem_edges.at[(k * 2 + side) * 4 + turn + 1],
                    )
                )
                edges[-1].start()
            layer = 2 * k if side == 0 else block_first - 2 * k - 2
            edges.append(
                pltpu.make_async_copy(
                    p.at[pl.ds(layer * plane, 2 * plane)],
                    p_edges.at[k, side],
                    sem_edges.at[(k * 2 + side) * 4 + 3],
                )
            )
            edges[-1].start()

    def layout_of(low, unroll):
        def layout(b):
            local = low + b * unroll
            return [Segment(unroll, local, local + HALO, local, local, local)]

        return layout

    export(0)
    for k in range(1, STEPS):
        low, high = 2 * k, block_first - 2 * k
        unroll = largest_divisor(high - low, BODY_LAYERS)
        lattice.advance(
            k, (q0, q1)[(k - 1) % 2], (q0, q1)[k % 2], (high - low) // unroll, layout_of(low, unroll)
        )
        export(k)
    for side in range(2):
        layer = 0 if side == 0 else block_first - HALO
        edges.append(
            pltpu.make_async_copy(
                acc.at[pl.ds(layer * plane, HALO * plane)], acc_edges.at[side], sem_edges.at[32 + side]
            )
        )
        edges[-1].start()
    inner = block_first - 2 * HALO
    unroll = largest_divisor(inner, 8)
    mass, hit = lattice.finish((q0, q1)[(STEPS - 1) % 2], inner // unroll, layout_of(HALO, unroll))
    sums[pl.ds(0, ROWS), :] = mass
    sums[pl.ds(ROWS, ROWS), :] = hit
    gather = parity_matrix(True)
    in_groups(inner, 4, lambda i: lattice.restore(HALO + i, staged, i, gather))
    out = pltpu.make_async_copy(staged, occupancy.at[pl.ds(HALO, inner)], sem_out)
    out.start()
    out.wait()
    wait_all(edges)


SIDE = 2 * HALO + 2
SIDE_MOVED = HALO + 4


def edges_kernel(
    dims, devices,
    first_halo, second_halo, first_corner, second_corner, stay_all, q_edges, p_edges, acc_edges, sums_in,
    weights, free, offsets, series, firsts, kinds, occupancy_in,
    occupancy, row_out,
    p, acc, q0, q1, q2, q3, stay, earlier, staged, sem_q, sem_p, sem_other, sem_out,
):
    block_first, block_second, _, _ = dims
    rows = block_second + 2 * HALO
    plane = 2 * rows
    q = (q0, q1, q2, q3)
    right_table = block_first - 2
    lattice = Lattice(
        rows, 1, (offsets, series, firsts, kinds), weights, free, stay, p, acc, 2 * SIDE_MOVED
    )
    early, late, imports = [], [], []
    p_imports = [[] for _ in range(STEPS)]
    for side in range(2):
        first = 2
        early.append(
            pltpu.make_async_copy(
                stay_all.at[pl.ds(((0, right_table)[side] + first) * plane, (SIDE - 4) * plane)],
                stay.at[pl.ds((side * SIDE + first) * plane, (SIDE - 4) * plane)],
                sem_other.at[side],
            )
        )
        late.append(
            pltpu.make_async_copy(
                acc_edges.at[side],
                earlier.at[pl.ds(side * HALO * plane, HALO * plane)],
                sem_other.at[2 + side],
            )
        )
        for k in range(STEPS):
            layer = 2 * k + HALO if side == 0 else SIDE + 8 - 2 * k
            p_imports[k].append(
                pltpu.make_async_copy(
                    p_edges.at[k, side], p.at[pl.ds(layer * plane, 2 * plane)], sem_p.at[k * 2 + side]
                )
            )
    for k in range(STEPS):
        imports.append([])
        for side in range(2):
            layer = HALO if side == 0 else SIDE_MOVED
            for turn in (-1, 0, 1):
                imports[k].append(
                    pltpu.make_async_copy(
                        q_edges.at[k, side, turn + 1],
                        q[k].at[pl.ds(lattice.moved(turn, layer * plane), 4 * plane)],
                        sem_q.at[(k * 2 + side) * 3 + turn + 1],
                    )
                )
    copy_all(imports[0])
    copy_all(early)
    copy_all(p_imports[0])
    for k in range(1, STEPS):
        copy_all(imports[k] + p_imports[k])
    copy_all(late)
    spread = parity_matrix(False)
    even = (lax.axis_index("gx") & 1) == 0
    for side in range(2):

        def layer(i, side=side):
            take_first = even if side == 1 else ~even
            corner = jnp.where(take_first, first_corner[i], second_corner[i])
            main = jnp.where(take_first, first_halo[i], second_halo[i])
            values = jnp.concatenate([corner[:HALO], main, corner[HALO:]], axis=0)
            lattice.ingest(
                q0,
                split_product(values, spread),
                i if side == 0 else SIDE + 10 + i,
                i if side == 0 else block_first + HALO + i,
                i if side == 0 else SIDE_MOVED + 4 + i,
                None,
            )

        in_groups(HALO, 4, layer)
    wait_all(early)

    def layout_of(k):
        def layout(b):
            return [
                Segment(HALO, 2 * k, 2 * k, 2, 0, 2 * k - HALO),
                Segment(
                    HALO, SIDE + 10 - 2 * k, block_first + HALO - 2 * k,
                    SIDE_MOVED + 2, SIDE_MOVED + 4, 2 * HALO - 2 * k,
                ),
            ]

        return layout

    for k in range(1, STEPS):
        wait_all(imports[k - 1] + p_imports[k - 1])
        own = [
            None if u < HALO - 2 * k else "new" if u >= HALO - 2 else "add" for u in range(HALO)
        ]
        own += own[::-1]
        lattice.advance(k, q[k - 1], q[k], 1, layout_of(k), own)
    wait_all(imports[STEPS - 1] + p_imports[STEPS - 1] + late)
    fresh = [u >= HALO - 2 for u in range(HALO)]
    mass, hit = lattice.finish(q[STEPS - 1], 1, layout_of(STEPS), earlier, fresh + fresh[::-1])
    gather = parity_matrix(True)
    outs = []
    for side in range(2):
        in_groups(
            HALO,
            4,
            lambda i, side=side: lattice.restore(side * HALO + i, staged, side * HALO + i, gather),
        )
        outs.append(
            pltpu.make_async_copy(
                staged.at[pl.ds(side * HALO, HALO)],
                occupancy.at[pl.ds(0 if side == 0 else block_first - HALO, HALO)],
                sem_out.at[side],
            )
        )
        outs[-1].start()
    mass = jnp.sum(mass + sums_in[pl.ds(0, ROWS), :])
    hit = jnp.sum(hit + sums_in[pl.ds(ROWS, ROWS), :])
    lane = lax.broadcasted_iota(jnp.int32, (devices, LANES), 1)
    row_out[...] = jnp.where(lane == 0, hit, jnp.where(lane == 1, mass, 0.0))
    wait_all(outs)


def body(density, reaction_rates, state_changes, target_box, truncation):
    block_first, block_second, species_third = density.shape
    extents = (
        block_first * lax.axis_size("gx"),
        block_second * lax.axis_size("gy"),
        species_third,
    )
    count_first, count_second = lax.axis_size("gx"), lax.axis_size("gy")
    devices = count_first * count_second
    rows = block_second + 2 * HALO
    plane = 2 * rows
    layers = block_first + 2 * HALO
    dims = (block_first, block_second, extents, (block_first, 2 * SIDE_MOVED))

    def exchange(pieces, axis, count):
        received = []
        for start, piece in enumerate(pieces):
            pairs = [(i, i + 1) for i in range(start, count - 1, 2)]
            received.append(lax.ppermute(piece, axis, pairs + [(j, i) for i, j in pairs]))
        return received

    f32 = jnp.float32
    smem = pl.BlockSpec(memory_space=pltpu.SMEM)
    vmem = pl.BlockSpec(memory_space=pltpu.VMEM)
    hbm = pl.BlockSpec(memory_space=pl.ANY)
    params = pltpu.CompilerParams(vmem_limit_bytes=VMEM_LIMIT)
    light = pl.CostEstimate(flops=1000, bytes_accessed=1000, transcendentals=0)
    def sends(axis, dim, *after):
        shape = tuple(HALO if d == dim else size for d, size in enumerate(density.shape))
        return pl.pallas_call(
            functools.partial(sends_kernel, axis, dim),
            out_shape=(jax.ShapeDtypeStruct(shape, f32),) * 2,
            in_specs=[hbm] * (1 + len(after)),
            out_specs=(hbm, hbm),
            scratch_shapes=[pltpu.VMEM((2,) + shape, f32), pltpu.SemaphoreType.DMA((4,))],
            compiler_params=params,
            cost_estimate=light,
            name="sends",
        )(density, *after)

    side_sends = sends("gy", 1)
    first_side, second_side = exchange(side_sends, "gy", count_second)
    first_halo, second_halo = exchange(sends("gx", 0, side_sends[0]), "gx", count_first)

    table_rows = -(-(layers + 2 * ABOVE) // 8) * 8
    stay, weights, free, *tables = pl.pallas_call(
        functools.partial(tables_kernel, dims),
        out_shape=(
            jax.ShapeDtypeStruct((layers * plane, LANES), f32),
            jax.ShapeDtypeStruct((12 * rows, LANES), f32),
            jax.ShapeDtypeStruct((6 * rows, LANES), f32),
            jax.ShapeDtypeStruct((24,), jnp.int32),
            jax.ShapeDtypeStruct((STEPS + 2,), f32),
            jax.ShapeDtypeStruct((table_rows, LANES), f32),
            jax.ShapeDtypeStruct((table_rows, LANES), jnp.int32),
        ),
        in_specs=[smem] * 4,
        out_specs=(hbm, vmem, vmem, smem, smem, vmem, vmem),
        scratch_shapes=[
            pltpu.VMEM((layers * plane, LANES), f32),
            pltpu.SemaphoreType.DMA((layers // largest_divisor(layers, 8),)),
        ],
        compiler_params=params,
        cost_estimate=light,
        name="tables",
    )(reaction_rates, state_changes.T, target_box, truncation)
    offsets = tables[0]

    corner = jax.ShapeDtypeStruct((HALO, 2 * HALO, species_third), f32)
    corner_sends = pl.pallas_call(
        corners_kernel,
        out_shape=(corner, corner),
        in_specs=[vmem, vmem, smem],
        out_specs=(vmem, vmem),
        compiler_params=params,
        cost_estimate=light,
        name="corners",
    )(first_side, second_side, offsets)
    first_corner, second_corner = exchange(corner_sends, "gx", count_first)

    def scratch(own, totals, moved, steps):
        return (
            [pltpu.VMEM((own * plane, LANES), f32), pltpu.VMEM((totals * plane, LANES), f32)]
            + [pltpu.VMEM((3 * moved * plane + 2 * PAD, LANES), f32) for _ in range(steps)]
            + [pltpu.VMEM((own * plane, LANES), f32)]
        )

    chunks = block_first // 8
    occupancy, q_edges, p_edges, acc_edges, sums = pl.pallas_call(
        functools.partial(interior_kernel, dims),
        out_shape=(
            jax.ShapeDtypeStruct(density.shape, f32),
            jax.ShapeDtypeStruct((STEPS, 2, 3, 4 * plane, LANES), f32),
            jax.ShapeDtypeStruct((STEPS, 2, 2 * plane, LANES), f32),
            jax.ShapeDtypeStruct((2, HALO * plane, LANES), f32),
            jax.ShapeDtypeStruct((2 * ROWS, LANES), f32),
        ),
        in_specs=[hbm, vmem, vmem, hbm, vmem, vmem] + [smem] * 4,
        out_specs=(hbm, hbm, hbm, hbm, vmem),
        scratch_shapes=scratch(block_first, block_first, block_first, 2)
        + [
            pltpu.VMEM((block_first, block_second, species_third), f32),
            pltpu.VMEM((block_first - 2 * HALO, block_second, species_third), f32),
            pltpu.SemaphoreType.DMA((chunks,)),
            pltpu.SemaphoreType.DMA,
            pltpu.SemaphoreType.DMA((34,)),
            pltpu.SemaphoreType.DMA,
        ],
        compiler_params=params,
        cost_estimate=light,
        name="interior",
    )(density, first_side, second_side, stay, weights, free, *tables)

    occupancy, row = pl.pallas_call(
        functools.partial(edges_kernel, dims, devices),
        out_shape=(
            jax.ShapeDtypeStruct(density.shape, f32),
            jax.ShapeDtypeStruct((devices, LANES), f32),
        ),
        in_specs=[vmem] * 4 + [hbm] * 4 + [vmem] * 3 + [smem] * 4 + [hbm],
        out_specs=(hbm, vmem),
        scratch_shapes=scratch(2 * SIDE, 2 * HALO, 2 * SIDE_MOVED, STEPS)
        + [
            pltpu.VMEM((2 * HALO * plane, LANES), f32),
            pltpu.VMEM((2 * HALO, block_second, species_third), f32),
            pltpu.SemaphoreType.DMA((24,)),
            pltpu.SemaphoreType.DMA((8,)),
            pltpu.SemaphoreType.DMA((4,)),
            pltpu.SemaphoreType.DMA((2,)),
        ],
        input_output_aliases={15: 0},
        compiler_params=params,
        name="edges",
    )(
        first_halo, second_halo, first_corner, second_corner, stay, q_edges, p_edges, acc_edges, sums,
        weights, free, *tables, occupancy,
    )
    rows_in = lax.all_to_all(row, ("gx", "gy"), 0, 0, tiled=True)
    summary = jnp.sum(rows_in[:, :2], axis=0) * (1.0 / math.prod(extents))
    return occupancy, summary


def solution(mesh):
    placed = (P("gx", "gy", None), P(), P(), P(), P())
    return jax.shard_map(
        body, mesh=mesh, in_specs=placed, out_specs=(P("gx", "gy", None), P()), check_vma=False
    )
```

```python
import functools
import math

import jax
import jax.numpy as jnp
from jax import lax
from jax.experimental import pallas as pl
from jax.experimental.pallas import tpu as pltpu
from jax.sharding import PartitionSpec as P

STEPS = 4
REACTIONS = 6
HALO = 2 * STEPS
LANES = 128
ROWS = 16
PAD = 8
BODY_LAYERS = 28

mean_jumps = 8.0
headroom = 1.05
series_length = 40

VMEM_LIMIT = 62 << 20


ABOVE = 2


def largest_divisor(number, limit):
    return max(u for u in range(1, limit + 1) if number % u == 0)


def counts_factor(values, order, extent):
    linear = values * (1.0 / extent)
    square = values * (values - 1.0) * (1.0 / (extent * extent))
    return jnp.where(order == 0, 1.0, jnp.where(order == 1, linear, square))


def tables_kernel(
    dims, rates, changes, box, truncation,
    stay, weights, free, offsets, series, firsts, kinds,
    staged, sem_stay,
):
    block_first, block_second, extents, kernel_layers = dims
    rows = block_second + 2 * HALO
    plane = 2 * rows
    layers = block_first + 2 * HALO
    anchor_first = lax.axis_index("gx") * block_first - HALO
    anchor_second = lax.axis_index("gy") * block_second - HALO

    plain = jnp.int32(REACTIONS - 1)
    for r in range(REACTIONS - 2, -1, -1):
        plain = jnp.where(changes[0, r] == 2, r, plain)

    def reaction_of(r):
        return jnp.where(r == 0, plain, jnp.where(r == plain, 0, r))

    def change(d, r):
        return changes[d, reaction_of(r)]

    def rate(r):
        return rates[reaction_of(r)]

    def order(r, d):
        return jnp.maximum(-change(d, r), 0)

    def by_reaction(index, value, copies=1):
        found = jnp.zeros(index.shape, jnp.float32)
        for r in range(REACTIONS):
            here = index == r
            for c in range(1, copies):
                here = here | (index == r + c * REACTIONS)
            found = jnp.where(here, value(r), found)
        return found

    def orders_by_reaction(index, d, copies):
        return by_reaction(index, lambda r: order(r, d).astype(jnp.float32), copies)

    corner = jnp.float32(0.0)
    for r in range(REACTIONS):
        term = rate(r)
        for d in range(3):
            e = float(extents[d])
            s = order(r, d)
            term = term * jnp.where(
                s == 0, 1.0, jnp.where(s == 1, (e - 1.0) / e, (e - 1.0) * (e - 2.0) / (e * e))
            )
        corner = corner + term
    inverse = 1.0 / jnp.full((rows, LANES), headroom * corner, jnp.float32)
    row = lax.broadcasted_iota(jnp.int32, (rows, LANES), 0) + anchor_second
    lane = lax.broadcasted_iota(jnp.int32, (rows, LANES), 1)
    real_row = (row >= 0) & (row < extents[1])
    box_row = (row >= box[0, 1]) & (row < box[1, 1])
    for h in range(2):
        third = 2 * lane + h
        box_here = box_row & (third >= box[0, 2]) & (third < box[1, 2])
        free[pl.ds(h * rows, rows), :] = jnp.where(real_row, 1.0, 0.0)
        free[pl.ds(plane + h * rows, rows), :] = jnp.where(real_row & ~box_here, 1.0, 0.0)
        free[pl.ds(2 * plane + h * rows, rows), :] = jnp.zeros((rows, LANES), jnp.float32)

    copies = 3
    split_lane = lax.broadcasted_iota(jnp.int32, (1, LANES), 1)
    first_order = orders_by_reaction(split_lane, 0, copies)
    along_rows = jnp.where(
        lane < copies * REACTIONS,
        counts_factor(
            row.astype(jnp.float32),
            orders_by_reaction(split_lane, 1, copies),
            float(extents[1]),
        )
        * by_reaction(split_lane, lambda r: rate(r), copies)
        * inverse,
        0.0,
    )
    term = lax.broadcasted_iota(jnp.int32, (LANES, 2 * LANES), 0)
    place = lax.broadcasted_iota(jnp.int32, (LANES, 2 * LANES), 1)
    third = 2 * (place & (LANES - 1)) + (place >> 7)
    along_third = counts_factor(
        third.astype(jnp.float32),
        orders_by_reaction(term[:, :LANES], 2, copies)[:, :1],
        float(extents[2]),
    )
    high = along_third.astype(jnp.bfloat16).astype(jnp.float32)
    low = along_third - high
    is_low = (term >= REACTIONS) & (term < 2 * REACTIONS)
    along_third = jnp.where(
        term < copies * REACTIONS, jnp.where(is_low, low, high), 0.0
    ).astype(jnp.bfloat16)

    stay_copies = []
    chunk = largest_divisor(layers, 8)

    def stay_layer(i):
        n0 = anchor_first + i
        real = (n0 >= 0) & (n0 < extents[0])
        in_box = (n0 >= box[0, 0]) & (n0 < box[1, 0])
        kind = jnp.where(real, jnp.where(in_box, 1, 0), 2)
        along_first = counts_factor(
            jnp.full((1, LANES), n0, jnp.int32).astype(jnp.float32), first_order, float(extents[0])
        )
        whole = along_rows * along_first
        upper = whole.astype(jnp.bfloat16).astype(jnp.float32)
        split = jnp.where(lane < 2 * REACTIONS, upper, whole - upper).astype(jnp.bfloat16)
        total = jnp.dot(split, along_third, preferred_element_type=jnp.float32)
        for h in range(2):
            mask = free[pl.ds(pl.multiple_of(kind * plane + h * rows, 8), rows), :]
            at = pl.multiple_of(i * plane + h * rows, 8)
            staged[pl.ds(at, rows), :] = 1.0 - mask * total[:, h * LANES : (h + 1) * LANES]

    for c in range(layers // chunk):
        in_groups(chunk, 4, lambda i, c=c: stay_layer(c * chunk + i))
        at = pl.ds(c * chunk * plane, chunk * plane)
        stay_copies.append(pltpu.make_async_copy(staged.at[at], stay.at[at], sem_stay.at[c]))
        stay_copies[-1].start()

    for h in range(2):
        third = 2 * lane + h

        def coefficient(r, carry, h=h, third=third):
            from_row = row - change(1, r)
            from_third = third - change(2, r)
            moved = (
                inverse
                * rate(r)
                * counts_factor(from_row.astype(jnp.float32), order(r, 1), float(extents[1]))
                * counts_factor(from_third.astype(jnp.float32), order(r, 2), float(extents[2]))
            )
            inside = (from_third >= 0) & (from_third < extents[2])
            at = pl.ds(pl.multiple_of((r * 2 + h) * rows, 8), rows)
            weights[at, :] = jnp.where(inside, moved, 0.0)
            return carry

        lax.fori_loop(0, REACTIONS, coefficient, 0)
    for which in range(2):
        for r in range(REACTIONS):
            for h in range(2):
                source = h - change(2, r)
                offsets[which * 12 + r * 2 + h] = (
                    PAD
                    + (((source >> 1) + 1) * kernel_layers[which] - change(0, r)) * plane
                    + (source & 1) * rows
                    - change(1, r)
                )
    n0 = lax.broadcasted_iota(jnp.int32, firsts.shape, 1) + (anchor_first - ABOVE)
    reaction = lax.broadcasted_iota(jnp.int32, firsts.shape, 0)
    moves = by_reaction(reaction, lambda r: change(0, r).astype(jnp.float32))
    firsts[...] = counts_factor(
        n0.astype(jnp.float32) - moves, orders_by_reaction(reaction, 0, 1), float(extents[0])
    )
    real = (n0 >= 0) & (n0 < extents[0])
    in_box = (n0 >= box[0, 0]) & (n0 < box[1, 0])
    kinds[...] = jnp.where(real, jnp.where(in_box, 1, 0), 2)
    table = [
        math.exp(-mean_jumps) * mean_jumps**j / math.factorial(j) for j in range(series_length)
    ]
    for j in range(STEPS):
        series[j] = jnp.float32(table[j])
    for which in range(2):
        tail = jnp.float32(0.0)
        for j in range(STEPS + 1, series_length):
            tail = tail + jnp.where(j <= truncation[which], jnp.float32(table[j]), 0.0)
        series[STEPS + which] = jnp.float32(table[STEPS]) + tail
    wait_all(stay_copies)


def split_product(values, matrix):
    high = values.astype(jnp.bfloat16)
    low = (values - high.astype(jnp.float32)).astype(jnp.bfloat16)
    return jnp.dot(high, matrix, preferred_element_type=jnp.float32) + jnp.dot(
        low, matrix, preferred_element_type=jnp.float32
    )


def parity_matrix(transposed):
    size = 2 * LANES
    third = lax.broadcasted_iota(jnp.int32, (size, size), 1 if transposed else 0)
    place = lax.broadcasted_iota(jnp.int32, (size, size), 0 if transposed else 1)
    return jnp.where(place == (third & 1) * LANES + (third >> 1), 1.0, 0.0).astype(jnp.bfloat16)


class Segment:
    def __init__(self, count, own, table, source, target, totals):
        self.count, self.own, self.table = count, own, table
        self.source, self.target, self.totals = source, target, totals


class Lattice:
    def __init__(self, rows, which, tables, weights, free, stay, p, acc, moved_layers):
        self.rows, self.plane = rows, 2 * rows
        self.which = which
        self.offsets, self.series, self.firsts, self.kinds = tables
        self.weights, self.free, self.stay = weights, free, stay
        self.p, self.acc, self.moved_layers = p, acc, moved_layers
        self.never = jnp.full((ROWS, LANES), self.kinds[0, 0], jnp.int32) < 0

    def moved(self, turn, row):
        return PAD + (turn + 1) * self.moved_layers * self.plane + row

    def kind(self, table):
        return self.kinds[0, ABOVE + table]

    def first(self, table, r):
        return self.firsts[r, ABOVE + table]

    def mask(self, kind, h, row0, count):
        at = pl.multiple_of(kind * self.plane + h * self.rows + row0, 8)
        return self.free[pl.ds(at, count), :]

    def ingest(self, q, values, local, table, target, totals):
        kind = self.kind(table)
        rows = self.rows
        for h in range(2):
            part = values[:, h * LANES : (h + 1) * LANES]
            at = pl.multiple_of(local * self.plane + h * rows, 8)
            self.p[pl.ds(at, rows), :] = part
            if totals is not None:
                at = pl.multiple_of(totals * self.plane + h * rows, 8)
                self.acc[pl.ds(at, rows), :] = part * self.series[0]
            masked = part * self.mask(kind, h, 0, rows)
            at = target * self.plane + h * rows
            for turn in (0, -1, 1):
                lanes = masked if turn == 0 else pltpu.roll(masked, 1 if turn < 0 else LANES - 1, 1)
                q[pl.ds(pl.multiple_of(self.moved(turn, at), 8), rows), :] = lanes

    def coefficients(self, row0):
        return [
            [
                self.weights[pl.ds(pl.multiple_of((r * 2 + h) * self.rows + row0, 8), ROWS), :]
                for h in range(2)
            ]
            for r in range(REACTIONS)
        ]

    def places(self, segments, row0):
        found = []
        for segment in segments:
            own = segment.own * self.plane + row0
            target = segment.target * self.plane + row0
            totals = None if segment.totals is None else segment.totals * self.plane + row0
            shift = segment.source * self.plane + row0
            sources = [
                [self.offsets[self.which * 12 + r * 2 + h] + shift for h in range(2)]
                for r in range(REACTIONS)
            ]
            for u in range(segment.count):
                found.append((segment, u, own, target, totals, sources))
        return found

    def value(self, source, place, h, coefficients, firsts, rolled=None):
        segment, u, own, _, _, sources = place
        at = pl.multiple_of(own + u * self.plane + h * self.rows, 8)
        value = self.p[pl.ds(at, ROWS), :]
        if rolled is not None:
            value = jnp.where(self.never, rolled, value)
        value = value * self.stay[pl.ds(at, ROWS), :]
        terms = [value]
        for r in range(REACTIONS):
            arriving = source[pl.ds(sources[r][h] + u * self.plane, ROWS), :]
            term = arriving * coefficients[r][h]
            terms.append(term if r == 0 else term * firsts[r])
        while len(terms) > 1:
            pairs = [terms[i : i + 2] for i in range(0, len(terms), 2)]
            terms = [pair[0] + pair[1] if len(pair) == 2 else pair[0] for pair in pairs]
        return at, terms[0]

    def advance(self, k, source, target, blocks, layout, totals_by_layer=None):
        weight = self.series[k]
        plane, rows = self.plane, self.rows
        counts = [segment.count for segment in layout(0)]
        size = sum(counts)
        offsets = [(s, u) for s, count in enumerate(counts) for u in range(count)]
        lag = min(6, size // 2)

        def center_row(before, index, h):
            s, u = offsets[index]
            return before[s] + u * plane + h * rows

        def roll_layer(before, index):
            pairs = []
            for h in range(2):
                at = self.moved(0, center_row(before, index, h))
                values = target[pl.ds(pl.multiple_of(at, 8), ROWS), :]
                pairs.append((pltpu.roll(values, 1, 1), pltpu.roll(values, LANES - 1, 1)))
            return pairs

        def store_layer(before, index, pairs):
            for h in range(2):
                row = center_row(before, index, h)
                for side, turn in enumerate((-1, 1)):
                    at = pl.multiple_of(self.moved(turn, row), 8)
                    target[pl.ds(at, ROWS), :] = pairs[h][side]

        def group(g, before):
            row0 = pl.multiple_of(g * ROWS, ROWS)
            coefficients = self.coefficients(row0)

            def block(b, before):
                places = self.places(layout(b), row0)
                rolled = [roll_layer(before, index) for index in range(size)]
                stored = 0
                for index, place in enumerate(places):
                    segment, u, own, target0, totals0, _ = place
                    table = segment.table + u
                    kind = self.kind(table)
                    firsts = [None] + [self.first(table, r) for r in range(1, REACTIONS)]
                    ready = -1
                    if index >= lag:
                        ready = ((index - lag + 1) * size + size - lag - 1) // (size - lag) - 1
                    for h in range(2):
                        at, value = self.value(
                            source, place, h, coefficients, firsts,
                            rolled[ready][1][1] if ready >= 0 and h == 1 else None,
                        )
                        self.p[pl.ds(at, ROWS), :] = value
                        masked = value * self.mask(kind, h, row0, ROWS)
                        row = target0 + u * plane + h * rows
                        target[pl.ds(pl.multiple_of(self.moved(0, row), 8), ROWS), :] = masked
                        if totals_by_layer is None or totals_by_layer[index]:
                            at = pl.ds(pl.multiple_of(totals0 + u * plane + h * rows, 8), ROWS)
                            total = value * weight
                            if totals_by_layer is None or totals_by_layer[index] == "add":
                                total = total + self.acc[at, :]
                            self.acc[at, :] = total
                    while stored <= ready:
                        store_layer(before, stored, rolled[stored])
                        stored += 1
                while stored < size:
                    store_layer(before, stored, rolled[stored])
                    stored += 1
                return tuple(
                    pl.multiple_of(jnp.int32(segment.target * plane) + row0, 8)
                    for segment in layout(b)
                )

            return lax.fori_loop(0, blocks, block, before)

        before = tuple(jnp.int32(segment.target * plane) for segment in layout(jnp.int32(0)))
        last = lax.fori_loop(0, rows // ROWS, group, before)
        for index in range(size):
            store_layer(last, index, roll_layer(last, index))

    def finish(self, source, blocks, layout, more=None, fresh=None):
        weight_density = self.series[STEPS]
        weight_totals = self.series[STEPS + 1]

        def group(g, sums):
            row0 = pl.multiple_of(g * ROWS + HALO, 8)
            coefficients = self.coefficients(row0)

            def block(b, sums):
                mass, hit = sums
                for index, place in enumerate(self.places(layout(b), row0)):
                    segment, u, _, _, totals0, _ = place
                    table = segment.table + u
                    kind = self.kind(table)
                    firsts = [None] + [self.first(table, r) for r in range(1, REACTIONS)]
                    for h in range(2):
                        _, value = self.value(source, place, h, coefficients, firsts)
                        row = pl.multiple_of(totals0 + u * self.plane + h * self.rows, 8)
                        so_far = (self.acc if more is None else more)[pl.ds(row, ROWS), :]
                        if more is not None and not fresh[index]:
                            so_far = so_far + self.acc[pl.ds(row, ROWS), :]
                        totals = so_far + value * weight_totals
                        mass = mass + totals
                        hit = hit + totals * (1.0 - self.mask(kind, h, row0, ROWS))
                        self.acc[pl.ds(row, ROWS), :] = so_far + value * weight_density
                return mass, hit

            return lax.fori_loop(0, blocks, block, sums)

        zero = jnp.zeros((ROWS, LANES), jnp.float32)
        return lax.fori_loop(0, (self.rows - 2 * HALO) // ROWS, group, (zero, zero))

    def restore(self, local, out, index, matrix):
        own = self.rows - 2 * HALO
        even = self.acc[pl.ds(pl.multiple_of(local * self.plane + HALO, 8), own), :]
        odd = self.acc[pl.ds(pl.multiple_of(local * self.plane + self.rows + HALO, 8), own), :]
        out[index] = split_product(jnp.concatenate([even, odd], axis=1), matrix)


def copy_all(copies):
    for copy in copies:
        copy.start()
    return copies


def wait_all(copies):
    for copy in copies:
        copy.wait()


def in_groups(count, limit, function):
    size = largest_divisor(count, limit)

    def several(g, carry):
        for i in range(size):
            function(g * size + i)
        return carry

    lax.fori_loop(0, count // size, several, 0)


def sends_kernel(source, *refs):
    outs, stages, sems = refs[:4], refs[4:6], refs[6]
    loads, stores = [], []
    for j, (axis, dim) in enumerate((("gy", 1), ("gx", 0))):
        odd = lax.axis_index(axis) & 1
        last = source.shape[dim] - HALO
        for i, start in enumerate(((1 - odd) * last, odd * last)):
            at = pl.ds(pl.multiple_of(start, HALO), HALO)
            piece = source.at[at] if dim == 0 else source.at[:, at]
            loads.append(pltpu.make_async_copy(piece, stages[j].at[i], sems.at[2 * j + i]))
    copy_all(loads)
    for j in range(2):
        for i in range(2):
            loads[2 * j + i].wait()
            stores.append(
                pltpu.make_async_copy(stages[j].at[i], outs[2 * j + i], sems.at[4 + 2 * j + i])
            )
            stores[-1].start()
    wait_all(stores)


def corners_kernel(first_in, second_in, offsets, first, second):
    odd = lax.axis_index("gx") & 1
    last = first_in.shape[0] - HALO
    swapped = (lax.axis_index("gy") & 1) == 0
    for out, start in ((first, (1 - odd) * last), (second, odd * last)):
        at = pl.ds(pl.multiple_of(start, HALO), HALO)
        low, high = first_in[at], second_in[at]
        out[:, pl.ds(0, HALO)] = jnp.where(swapped, high, low)
        out[:, pl.ds(HALO, HALO)] = jnp.where(swapped, low, high)


def interior_kernel(
    dims,
    density, first_side, second_side, stay_all, weights_all, free, offsets, series, firsts, kinds,
    occupancy, q_edges, p_edges, acc_edges, sums,
    p, acc, q0, q1, stay, block, staged, sem_in, sem_late, weights, sem_edges, sem_out,
):
    block_first, block_second, _, _ = dims
    rows = block_second + 2 * HALO
    plane = 2 * rows
    chunk = 8
    chunks = block_first // chunk
    even = (lax.axis_index("gy") & 1) == 0
    lattice = Lattice(
        rows, 0, (offsets, series, firsts, kinds), weights, free, stay, p, acc, block_first
    )
    loads = [
        pltpu.make_async_copy(
            density.at[pl.ds(c * chunk, chunk)], block.at[pl.ds(c * chunk, chunk)], sem_in.at[c]
        )
        for c in range(chunks)
    ]
    copy_all(loads)
    late = [
        pltpu.make_async_copy(
            stay_all.at[pl.ds(HALO * plane, block_first * plane)], stay, sem_late.at[0]
        ),
        pltpu.make_async_copy(weights_all, weights, sem_late.at[1]),
    ]
    copy_all(late)
    spread = parity_matrix(False)
    for c in range(chunks):
        loads[c].wait()

        def layer(i, c=c):
            local = c * chunk + i
            first, second = first_side[local], second_side[local]
            below = jnp.where(even, second, first)
            above = jnp.where(even, first, second)
            values = jnp.concatenate([below, block[local], above], axis=0)
            lattice.ingest(
                q0, split_product(values, spread), local, local + HALO, local, local
            )

        in_groups(chunk, 8, layer)
    wait_all(late)

    edges = []

    def export(k):
        q = (q0, q1)[k % 2]
        for side in range(2):
            layer = 2 * k if side == 0 else block_first - 2 * k - 4
            for turn in (-1, 0, 1):
                edges.append(
                    pltpu.make_async_copy(
                        q.at[pl.ds(lattice.moved(turn, layer * plane), 4 * plane)],
                        q_edges.at[k, side, turn + 1],
                        sem_edges.at[(k * 2 + side) * 4 + turn + 1],
                    )
                )
                edges[-1].start()
            layer = 2 * k if side == 0 else block_first - 2 * k - 2
            edges.append(
                pltpu.make_async_copy(
                    p.at[pl.ds(layer * plane, 2 * plane)],
                    p_edges.at[k, side],
                    sem_edges.at[(k * 2 + side) * 4 + 3],
                )
            )
            edges[-1].start()

    def layout_of(low, unroll):
        def layout(b):
            local = low + b * unroll
            return [Segment(unroll, local, local + HALO, local, local, local)]

        return layout

    export(0)
    for k in range(1, STEPS):
        low, high = 2 * k, block_first - 2 * k
        unroll = largest_divisor(high - low, BODY_LAYERS)
        lattice.advance(
            k, (q0, q1)[(k - 1) % 2], (q0, q1)[k % 2], (high - low) // unroll, layout_of(low, unroll)
        )
        export(k)
    for side in range(2):
        layer = 0 if side == 0 else block_first - HALO
        edges.append(
            pltpu.make_async_copy(
                acc.at[pl.ds(layer * plane, HALO * plane)], acc_edges.at[side], sem_edges.at[32 + side]
            )
        )
        edges[-1].start()
    inner = block_first - 2 * HALO
    unroll = largest_divisor(inner, 8)
    mass, hit = lattice.finish((q0, q1)[(STEPS - 1) % 2], inner // unroll, layout_of(HALO, unroll))
    sums[pl.ds(0, ROWS), :] = mass
    sums[pl.ds(ROWS, ROWS), :] = hit
    gather = parity_matrix(True)
    outs = []
    part = largest_divisor(inner, 8)
    for c in range(inner // part):
        in_groups(
            part, 4, lambda i, c=c: lattice.restore(HALO + c * part + i, staged, c * part + i, gather)
        )
        outs.append(
            pltpu.make_async_copy(
                staged.at[pl.ds(c * part, part)],
                occupancy.at[pl.ds(HALO + c * part, part)],
                sem_out.at[c],
            )
        )
        outs[-1].start()
    wait_all(outs)
    wait_all(edges)


SIDE = 2 * HALO + 2
SIDE_MOVED = HALO + 4


def edges_kernel(
    dims, devices,
    first_halo, second_halo, first_corner, second_corner, stay_all, q_edges, p_edges, acc_edges, sums_in,
    weights_all, free, offsets, series, firsts, kinds, occupancy_in,
    occupancy, row_out,
    p, acc, q0, q1, q2, q3, stay, earlier, weights, staged, sem_q, sem_p, sem_other, sem_out,
):
    block_first, block_second, extents, _ = dims
    rows = block_second + 2 * HALO
    plane = 2 * rows
    q = (q0, q1, q2, q3)
    right_table = block_first - 2
    lattice = Lattice(
        rows, 1, (offsets, series, firsts, kinds), weights, free, stay, p, acc, 2 * SIDE_MOVED
    )
    early, late, imports = [], [], []
    p_imports = [[] for _ in range(STEPS)]
    for side in range(2):
        first = 2
        early.append(
            pltpu.make_async_copy(
                stay_all.at[pl.ds(((0, right_table)[side] + first) * plane, (SIDE - 4) * plane)],
                stay.at[pl.ds((side * SIDE + first) * plane, (SIDE - 4) * plane)],
                sem_other.at[side],
            )
        )
        late.append(
            pltpu.make_async_copy(
                acc_edges.at[side],
                earlier.at[pl.ds(side * HALO * plane, HALO * plane)],
                sem_other.at[2 + side],
            )
        )
        for k in range(STEPS):
            layer = 2 * k + HALO if side == 0 else SIDE + 8 - 2 * k
            p_imports[k].append(
                pltpu.make_async_copy(
                    p_edges.at[k, side], p.at[pl.ds(layer * plane, 2 * plane)], sem_p.at[k * 2 + side]
                )
            )
    for k in range(STEPS):
        imports.append([])
        for side in range(2):
            layer = HALO if side == 0 else SIDE_MOVED
            for turn in (-1, 0, 1):
                imports[k].append(
                    pltpu.make_async_copy(
                        q_edges.at[k, side, turn + 1],
                        q[k].at[pl.ds(lattice.moved(turn, layer * plane), 4 * plane)],
                        sem_q.at[(k * 2 + side) * 3 + turn + 1],
                    )
                )
    early.append(pltpu.make_async_copy(weights_all, weights, sem_other.at[4]))
    copy_all(imports[0] + early + p_imports[0])
    spread = parity_matrix(False)
    even = (lax.axis_index("gx") & 1) == 0
    for side in range(2):

        def layer(i, side=side):
            take_first = even if side == 1 else ~even
            corner = jnp.where(take_first, first_corner[i], second_corner[i])
            main = jnp.where(take_first, first_halo[i], second_halo[i])
            values = jnp.concatenate([corner[:HALO], main, corner[HALO:]], axis=0)
            lattice.ingest(
                q0,
                split_product(values, spread),
                i if side == 0 else SIDE + 10 + i,
                i if side == 0 else block_first + HALO + i,
                i if side == 0 else SIDE_MOVED + 4 + i,
                None,
            )

        in_groups(HALO, 4, layer)
    wait_all(early)

    def layout_of(k):
        def layout(b):
            return [
                Segment(HALO, 2 * k, 2 * k, 2, 0, 2 * k - HALO),
                Segment(
                    HALO, SIDE + 10 - 2 * k, block_first + HALO - 2 * k,
                    SIDE_MOVED + 2, SIDE_MOVED + 4, 2 * HALO - 2 * k,
                ),
            ]

        return layout

    for k in range(1, STEPS):
        wait_all(imports[k - 1] + p_imports[k - 1])
        copy_all(imports[k] + p_imports[k])
        if k == STEPS - 1:
            copy_all(late)
        own = [
            None if u < HALO - 2 * k else "new" if u >= HALO - 2 else "add" for u in range(HALO)
        ]
        own += own[::-1]
        lattice.advance(k, q[k - 1], q[k], 1, layout_of(k), own)
    wait_all(imports[STEPS - 1] + p_imports[STEPS - 1] + late)
    fresh = [u >= HALO - 2 for u in range(HALO)]
    mass, hit = lattice.finish(q[STEPS - 1], 1, layout_of(STEPS), earlier, fresh + fresh[::-1])
    gather = parity_matrix(True)
    outs = []
    for side in range(2):
        in_groups(
            HALO,
            4,
            lambda i, side=side: lattice.restore(side * HALO + i, staged, side * HALO + i, gather),
        )
        outs.append(
            pltpu.make_async_copy(
                staged.at[pl.ds(side * HALO, HALO)],
                occupancy.at[pl.ds(0 if side == 0 else block_first - HALO, HALO)],
                sem_out.at[side],
            )
        )
        outs[-1].start()
    share = 1.0 / math.prod(extents)
    mass = jnp.sum(mass + sums_in[pl.ds(0, ROWS), :]) * share
    hit = jnp.sum(hit + sums_in[pl.ds(ROWS, ROWS), :]) * share
    lane = lax.broadcasted_iota(jnp.int32, (devices, LANES), 1)
    row_out[...] = jnp.where(lane == 0, hit, jnp.where(lane == 1, mass, 0.0))
    wait_all(outs)


def body(density, reaction_rates, state_changes, target_box, truncation):
    block_first, block_second, species_third = density.shape
    extents = (
        block_first * lax.axis_size("gx"),
        block_second * lax.axis_size("gy"),
        species_third,
    )
    count_first, count_second = lax.axis_size("gx"), lax.axis_size("gy")
    devices = count_first * count_second
    rows = block_second + 2 * HALO
    plane = 2 * rows
    layers = block_first + 2 * HALO
    dims = (block_first, block_second, extents, (block_first, 2 * SIDE_MOVED))

    def exchange(pieces, axis, count):
        received = []
        for start, piece in enumerate(pieces):
            pairs = [(i, i + 1) for i in range(start, count - 1, 2)]
            received.append(lax.ppermute(piece, axis, pairs + [(j, i) for i, j in pairs]))
        return received

    f32 = jnp.float32
    smem = pl.BlockSpec(memory_space=pltpu.SMEM)
    vmem = pl.BlockSpec(memory_space=pltpu.VMEM)
    hbm = pl.BlockSpec(memory_space=pl.ANY)
    params = pltpu.CompilerParams(vmem_limit_bytes=VMEM_LIMIT)
    light = pl.CostEstimate(flops=1000, bytes_accessed=1000, transcendentals=0)
    side_shape = (block_first, HALO, species_third)
    halo_shape = (HALO, block_second, species_third)
    sends = pl.pallas_call(
        sends_kernel,
        out_shape=(jax.ShapeDtypeStruct(side_shape, f32),) * 2
        + (jax.ShapeDtypeStruct(halo_shape, f32),) * 2,
        in_specs=[hbm],
        out_specs=(hbm,) * 4,
        scratch_shapes=[
            pltpu.VMEM((2,) + side_shape, f32),
            pltpu.VMEM((2,) + halo_shape, f32),
            pltpu.SemaphoreType.DMA((8,)),
        ],
        compiler_params=params,
        cost_estimate=light,
        name="sends",
    )(density)
    first_side, second_side = exchange(sends[:2], "gy", count_second)
    first_halo, second_halo = exchange(sends[2:], "gx", count_first)

    table_lanes = -(-(layers + 2 * ABOVE) // LANES) * LANES
    stay, weights, free, *tables = pl.pallas_call(
        functools.partial(tables_kernel, dims),
        out_shape=(
            jax.ShapeDtypeStruct((layers * plane, LANES), f32),
            jax.ShapeDtypeStruct((12 * rows, LANES), f32),
            jax.ShapeDtypeStruct((6 * rows, LANES), f32),
            jax.ShapeDtypeStruct((24,), jnp.int32),
            jax.ShapeDtypeStruct((STEPS + 2,), f32),
            jax.ShapeDtypeStruct((8, table_lanes), f32),
            jax.ShapeDtypeStruct((8, table_lanes), jnp.int32),
        ),
        in_specs=[smem] * 4,
        out_specs=(hbm, vmem, vmem, smem, smem, vmem, vmem),
        scratch_shapes=[
            pltpu.VMEM((layers * plane, LANES), f32),
            pltpu.SemaphoreType.DMA((layers // largest_divisor(layers, 8),)),
        ],
        compiler_params=params,
        cost_estimate=light,
        name="tables",
    )(reaction_rates, state_changes.T, target_box, truncation)
    offsets = tables[0]

    corner = jax.ShapeDtypeStruct((HALO, 2 * HALO, species_third), f32)
    corner_sends = pl.pallas_call(
        corners_kernel,
        out_shape=(corner, corner),
        in_specs=[vmem, vmem, smem],
        out_specs=(vmem, vmem),
        compiler_params=params,
        cost_estimate=light,
        name="corners",
    )(first_side, second_side, offsets)
    first_corner, second_corner = exchange(corner_sends, "gx", count_first)

    def scratch(own, totals, moved, steps):
        return (
            [pltpu.VMEM((own * plane, LANES), f32), pltpu.VMEM((totals * plane, LANES), f32)]
            + [pltpu.VMEM((3 * moved * plane + 2 * PAD, LANES), f32) for _ in range(steps)]
            + [pltpu.VMEM((own * plane, LANES), f32)]
        )

    chunks = block_first // 8
    occupancy, q_edges, p_edges, acc_edges, sums = pl.pallas_call(
        functools.partial(interior_kernel, dims),
        out_shape=(
            jax.ShapeDtypeStruct(density.shape, f32),
            jax.ShapeDtypeStruct((STEPS, 2, 3, 4 * plane, LANES), f32),
            jax.ShapeDtypeStruct((STEPS, 2, 2 * plane, LANES), f32),
            jax.ShapeDtypeStruct((2, HALO * plane, LANES), f32),
            jax.ShapeDtypeStruct((2 * ROWS, LANES), f32),
        ),
        in_specs=[hbm, vmem, vmem, hbm, hbm, vmem] + [smem] * 4,
        out_specs=(hbm, hbm, hbm, hbm, vmem),
        scratch_shapes=scratch(block_first, block_first, block_first, 2)
        + [
            pltpu.VMEM((block_first, block_second, species_third), f32),
            pltpu.VMEM((block_first - 2 * HALO, block_second, species_third), f32),
            pltpu.SemaphoreType.DMA((chunks,)),
            pltpu.SemaphoreType.DMA((2,)),
            pltpu.VMEM((12 * rows, LANES), f32),
            pltpu.SemaphoreType.DMA((34,)),
            pltpu.SemaphoreType.DMA((block_first // HALO,)),
        ],
        compiler_params=params,
        cost_estimate=light,
        name="interior",
    )(density, first_side, second_side, stay, weights, free, *tables)

    occupancy, row = pl.pallas_call(
        functools.partial(edges_kernel, dims, devices),
        out_shape=(
            jax.ShapeDtypeStruct(density.shape, f32),
            jax.ShapeDtypeStruct((devices, LANES), f32),
        ),
        in_specs=[vmem] * 4 + [hbm] * 4 + [vmem, hbm, vmem] + [smem] * 4 + [hbm],
        out_specs=(hbm, vmem),
        scratch_shapes=scratch(2 * SIDE, 2 * HALO, 2 * SIDE_MOVED, STEPS)
        + [
            pltpu.VMEM((2 * HALO * plane, LANES), f32),
            pltpu.VMEM((12 * rows, LANES), f32),
            pltpu.VMEM((2 * HALO, block_second, species_third), f32),
            pltpu.SemaphoreType.DMA((24,)),
            pltpu.SemaphoreType.DMA((8,)),
            pltpu.SemaphoreType.DMA((5,)),
            pltpu.SemaphoreType.DMA((2,)),
        ],
        input_output_aliases={15: 0},
        compiler_params=params,
        name="edges",
    )(
        first_halo, second_halo, first_corner, second_corner, stay, q_edges, p_edges, acc_edges, sums,
        weights, free, *tables, occupancy,
    )
    rows_in = lax.all_to_all(row, ("gx", "gy"), 0, 0, tiled=True)
    summary = jnp.sum(rows_in[:, :2], axis=0)
    return occupancy, summary


def solution(mesh):
    placed = (P("gx", "gy", None), P(), P(), P(), P())
    return jax.shard_map(
        body, mesh=mesh, in_specs=placed, out_specs=(P("gx", "gy", None), P()), check_vma=False
    )
```

```python
import functools
import math

import jax
import jax.numpy as jnp
from jax import lax
from jax.experimental import pallas as pl
from jax.experimental.pallas import tpu as pltpu
from jax.sharding import PartitionSpec as P

STEPS = 4
REACTIONS = 6
HALO = 2 * STEPS
LANES = 128
ROWS = 16
PAD = 8
BODY_LAYERS = 28

mean_jumps = 8.0
headroom = 1.05
series_length = 40

VMEM_LIMIT = 62 << 20


ABOVE = 2


def largest_divisor(number, limit):
    return max(u for u in range(1, limit + 1) if number % u == 0)


def counts_factor(values, order, extent):
    linear = values * (1.0 / extent)
    square = values * (values - 1.0) * (1.0 / (extent * extent))
    return jnp.where(order == 0, 1.0, jnp.where(order == 1, linear, square))


def tables_kernel(
    dims, rates, changes, box, truncation, density, side_send,
    stay, weights, free, offsets, series, firsts, kinds, first_send, second_send,
    staged, sent, sem_stay, sem_sends,
):
    block_first, block_second, extents, kernel_layers = dims
    rows = block_second + 2 * HALO
    plane = 2 * rows
    layers = block_first + 2 * HALO
    anchor_first = lax.axis_index("gx") * block_first - HALO
    anchor_second = lax.axis_index("gy") * block_second - HALO
    send_loads = start_sends("gx", 0, density, sent, sem_sends)

    plain = jnp.int32(REACTIONS - 1)
    for r in range(REACTIONS - 2, -1, -1):
        plain = jnp.where(changes[0, r] == 2, r, plain)

    def reaction_of(r):
        return jnp.where(r == 0, plain, jnp.where(r == plain, 0, r))

    def change(d, r):
        return changes[d, reaction_of(r)]

    def rate(r):
        return rates[reaction_of(r)]

    def order(r, d):
        return jnp.maximum(-change(d, r), 0)

    def by_reaction(index, value, copies=1):
        found = jnp.zeros(index.shape, jnp.float32)
        for r in range(REACTIONS):
            here = index == r
            for c in range(1, copies):
                here = here | (index == r + c * REACTIONS)
            found = jnp.where(here, value(r), found)
        return found

    def orders_by_reaction(index, d, copies):
        return by_reaction(index, lambda r: order(r, d).astype(jnp.float32), copies)

    corner = jnp.float32(0.0)
    for r in range(REACTIONS):
        term = rate(r)
        for d in range(3):
            e = float(extents[d])
            s = order(r, d)
            term = term * jnp.where(
                s == 0, 1.0, jnp.where(s == 1, (e - 1.0) / e, (e - 1.0) * (e - 2.0) / (e * e))
            )
        corner = corner + term
    inverse = 1.0 / jnp.full((rows, LANES), headroom * corner, jnp.float32)
    row = lax.broadcasted_iota(jnp.int32, (rows, LANES), 0) + anchor_second
    lane = lax.broadcasted_iota(jnp.int32, (rows, LANES), 1)
    real_row = (row >= 0) & (row < extents[1])
    box_row = (row >= box[0, 1]) & (row < box[1, 1])
    for h in range(2):
        third = 2 * lane + h
        box_here = box_row & (third >= box[0, 2]) & (third < box[1, 2])
        free[pl.ds(h * rows, rows), :] = jnp.where(real_row, 1.0, 0.0)
        free[pl.ds(plane + h * rows, rows), :] = jnp.where(real_row & ~box_here, 1.0, 0.0)
        free[pl.ds(2 * plane + h * rows, rows), :] = jnp.zeros((rows, LANES), jnp.float32)

    copies = 3
    split_lane = lax.broadcasted_iota(jnp.int32, (1, LANES), 1)
    first_order = orders_by_reaction(split_lane, 0, copies)
    along_rows = jnp.where(
        lane < copies * REACTIONS,
        counts_factor(
            row.astype(jnp.float32),
            orders_by_reaction(split_lane, 1, copies),
            float(extents[1]),
        )
        * by_reaction(split_lane, lambda r: rate(r), copies)
        * inverse,
        0.0,
    )
    term = lax.broadcasted_iota(jnp.int32, (LANES, 2 * LANES), 0)
    place = lax.broadcasted_iota(jnp.int32, (LANES, 2 * LANES), 1)
    third = 2 * (place & (LANES - 1)) + (place >> 7)
    along_third = counts_factor(
        third.astype(jnp.float32),
        orders_by_reaction(term[:, :LANES], 2, copies)[:, :1],
        float(extents[2]),
    )
    high = along_third.astype(jnp.bfloat16).astype(jnp.float32)
    low = along_third - high
    is_low = (term >= REACTIONS) & (term < 2 * REACTIONS)
    along_third = jnp.where(
        term < copies * REACTIONS, jnp.where(is_low, low, high), 0.0
    ).astype(jnp.bfloat16)

    stay_copies = []
    chunk = largest_divisor(layers, 8)

    def stay_layer(i):
        n0 = anchor_first + i
        real = (n0 >= 0) & (n0 < extents[0])
        in_box = (n0 >= box[0, 0]) & (n0 < box[1, 0])
        kind = jnp.where(real, jnp.where(in_box, 1, 0), 2)
        along_first = counts_factor(
            jnp.full((1, LANES), n0, jnp.int32).astype(jnp.float32), first_order, float(extents[0])
        )
        whole = along_rows * along_first
        upper = whole.astype(jnp.bfloat16).astype(jnp.float32)
        split = jnp.where(lane < 2 * REACTIONS, upper, whole - upper).astype(jnp.bfloat16)
        total = jnp.dot(split, along_third, preferred_element_type=jnp.float32)
        for h in range(2):
            mask = free[pl.ds(pl.multiple_of(kind * plane + h * rows, 8), rows), :]
            at = pl.multiple_of(i * plane + h * rows, 8)
            staged[pl.ds(at, rows), :] = 1.0 - mask * total[:, h * LANES : (h + 1) * LANES]

    for c in range(layers // chunk):
        in_groups(chunk, 4, lambda i, c=c: stay_layer(c * chunk + i))
        at = pl.ds(c * chunk * plane, chunk * plane)
        stay_copies.append(pltpu.make_async_copy(staged.at[at], stay.at[at], sem_stay.at[c]))
        stay_copies[-1].start()
        if c == 0:
            send_stores = finish_sends(send_loads, sent, (first_send, second_send), sem_sends)

    for h in range(2):
        third = 2 * lane + h

        def coefficient(r, carry, h=h, third=third):
            from_row = row - change(1, r)
            from_third = third - change(2, r)
            moved = (
                inverse
                * rate(r)
                * counts_factor(from_row.astype(jnp.float32), order(r, 1), float(extents[1]))
                * counts_factor(from_third.astype(jnp.float32), order(r, 2), float(extents[2]))
            )
            inside = (from_third >= 0) & (from_third < extents[2])
            at = pl.ds(pl.multiple_of((r * 2 + h) * rows, 8), rows)
            weights[at, :] = jnp.where(inside, moved, 0.0)
            return carry

        lax.fori_loop(0, REACTIONS, coefficient, 0)
    for which in range(2):
        for r in range(REACTIONS):
            for h in range(2):
                source = h - change(2, r)
                offsets[which * 12 + r * 2 + h] = (
                    PAD
                    + (((source >> 1) + 1) * kernel_layers[which] - change(0, r)) * plane
                    + (source & 1) * rows
                    - change(1, r)
                )
    n0 = lax.broadcasted_iota(jnp.int32, firsts.shape, 1) + (anchor_first - ABOVE)
    reaction = lax.broadcasted_iota(jnp.int32, firsts.shape, 0)
    moves = by_reaction(reaction, lambda r: change(0, r).astype(jnp.float32))
    firsts[...] = counts_factor(
        n0.astype(jnp.float32) - moves, orders_by_reaction(reaction, 0, 1), float(extents[0])
    )
    real = (n0 >= 0) & (n0 < extents[0])
    in_box = (n0 >= box[0, 0]) & (n0 < box[1, 0])
    kinds[...] = jnp.where(real, jnp.where(in_box, 1, 0), 2)
    table = [
        math.exp(-mean_jumps) * mean_jumps**j / math.factorial(j) for j in range(series_length)
    ]
    for j in range(STEPS):
        series[j] = jnp.float32(table[j])
    for which in range(2):
        tail = jnp.float32(0.0)
        for j in range(STEPS + 1, series_length):
            tail = tail + jnp.where(j <= truncation[which], jnp.float32(table[j]), 0.0)
        series[STEPS + which] = jnp.float32(table[STEPS]) + tail
    wait_all(send_stores)
    wait_all(stay_copies)


def split_product(values, matrix):
    high = values.astype(jnp.bfloat16)
    low = (values - high.astype(jnp.float32)).astype(jnp.bfloat16)
    return jnp.dot(high, matrix, preferred_element_type=jnp.float32) + jnp.dot(
        low, matrix, preferred_element_type=jnp.float32
    )


def parity_matrix(transposed):
    size = 2 * LANES
    third = lax.broadcasted_iota(jnp.int32, (size, size), 1 if transposed else 0)
    place = lax.broadcasted_iota(jnp.int32, (size, size), 0 if transposed else 1)
    return jnp.where(place == (third & 1) * LANES + (third >> 1), 1.0, 0.0).astype(jnp.bfloat16)


class Segment:
    def __init__(self, count, own, table, source, target, totals):
        self.count, self.own, self.table = count, own, table
        self.source, self.target, self.totals = source, target, totals


class Lattice:
    def __init__(self, rows, which, tables, weights, free, stay, p, acc, moved_layers):
        self.rows, self.plane = rows, 2 * rows
        self.which = which
        self.offsets, self.series, self.firsts, self.kinds = tables
        self.weights, self.free, self.stay = weights, free, stay
        self.p, self.acc, self.moved_layers = p, acc, moved_layers
        self.never = jnp.full((ROWS, LANES), self.kinds[0, 0], jnp.int32) < 0

    def moved(self, turn, row):
        return PAD + (turn + 1) * self.moved_layers * self.plane + row

    def kind(self, table):
        return self.kinds[0, ABOVE + table]

    def first(self, table, r):
        return self.firsts[r, ABOVE + table]

    def mask(self, kind, h, row0, count):
        at = pl.multiple_of(kind * self.plane + h * self.rows + row0, 8)
        return self.free[pl.ds(at, count), :]

    def ingest(self, q, values, local, table, target, totals):
        kind = self.kind(table)
        rows = self.rows
        for h in range(2):
            part = values[:, h * LANES : (h + 1) * LANES]
            at = pl.multiple_of(local * self.plane + h * rows, 8)
            self.p[pl.ds(at, rows), :] = part
            if totals is not None:
                at = pl.multiple_of(totals * self.plane + h * rows, 8)
                self.acc[pl.ds(at, rows), :] = part * self.series[0]
            masked = part * self.mask(kind, h, 0, rows)
            at = target * self.plane + h * rows
            for turn in (0, -1, 1):
                lanes = masked if turn == 0 else pltpu.roll(masked, 1 if turn < 0 else LANES - 1, 1)
                q[pl.ds(pl.multiple_of(self.moved(turn, at), 8), rows), :] = lanes

    def coefficients(self, row0):
        return [
            [
                self.weights[pl.ds(pl.multiple_of((r * 2 + h) * self.rows + row0, 8), ROWS), :]
                for h in range(2)
            ]
            for r in range(REACTIONS)
        ]

    def places(self, segments, row0):
        found = []
        for segment in segments:
            own = segment.own * self.plane + row0
            target = segment.target * self.plane + row0
            totals = None if segment.totals is None else segment.totals * self.plane + row0
            shift = segment.source * self.plane + row0
            sources = [
                [self.offsets[self.which * 12 + r * 2 + h] + shift for h in range(2)]
                for r in range(REACTIONS)
            ]
            for u in range(segment.count):
                found.append((segment, u, own, target, totals, sources))
        return found

    def value(self, source, place, h, coefficients, firsts, rolled=None):
        segment, u, own, _, _, sources = place
        at = pl.multiple_of(own + u * self.plane + h * self.rows, 8)
        value = self.p[pl.ds(at, ROWS), :]
        if rolled is not None:
            value = jnp.where(self.never, rolled, value)
        value = value * self.stay[pl.ds(at, ROWS), :]
        terms = [value]
        for r in range(REACTIONS):
            arriving = source[pl.ds(sources[r][h] + u * self.plane, ROWS), :]
            term = arriving * coefficients[r][h]
            terms.append(term if r == 0 else term * firsts[r])
        while len(terms) > 1:
            pairs = [terms[i : i + 2] for i in range(0, len(terms), 2)]
            terms = [pair[0] + pair[1] if len(pair) == 2 else pair[0] for pair in pairs]
        return at, terms[0]

    def advance(self, k, source, target, blocks, layout, totals_by_layer=None):
        weight = self.series[k]
        plane, rows = self.plane, self.rows
        counts = [segment.count for segment in layout(0)]
        size = sum(counts)
        offsets = [(s, u) for s, count in enumerate(counts) for u in range(count)]
        lag = min(6, size // 2)

        def center_row(before, index, h):
            s, u = offsets[index]
            return before[s] + u * plane + h * rows

        def roll_layer(before, index):
            pairs = []
            for h in range(2):
                at = self.moved(0, center_row(before, index, h))
                values = target[pl.ds(pl.multiple_of(at, 8), ROWS), :]
                pairs.append((pltpu.roll(values, 1, 1), pltpu.roll(values, LANES - 1, 1)))
            return pairs

        def store_layer(before, index, pairs):
            for h in range(2):
                row = center_row(before, index, h)
                for side, turn in enumerate((-1, 1)):
                    at = pl.multiple_of(self.moved(turn, row), 8)
                    target[pl.ds(at, ROWS), :] = pairs[h][side]

        def group(g, before):
            row0 = pl.multiple_of(g * ROWS, ROWS)
            coefficients = self.coefficients(row0)

            def block(b, before):
                places = self.places(layout(b), row0)
                rolled = [roll_layer(before, index) for index in range(size)]
                stored = 0
                for index, place in enumerate(places):
                    segment, u, own, target0, totals0, _ = place
                    table = segment.table + u
                    kind = self.kind(table)
                    firsts = [None] + [self.first(table, r) for r in range(1, REACTIONS)]
                    ready = -1
                    if index >= lag:
                        ready = ((index - lag + 1) * size + size - lag - 1) // (size - lag) - 1
                    for h in range(2):
                        at, value = self.value(
                            source, place, h, coefficients, firsts,
                            rolled[ready][1][1] if ready >= 0 and h == 1 else None,
                        )
                        self.p[pl.ds(at, ROWS), :] = value
                        masked = value * self.mask(kind, h, row0, ROWS)
                        row = target0 + u * plane + h * rows
                        target[pl.ds(pl.multiple_of(self.moved(0, row), 8), ROWS), :] = masked
                        if totals_by_layer is None or totals_by_layer[index]:
                            at = pl.ds(pl.multiple_of(totals0 + u * plane + h * rows, 8), ROWS)
                            total = value * weight
                            if totals_by_layer is None or totals_by_layer[index] == "add":
                                total = total + self.acc[at, :]
                            self.acc[at, :] = total
                    while stored <= ready:
                        store_layer(before, stored, rolled[stored])
                        stored += 1
                while stored < size:
                    store_layer(before, stored, rolled[stored])
                    stored += 1
                return tuple(
                    pl.multiple_of(jnp.int32(segment.target * plane) + row0, 8)
                    for segment in layout(b)
                )

            return lax.fori_loop(0, blocks, block, before)

        before = tuple(jnp.int32(segment.target * plane) for segment in layout(jnp.int32(0)))
        last = lax.fori_loop(0, rows // ROWS, group, before)
        for index in range(size):
            store_layer(last, index, roll_layer(last, index))

    def finish(self, source, blocks, layout, more=None, fresh=None):
        weight_density = self.series[STEPS]
        weight_totals = self.series[STEPS + 1]

        def group(g, sums):
            row0 = pl.multiple_of(g * ROWS + HALO, 8)
            coefficients = self.coefficients(row0)

            def block(b, sums):
                mass, hit = sums
                for index, place in enumerate(self.places(layout(b), row0)):
                    segment, u, _, _, totals0, _ = place
                    table = segment.table + u
                    kind = self.kind(table)
                    firsts = [None] + [self.first(table, r) for r in range(1, REACTIONS)]
                    for h in range(2):
                        _, value = self.value(source, place, h, coefficients, firsts)
                        row = pl.multiple_of(totals0 + u * self.plane + h * self.rows, 8)
                        so_far = (self.acc if more is None else more)[pl.ds(row, ROWS), :]
                        if more is not None and not fresh[index]:
                            so_far = so_far + self.acc[pl.ds(row, ROWS), :]
                        totals = so_far + value * weight_totals
                        mass = mass + totals
                        hit = hit + totals * (1.0 - self.mask(kind, h, row0, ROWS))
                        self.acc[pl.ds(row, ROWS), :] = so_far + value * weight_density
                return mass, hit

            return lax.fori_loop(0, blocks, block, sums)

        zero = jnp.zeros((ROWS, LANES), jnp.float32)
        return lax.fori_loop(0, (self.rows - 2 * HALO) // ROWS, group, (zero, zero))

    def restore(self, local, out, index, matrix):
        own = self.rows - 2 * HALO
        even = self.acc[pl.ds(pl.multiple_of(local * self.plane + HALO, 8), own), :]
        odd = self.acc[pl.ds(pl.multiple_of(local * self.plane + self.rows + HALO, 8), own), :]
        out[index] = split_product(jnp.concatenate([even, odd], axis=1), matrix)


def copy_all(copies):
    for copy in copies:
        copy.start()
    return copies


def wait_all(copies):
    for copy in copies:
        copy.wait()


def in_groups(count, limit, function):
    size = largest_divisor(count, limit)

    def several(g, carry):
        for i in range(size):
            function(g * size + i)
        return carry

    lax.fori_loop(0, count // size, several, 0)


def start_sends(axis, dim, source, stage, sems):
    odd = lax.axis_index(axis) & 1
    last = source.shape[dim] - HALO
    loads = []
    for i, start in enumerate(((1 - odd) * last, odd * last)):
        at = pl.ds(pl.multiple_of(start, HALO), HALO)
        piece = source.at[at] if dim == 0 else source.at[:, at]
        loads.append(pltpu.make_async_copy(piece, stage.at[i], sems.at[i]))
    return copy_all(loads)


def finish_sends(loads, stage, outs, sems):
    stores = []
    for i, out in enumerate(outs):
        loads[i].wait()
        stores.append(pltpu.make_async_copy(stage.at[i], out, sems.at[2 + i]))
        stores[-1].start()
    return stores


def sends_kernel(source, first, second, stage, sems):
    loads = start_sends("gy", 1, source, stage, sems)
    wait_all(finish_sends(loads, stage, (first, second), sems))


def corners_kernel(first_in, second_in, offsets, first, second):
    odd = lax.axis_index("gx") & 1
    last = first_in.shape[0] - HALO
    swapped = (lax.axis_index("gy") & 1) == 0
    for out, start in ((first, (1 - odd) * last), (second, odd * last)):
        at = pl.ds(pl.multiple_of(start, HALO), HALO)
        low, high = first_in[at], second_in[at]
        out[:, pl.ds(0, HALO)] = jnp.where(swapped, high, low)
        out[:, pl.ds(HALO, HALO)] = jnp.where(swapped, low, high)


def interior_kernel(
    dims,
    density, first_side, second_side, stay_all, weights_all, free, offsets, series, firsts, kinds,
    occupancy, q_edges, p_edges, acc_edges, sums,
    p, acc, q0, q1, stay, block, staged, sem_in, sem_late, weights, sem_edges, sem_out,
):
    block_first, block_second, _, _ = dims
    rows = block_second + 2 * HALO
    plane = 2 * rows
    chunk = 8
    chunks = block_first // chunk
    even = (lax.axis_index("gy") & 1) == 0
    lattice = Lattice(
        rows, 0, (offsets, series, firsts, kinds), weights, free, stay, p, acc, block_first
    )
    loads = [
        pltpu.make_async_copy(
            density.at[pl.ds(c * chunk, chunk)], block.at[pl.ds(c * chunk, chunk)], sem_in.at[c]
        )
        for c in range(chunks)
    ]
    copy_all(loads)
    late = [
        pltpu.make_async_copy(
            stay_all.at[pl.ds(HALO * plane, block_first * plane)], stay, sem_late.at[0]
        ),
        pltpu.make_async_copy(weights_all, weights, sem_late.at[1]),
    ]
    copy_all(late)
    spread = parity_matrix(False)
    for c in range(chunks):
        loads[c].wait()

        def layer(i, c=c):
            local = c * chunk + i
            first, second = first_side[local], second_side[local]
            below = jnp.where(even, second, first)
            above = jnp.where(even, first, second)
            values = jnp.concatenate([below, block[local], above], axis=0)
            lattice.ingest(
                q0, split_product(values, spread), local, local + HALO, local, local
            )

        in_groups(chunk, 8, layer)
    wait_all(late)

    edges = []

    def export(k):
        q = (q0, q1)[k % 2]
        for side in range(2):
            layer = 2 * k if side == 0 else block_first - 2 * k - 4
            for turn in (-1, 0, 1):
                edges.append(
                    pltpu.make_async_copy(
                        q.at[pl.ds(lattice.moved(turn, layer * plane), 4 * plane)],
                        q_edges.at[k, side, turn + 1],
                        sem_edges.at[(k * 2 + side) * 4 + turn + 1],
                    )
                )
                edges[-1].start()
            layer = 2 * k if side == 0 else block_first - 2 * k - 2
            edges.append(
                pltpu.make_async_copy(
                    p.at[pl.ds(layer * plane, 2 * plane)],
                    p_edges.at[k, side],
                    sem_edges.at[(k * 2 + side) * 4 + 3],
                )
            )
            edges[-1].start()

    def layout_of(low, unroll):
        def layout(b):
            local = low + b * unroll
            return [Segment(unroll, local, local + HALO, local, local, local)]

        return layout

    export(0)
    for k in range(1, STEPS):
        low, high = 2 * k, block_first - 2 * k
        unroll = largest_divisor(high - low, BODY_LAYERS)
        lattice.advance(
            k, (q0, q1)[(k - 1) % 2], (q0, q1)[k % 2], (high - low) // unroll, layout_of(low, unroll)
        )
        export(k)
    for side in range(2):
        layer = 0 if side == 0 else block_first - HALO
        edges.append(
            pltpu.make_async_copy(
                acc.at[pl.ds(layer * plane, HALO * plane)], acc_edges.at[side], sem_edges.at[32 + side]
            )
        )
        edges[-1].start()
    inner = block_first - 2 * HALO
    unroll = largest_divisor(inner, 8)
    mass, hit = lattice.finish((q0, q1)[(STEPS - 1) % 2], inner // unroll, layout_of(HALO, unroll))
    sums[pl.ds(0, ROWS), :] = mass
    sums[pl.ds(ROWS, ROWS), :] = hit
    gather = parity_matrix(True)
    outs = []
    part = largest_divisor(inner, 8)
    for c in range(inner // part):
        in_groups(
            part, 4, lambda i, c=c: lattice.restore(HALO + c * part + i, staged, c * part + i, gather)
        )
        outs.append(
            pltpu.make_async_copy(
                staged.at[pl.ds(c * part, part)],
                occupancy.at[pl.ds(HALO + c * part, part)],
                sem_out.at[c],
            )
        )
        outs[-1].start()
    wait_all(outs)
    wait_all(edges)


SIDE = 2 * HALO + 2
SIDE_MOVED = HALO + 4


def edges_kernel(
    dims, devices,
    first_halo, second_halo, first_corner, second_corner, stay_all, q_edges, p_edges, acc_edges, sums_in,
    weights_all, free, offsets, series, firsts, kinds, occupancy_in,
    occupancy, row_out,
    p, acc, q0, q1, q2, q3, stay, earlier, weights, staged, sem_q, sem_p, sem_other, sem_out,
):
    block_first, block_second, extents, _ = dims
    rows = block_second + 2 * HALO
    plane = 2 * rows
    q = (q0, q1, q2, q3)
    right_table = block_first - 2
    lattice = Lattice(
        rows, 1, (offsets, series, firsts, kinds), weights, free, stay, p, acc, 2 * SIDE_MOVED
    )
    early, late, imports = [], [], []
    p_imports = [[] for _ in range(STEPS)]
    for side in range(2):
        first = 2
        early.append(
            pltpu.make_async_copy(
                stay_all.at[pl.ds(((0, right_table)[side] + first) * plane, (SIDE - 4) * plane)],
                stay.at[pl.ds((side * SIDE + first) * plane, (SIDE - 4) * plane)],
                sem_other.at[side],
            )
        )
        late.append(
            pltpu.make_async_copy(
                acc_edges.at[side],
                earlier.at[pl.ds(side * HALO * plane, HALO * plane)],
                sem_other.at[2 + side],
            )
        )
        for k in range(STEPS):
            layer = 2 * k + HALO if side == 0 else SIDE + 8 - 2 * k
            p_imports[k].append(
                pltpu.make_async_copy(
                    p_edges.at[k, side], p.at[pl.ds(layer * plane, 2 * plane)], sem_p.at[k * 2 + side]
                )
            )
    for k in range(STEPS):
        imports.append([])
        for side in range(2):
            layer = HALO if side == 0 else SIDE_MOVED
            for turn in (-1, 0, 1):
                imports[k].append(
                    pltpu.make_async_copy(
                        q_edges.at[k, side, turn + 1],
                        q[k].at[pl.ds(lattice.moved(turn, layer * plane), 4 * plane)],
                        sem_q.at[(k * 2 + side) * 3 + turn + 1],
                    )
                )
    early.append(pltpu.make_async_copy(weights_all, weights, sem_other.at[4]))
    copy_all(imports[0] + early + p_imports[0])
    spread = parity_matrix(False)
    even = (lax.axis_index("gx") & 1) == 0
    for side in range(2):

        def layer(i, side=side):
            take_first = even if side == 1 else ~even
            corner = jnp.where(take_first, first_corner[i], second_corner[i])
            main = jnp.where(take_first, first_halo[i], second_halo[i])
            values = jnp.concatenate([corner[:HALO], main, corner[HALO:]], axis=0)
            lattice.ingest(
                q0,
                split_product(values, spread),
                i if side == 0 else SIDE + 10 + i,
                i if side == 0 else block_first + HALO + i,
                i if side == 0 else SIDE_MOVED + 4 + i,
                None,
            )

        in_groups(HALO, 4, layer)
    wait_all(early)

    def layout_of(k):
        def layout(b):
            return [
                Segment(HALO, 2 * k, 2 * k, 2, 0, 2 * k - HALO),
                Segment(
                    HALO, SIDE + 10 - 2 * k, block_first + HALO - 2 * k,
                    SIDE_MOVED + 2, SIDE_MOVED + 4, 2 * HALO - 2 * k,
                ),
            ]

        return layout

    for k in range(1, STEPS):
        wait_all(imports[k - 1] + p_imports[k - 1])
        copy_all(imports[k] + p_imports[k])
        if k == STEPS - 1:
            copy_all(late)
        own = [
            None if u < HALO - 2 * k else "new" if u >= HALO - 2 else "add" for u in range(HALO)
        ]
        own += own[::-1]
        lattice.advance(k, q[k - 1], q[k], 1, layout_of(k), own)
    wait_all(imports[STEPS - 1] + p_imports[STEPS - 1] + late)
    fresh = [u >= HALO - 2 for u in range(HALO)]
    mass, hit = lattice.finish(q[STEPS - 1], 1, layout_of(STEPS), earlier, fresh + fresh[::-1])
    gather = parity_matrix(True)
    outs = []
    for side in range(2):
        in_groups(
            HALO,
            4,
            lambda i, side=side: lattice.restore(side * HALO + i, staged, side * HALO + i, gather),
        )
        outs.append(
            pltpu.make_async_copy(
                staged.at[pl.ds(side * HALO, HALO)],
                occupancy.at[pl.ds(0 if side == 0 else block_first - HALO, HALO)],
                sem_out.at[side],
            )
        )
        outs[-1].start()
    share = 1.0 / math.prod(extents)
    mass = jnp.sum(mass + sums_in[pl.ds(0, ROWS), :]) * share
    hit = jnp.sum(hit + sums_in[pl.ds(ROWS, ROWS), :]) * share
    lane = lax.broadcasted_iota(jnp.int32, (devices, LANES), 1)
    row_out[...] = jnp.where(lane == 0, hit, jnp.where(lane == 1, mass, 0.0))
    wait_all(outs)


def body(density, reaction_rates, state_changes, target_box, truncation):
    block_first, block_second, species_third = density.shape
    extents = (
        block_first * lax.axis_size("gx"),
        block_second * lax.axis_size("gy"),
        species_third,
    )
    count_first, count_second = lax.axis_size("gx"), lax.axis_size("gy")
    devices = count_first * count_second
    rows = block_second + 2 * HALO
    plane = 2 * rows
    layers = block_first + 2 * HALO
    dims = (block_first, block_second, extents, (block_first, 2 * SIDE_MOVED))

    def exchange(pieces, axis, count):
        received = []
        for start, piece in enumerate(pieces):
            pairs = [(i, i + 1) for i in range(start, count - 1, 2)]
            received.append(lax.ppermute(piece, axis, pairs + [(j, i) for i, j in pairs]))
        return received

    f32 = jnp.float32
    smem = pl.BlockSpec(memory_space=pltpu.SMEM)
    vmem = pl.BlockSpec(memory_space=pltpu.VMEM)
    hbm = pl.BlockSpec(memory_space=pl.ANY)
    params = pltpu.CompilerParams(vmem_limit_bytes=VMEM_LIMIT)
    heavy = pl.CostEstimate(flops=200_000_000_000, bytes_accessed=400_000_000, transcendentals=0)
    light = pl.CostEstimate(flops=1000, bytes_accessed=1000, transcendentals=0)
    side_shape = (block_first, HALO, species_third)
    halo_shape = (HALO, block_second, species_third)
    side_sends = pl.pallas_call(
        sends_kernel,
        out_shape=(jax.ShapeDtypeStruct(side_shape, f32),) * 2,
        in_specs=[hbm],
        out_specs=(hbm,) * 2,
        scratch_shapes=[pltpu.VMEM((2,) + side_shape, f32), pltpu.SemaphoreType.DMA((4,))],
        compiler_params=params,
        cost_estimate=light,
        name="sends",
    )(density)
    first_side, second_side = exchange(side_sends, "gy", count_second)

    table_lanes = -(-(layers + 2 * ABOVE) // LANES) * LANES
    stay, weights, free, *tables, first_send, second_send = pl.pallas_call(
        functools.partial(tables_kernel, dims),
        out_shape=(
            jax.ShapeDtypeStruct((layers * plane, LANES), f32),
            jax.ShapeDtypeStruct((12 * rows, LANES), f32),
            jax.ShapeDtypeStruct((6 * rows, LANES), f32),
            jax.ShapeDtypeStruct((24,), jnp.int32),
            jax.ShapeDtypeStruct((STEPS + 2,), f32),
            jax.ShapeDtypeStruct((8, table_lanes), f32),
            jax.ShapeDtypeStruct((8, table_lanes), jnp.int32),
            jax.ShapeDtypeStruct(halo_shape, f32),
            jax.ShapeDtypeStruct(halo_shape, f32),
        ),
        in_specs=[smem] * 4 + [hbm, hbm],
        out_specs=(hbm, vmem, vmem, smem, smem, vmem, vmem, hbm, hbm),
        scratch_shapes=[
            pltpu.VMEM((layers * plane, LANES), f32),
            pltpu.VMEM((2,) + halo_shape, f32),
            pltpu.SemaphoreType.DMA((layers // largest_divisor(layers, 8),)),
            pltpu.SemaphoreType.DMA((4,)),
        ],
        compiler_params=params,
        cost_estimate=light,
        name="tables",
    )(reaction_rates, state_changes.T, target_box, truncation, density, side_sends[0])
    first_halo, second_halo = exchange((first_send, second_send), "gx", count_first)
    offsets = tables[0]

    corner = jax.ShapeDtypeStruct((HALO, 2 * HALO, species_third), f32)
    corner_sends = pl.pallas_call(
        corners_kernel,
        out_shape=(corner, corner),
        in_specs=[vmem, vmem, smem],
        out_specs=(vmem, vmem),
        compiler_params=params,
        cost_estimate=light,
        name="corners",
    )(first_side, second_side, offsets)
    first_corner, second_corner = exchange(corner_sends, "gx", count_first)

    def scratch(own, totals, moved, steps):
        return (
            [pltpu.VMEM((own * plane, LANES), f32), pltpu.VMEM((totals * plane, LANES), f32)]
            + [pltpu.VMEM((3 * moved * plane + 2 * PAD, LANES), f32) for _ in range(steps)]
            + [pltpu.VMEM((own * plane, LANES), f32)]
        )

    chunks = block_first // 8
    occupancy, q_edges, p_edges, acc_edges, sums = pl.pallas_call(
        functools.partial(interior_kernel, dims),
        out_shape=(
            jax.ShapeDtypeStruct(density.shape, f32),
            jax.ShapeDtypeStruct((STEPS, 2, 3, 4 * plane, LANES), f32),
            jax.ShapeDtypeStruct((STEPS, 2, 2 * plane, LANES), f32),
            jax.ShapeDtypeStruct((2, HALO * plane, LANES), f32),
            jax.ShapeDtypeStruct((2 * ROWS, LANES), f32),
        ),
        in_specs=[hbm, vmem, vmem, hbm, hbm, vmem] + [smem] * 4,
        out_specs=(hbm, hbm, hbm, hbm, vmem),
        scratch_shapes=scratch(block_first, block_first, block_first, 2)
        + [
            pltpu.VMEM((block_first, block_second, species_third), f32),
            pltpu.VMEM((block_first - 2 * HALO, block_second, species_third), f32),
            pltpu.SemaphoreType.DMA((chunks,)),
            pltpu.SemaphoreType.DMA((2,)),
            pltpu.VMEM((12 * rows, LANES), f32),
            pltpu.SemaphoreType.DMA((34,)),
            pltpu.SemaphoreType.DMA((block_first // HALO,)),
        ],
        compiler_params=params,
        cost_estimate=heavy,
        name="interior",
    )(density, first_side, second_side, stay, weights, free, *tables)

    occupancy, row = pl.pallas_call(
        functools.partial(edges_kernel, dims, devices),
        out_shape=(
            jax.ShapeDtypeStruct(density.shape, f32),
            jax.ShapeDtypeStruct((devices, LANES), f32),
        ),
        in_specs=[vmem] * 4 + [hbm] * 4 + [vmem, hbm, vmem] + [smem] * 4 + [hbm],
        out_specs=(hbm, vmem),
        scratch_shapes=scratch(2 * SIDE, 2 * HALO, 2 * SIDE_MOVED, STEPS)
        + [
            pltpu.VMEM((2 * HALO * plane, LANES), f32),
            pltpu.VMEM((12 * rows, LANES), f32),
            pltpu.VMEM((2 * HALO, block_second, species_third), f32),
            pltpu.SemaphoreType.DMA((24,)),
            pltpu.SemaphoreType.DMA((8,)),
            pltpu.SemaphoreType.DMA((5,)),
            pltpu.SemaphoreType.DMA((2,)),
        ],
        input_output_aliases={15: 0},
        compiler_params=params,
        name="edges",
    )(
        first_halo, second_halo, first_corner, second_corner, stay, q_edges, p_edges, acc_edges, sums,
        weights, free, *tables, occupancy,
    )
    rows_in = lax.all_to_all(row, ("gx", "gy"), 0, 0, tiled=True)
    summary = jnp.sum(rows_in[:, :2], axis=0)
    return occupancy, summary


def solution(mesh):
    placed = (P("gx", "gy", None), P(), P(), P(), P())
    return jax.shard_map(
        body, mesh=mesh, in_specs=placed, out_specs=(P("gx", "gy", None), P()), check_vma=False
    )
```

```python
import functools
import math

import jax
import jax.numpy as jnp
from jax import lax
from jax.experimental import pallas as pl
from jax.experimental.pallas import tpu as pltpu
from jax.sharding import PartitionSpec as P

STEPS = 4
REACTIONS = 6
HALO = 2 * STEPS
LANES = 128
ROWS = 16
PAD = 8
BODY_LAYERS = 14

mean_jumps = 8.0
headroom = 1.05
series_length = 40

VMEM_LIMIT = 62 << 20


ABOVE = 2


def largest_divisor(number, limit):
    return max(u for u in range(1, limit + 1) if number % u == 0)


def counts_factor(values, order, extent):
    linear = values * (1.0 / extent)
    square = values * (values - 1.0) * (1.0 / (extent * extent))
    return jnp.where(order == 0, 1.0, jnp.where(order == 1, linear, square))


def tables_kernel(
    dims, rates, changes, box, truncation, density, side_send,
    stay, weights, free, offsets, series, firsts, kinds, first_send, second_send,
    staged, sent, sem_stay, sem_sends,
):
    block_first, block_second, extents, kernel_layers = dims
    rows = block_second + 2 * HALO
    plane = 2 * rows
    layers = block_first + 2 * HALO
    anchor_first = lax.axis_index("gx") * block_first - HALO
    anchor_second = lax.axis_index("gy") * block_second - HALO
    send_loads = start_sends("gx", 0, density, sent, sem_sends)

    plain = jnp.int32(REACTIONS - 1)
    for r in range(REACTIONS - 2, -1, -1):
        plain = jnp.where(changes[0, r] == 2, r, plain)

    def reaction_of(r):
        return jnp.where(r == 0, plain, jnp.where(r == plain, 0, r))

    def change(d, r):
        return changes[d, reaction_of(r)]

    def rate(r):
        return rates[reaction_of(r)]

    def order(r, d):
        return jnp.maximum(-change(d, r), 0)

    def by_reaction(index, value, copies=1):
        found = jnp.zeros(index.shape, jnp.float32)
        for r in range(REACTIONS):
            here = index == r
            for c in range(1, copies):
                here = here | (index == r + c * REACTIONS)
            found = jnp.where(here, value(r), found)
        return found

    def orders_by_reaction(index, d, copies):
        return by_reaction(index, lambda r: order(r, d).astype(jnp.float32), copies)

    corner = jnp.float32(0.0)
    for r in range(REACTIONS):
        term = rate(r)
        for d in range(3):
            e = float(extents[d])
            s = order(r, d)
            term = term * jnp.where(
                s == 0, 1.0, jnp.where(s == 1, (e - 1.0) / e, (e - 1.0) * (e - 2.0) / (e * e))
            )
        corner = corner + term
    inverse = 1.0 / jnp.full((rows, LANES), headroom * corner, jnp.float32)
    row = lax.broadcasted_iota(jnp.int32, (rows, LANES), 0) + anchor_second
    lane = lax.broadcasted_iota(jnp.int32, (rows, LANES), 1)
    real_row = (row >= 0) & (row < extents[1])
    box_row = (row >= box[0, 1]) & (row < box[1, 1])
    for h in range(2):
        third = 2 * lane + h
        box_here = box_row & (third >= box[0, 2]) & (third < box[1, 2])
        free[pl.ds(h * rows, rows), :] = jnp.where(real_row, 1.0, 0.0)
        free[pl.ds(plane + h * rows, rows), :] = jnp.where(real_row & ~box_here, 1.0, 0.0)
        free[pl.ds(2 * plane + h * rows, rows), :] = jnp.zeros((rows, LANES), jnp.float32)

    copies = 3
    split_lane = lax.broadcasted_iota(jnp.int32, (1, LANES), 1)
    first_order = orders_by_reaction(split_lane, 0, copies)
    along_rows = jnp.where(
        lane < copies * REACTIONS,
        counts_factor(
            row.astype(jnp.float32),
            orders_by_reaction(split_lane, 1, copies),
            float(extents[1]),
        )
        * by_reaction(split_lane, lambda r: rate(r), copies)
        * inverse,
        0.0,
    )
    term = lax.broadcasted_iota(jnp.int32, (LANES, 2 * LANES), 0)
    place = lax.broadcasted_iota(jnp.int32, (LANES, 2 * LANES), 1)
    third = 2 * (place & (LANES - 1)) + (place >> 7)
    along_third = counts_factor(
        third.astype(jnp.float32),
        orders_by_reaction(term[:, :LANES], 2, copies)[:, :1],
        float(extents[2]),
    )
    high = along_third.astype(jnp.bfloat16).astype(jnp.float32)
    low = along_third - high
    is_low = (term >= REACTIONS) & (term < 2 * REACTIONS)
    along_third = jnp.where(
        term < copies * REACTIONS, jnp.where(is_low, low, high), 0.0
    ).astype(jnp.bfloat16)

    stay_copies = []
    chunk = largest_divisor(layers, 8)

    def stay_layer(i):
        n0 = anchor_first + i
        real = (n0 >= 0) & (n0 < extents[0])
        in_box = (n0 >= box[0, 0]) & (n0 < box[1, 0])
        kind = jnp.where(real, jnp.where(in_box, 1, 0), 2)
        along_first = counts_factor(
            jnp.full((1, LANES), n0, jnp.int32).astype(jnp.float32), first_order, float(extents[0])
        )
        whole = along_rows * along_first
        upper = whole.astype(jnp.bfloat16).astype(jnp.float32)
        split = jnp.where(lane < 2 * REACTIONS, upper, whole - upper).astype(jnp.bfloat16)
        total = jnp.dot(split, along_third, preferred_element_type=jnp.float32)
        for h in range(2):
            mask = free[pl.ds(pl.multiple_of(kind * plane + h * rows, 8), rows), :]
            at = pl.multiple_of(i * plane + h * rows, 8)
            staged[pl.ds(at, rows), :] = 1.0 - mask * total[:, h * LANES : (h + 1) * LANES]

    for c in range(layers // chunk):
        in_groups(chunk, 4, lambda i, c=c: stay_layer(c * chunk + i))
        at = pl.ds(c * chunk * plane, chunk * plane)
        stay_copies.append(pltpu.make_async_copy(staged.at[at], stay.at[at], sem_stay.at[c]))
        stay_copies[-1].start()
        if c == 0:
            send_stores = finish_sends(send_loads, sent, (first_send, second_send), sem_sends)

    for h in range(2):
        third = 2 * lane + h

        def coefficient(r, carry, h=h, third=third):
            from_row = row - change(1, r)
            from_third = third - change(2, r)
            moved = (
                inverse
                * rate(r)
                * counts_factor(from_row.astype(jnp.float32), order(r, 1), float(extents[1]))
                * counts_factor(from_third.astype(jnp.float32), order(r, 2), float(extents[2]))
            )
            inside = (from_third >= 0) & (from_third < extents[2])
            at = pl.ds(pl.multiple_of((r * 2 + h) * rows, 8), rows)
            weights[at, :] = jnp.where(inside, moved, 0.0)
            return carry

        lax.fori_loop(0, REACTIONS, coefficient, 0)
    for which in range(2):
        for r in range(REACTIONS):
            for h in range(2):
                source = h - change(2, r)
                offsets[which * 12 + r * 2 + h] = (
                    PAD
                    + (((source >> 1) + 1) * kernel_layers[which] - change(0, r)) * plane
                    + (source & 1) * rows
                    - change(1, r)
                )
    n0 = lax.broadcasted_iota(jnp.int32, firsts.shape, 1) + (anchor_first - ABOVE)
    reaction = lax.broadcasted_iota(jnp.int32, firsts.shape, 0)
    moves = by_reaction(reaction, lambda r: change(0, r).astype(jnp.float32))
    firsts[...] = counts_factor(
        n0.astype(jnp.float32) - moves, orders_by_reaction(reaction, 0, 1), float(extents[0])
    )
    real = (n0 >= 0) & (n0 < extents[0])
    in_box = (n0 >= box[0, 0]) & (n0 < box[1, 0])
    kinds[...] = jnp.where(real, jnp.where(in_box, 1, 0), 2)
    table = [
        math.exp(-mean_jumps) * mean_jumps**j / math.factorial(j) for j in range(series_length)
    ]
    for j in range(STEPS):
        series[j] = jnp.float32(table[j])
    for which in range(2):
        tail = jnp.float32(0.0)
        for j in range(STEPS + 1, series_length):
            tail = tail + jnp.where(j <= truncation[which], jnp.float32(table[j]), 0.0)
        series[STEPS + which] = jnp.float32(table[STEPS]) + tail
    wait_all(send_stores)
    wait_all(stay_copies)


def split_product(values, matrix):
    high = values.astype(jnp.bfloat16)
    low = (values - high.astype(jnp.float32)).astype(jnp.bfloat16)
    return jnp.dot(high, matrix, preferred_element_type=jnp.float32) + jnp.dot(
        low, matrix, preferred_element_type=jnp.float32
    )


def parity_matrix(transposed):
    size = 2 * LANES
    third = lax.broadcasted_iota(jnp.int32, (size, size), 1 if transposed else 0)
    place = lax.broadcasted_iota(jnp.int32, (size, size), 0 if transposed else 1)
    return jnp.where(place == (third & 1) * LANES + (third >> 1), 1.0, 0.0).astype(jnp.bfloat16)


class Segment:
    def __init__(self, count, own, table, source, target, totals):
        self.count, self.own, self.table = count, own, table
        self.source, self.target, self.totals = source, target, totals


class Lattice:
    def __init__(self, rows, which, tables, weights, free, stay, p, acc, moved_layers):
        self.rows, self.plane = rows, 2 * rows
        self.which = which
        self.offsets, self.series, self.firsts, self.kinds = tables
        self.weights, self.free, self.stay = weights, free, stay
        self.p, self.acc, self.moved_layers = p, acc, moved_layers
        self.never = jnp.full((ROWS, LANES), self.kinds[0, 0], jnp.int32) < 0

    def moved(self, turn, row):
        return PAD + (turn + 1) * self.moved_layers * self.plane + row

    def kind(self, table):
        return self.kinds[0, ABOVE + table]

    def first(self, table, r):
        return self.firsts[r, ABOVE + table]

    def mask(self, kind, h, row0, count):
        at = pl.multiple_of(kind * self.plane + h * self.rows + row0, 8)
        return self.free[pl.ds(at, count), :]

    def ingest(self, q, values, local, table, target, totals):
        kind = self.kind(table)
        rows = self.rows
        for h in range(2):
            part = values[:, h * LANES : (h + 1) * LANES]
            at = pl.multiple_of(local * self.plane + h * rows, 8)
            self.p[pl.ds(at, rows), :] = part
            if totals is not None:
                at = pl.multiple_of(totals * self.plane + h * rows, 8)
                self.acc[pl.ds(at, rows), :] = part * self.series[0]
            masked = part * self.mask(kind, h, 0, rows)
            at = target * self.plane + h * rows
            for turn in (0, -1, 1):
                lanes = masked if turn == 0 else pltpu.roll(masked, 1 if turn < 0 else LANES - 1, 1)
                q[pl.ds(pl.multiple_of(self.moved(turn, at), 8), rows), :] = lanes

    def coefficient(self, row0, r, h):
        at = pl.multiple_of((r * 2 + h) * self.rows + row0, 8)
        return self.weights[pl.ds(at, ROWS), :]

    def places(self, segments, row0):
        found = []
        for segment in segments:
            own = segment.own * self.plane + row0
            target = segment.target * self.plane + row0
            totals = None if segment.totals is None else segment.totals * self.plane + row0
            shift = segment.source * self.plane + row0
            sources = [
                [self.offsets[self.which * 12 + r * 2 + h] + shift for h in range(2)]
                for r in range(REACTIONS)
            ]
            for u in range(segment.count):
                found.append((segment, u, own, target, totals, sources))
        return found

    def value(self, source, place, h, coefficients, firsts, rolled=None):
        segment, u, own, _, _, sources = place
        at = pl.multiple_of(own + u * self.plane + h * self.rows, 8)
        value = self.p[pl.ds(at, ROWS), :]
        if rolled is not None:
            value = jnp.where(self.never, rolled, value)
        value = value * self.stay[pl.ds(at, ROWS), :]
        terms = [value]
        for r in range(REACTIONS):
            arriving = source[pl.ds(sources[r][h] + u * self.plane, ROWS), :]
            term = arriving * coefficients(r, h)
            terms.append(term if r == 0 else term * firsts[r])
        while len(terms) > 1:
            pairs = [terms[i : i + 2] for i in range(0, len(terms), 2)]
            terms = [pair[0] + pair[1] if len(pair) == 2 else pair[0] for pair in pairs]
        return at, terms[0]

    def advance(self, k, source, target, blocks, layout, totals_by_layer=None):
        weight = self.series[k]
        plane, rows = self.plane, self.rows
        counts = [segment.count for segment in layout(0)]
        size = sum(counts)
        offsets = [(s, u) for s, count in enumerate(counts) for u in range(count)]
        lag = min(6, size // 2)

        def center_row(before, index, h):
            s, u = offsets[index]
            return before[s] + u * plane + h * rows

        def roll_layer(before, index):
            pairs = []
            for h in range(2):
                at = self.moved(0, center_row(before, index, h))
                values = target[pl.ds(pl.multiple_of(at, 8), ROWS), :]
                pairs.append((pltpu.roll(values, 1, 1), pltpu.roll(values, LANES - 1, 1)))
            return pairs

        def store_layer(before, index, pairs):
            for h in range(2):
                row = center_row(before, index, h)
                for side, turn in enumerate((-1, 1)):
                    at = pl.multiple_of(self.moved(turn, row), 8)
                    target[pl.ds(at, ROWS), :] = pairs[h][side]

        def group(g, before):
            row0 = pl.multiple_of(g * ROWS, ROWS)
            coefficients = functools.partial(self.coefficient, row0)

            def block(b, before):
                places = self.places(layout(b), row0)
                rolled = [roll_layer(before, index) for index in range(size)]
                stored = 0
                for index, place in enumerate(places):
                    segment, u, own, target0, totals0, _ = place
                    table = segment.table + u
                    kind = self.kind(table)
                    firsts = [None] + [self.first(table, r) for r in range(1, REACTIONS)]
                    ready = -1
                    if index >= lag:
                        ready = ((index - lag + 1) * size + size - lag - 1) // (size - lag) - 1
                    for h in range(2):
                        at, value = self.value(
                            source, place, h, coefficients, firsts,
                            rolled[ready][1][1] if ready >= 0 and h == 1 else None,
                        )
                        self.p[pl.ds(at, ROWS), :] = value
                        masked = value * self.mask(kind, h, row0, ROWS)
                        row = target0 + u * plane + h * rows
                        target[pl.ds(pl.multiple_of(self.moved(0, row), 8), ROWS), :] = masked
                        if totals_by_layer is None or totals_by_layer[index]:
                            at = pl.ds(pl.multiple_of(totals0 + u * plane + h * rows, 8), ROWS)
                            total = value * weight
                            if totals_by_layer is None or totals_by_layer[index] == "add":
                                total = total + self.acc[at, :]
                            self.acc[at, :] = total
                    while stored <= ready:
                        store_layer(before, stored, rolled[stored])
                        stored += 1
                while stored < size:
                    store_layer(before, stored, rolled[stored])
                    stored += 1
                return tuple(
                    pl.multiple_of(jnp.int32(segment.target * plane) + row0, 8)
                    for segment in layout(b)
                )

            return lax.fori_loop(0, blocks, block, before)

        before = tuple(jnp.int32(segment.target * plane) for segment in layout(jnp.int32(0)))
        last = lax.fori_loop(0, rows // ROWS, group, before)
        for index in range(size):
            store_layer(last, index, roll_layer(last, index))

    def finish(self, source, blocks, layout, more=None, fresh=None):
        weight_density = self.series[STEPS]
        weight_totals = self.series[STEPS + 1]

        def group(g, sums):
            row0 = pl.multiple_of(g * ROWS + HALO, 8)
            held = [[self.coefficient(row0, r, h) for h in range(2)] for r in range(REACTIONS)]

            def coefficients(r, h):
                return held[r][h]

            def block(b, sums):
                mass, hit = sums
                for index, place in enumerate(self.places(layout(b), row0)):
                    segment, u, _, _, totals0, _ = place
                    table = segment.table + u
                    kind = self.kind(table)
                    firsts = [None] + [self.first(table, r) for r in range(1, REACTIONS)]
                    for h in range(2):
                        _, value = self.value(source, place, h, coefficients, firsts)
                        row = pl.multiple_of(totals0 + u * self.plane + h * self.rows, 8)
                        so_far = (self.acc if more is None else more)[pl.ds(row, ROWS), :]
                        if more is not None and not fresh[index]:
                            so_far = so_far + self.acc[pl.ds(row, ROWS), :]
                        totals = so_far + value * weight_totals
                        mass = mass + totals
                        hit = hit + totals * (1.0 - self.mask(kind, h, row0, ROWS))
                        self.acc[pl.ds(row, ROWS), :] = so_far + value * weight_density
                return mass, hit

            return lax.fori_loop(0, blocks, block, sums)

        zero = jnp.zeros((ROWS, LANES), jnp.float32)
        return lax.fori_loop(0, (self.rows - 2 * HALO) // ROWS, group, (zero, zero))

    def restore(self, local, out, index, matrix):
        own = self.rows - 2 * HALO
        even = self.acc[pl.ds(pl.multiple_of(local * self.plane + HALO, 8), own), :]
        odd = self.acc[pl.ds(pl.multiple_of(local * self.plane + self.rows + HALO, 8), own), :]
        out[index] = split_product(jnp.concatenate([even, odd], axis=1), matrix)


def copy_all(copies):
    for copy in copies:
        copy.start()
    return copies


def wait_all(copies):
    for copy in copies:
        copy.wait()


def in_groups(count, limit, function):
    size = largest_divisor(count, limit)

    def several(g, carry):
        for i in range(size):
            function(g * size + i)
        return carry

    lax.fori_loop(0, count // size, several, 0)


def start_sends(axis, dim, source, stage, sems):
    odd = lax.axis_index(axis) & 1
    last = source.shape[dim] - HALO
    loads = []
    for i, start in enumerate(((1 - odd) * last, odd * last)):
        at = pl.ds(pl.multiple_of(start, HALO), HALO)
        piece = source.at[at] if dim == 0 else source.at[:, at]
        loads.append(pltpu.make_async_copy(piece, stage.at[i], sems.at[i]))
    return copy_all(loads)


def finish_sends(loads, stage, outs, sems):
    stores = []
    for i, out in enumerate(outs):
        loads[i].wait()
        stores.append(pltpu.make_async_copy(stage.at[i], out, sems.at[2 + i]))
        stores[-1].start()
    return stores


def sends_kernel(source, first, second, stage, sems):
    loads = start_sends("gy", 1, source, stage, sems)
    wait_all(finish_sends(loads, stage, (first, second), sems))


def interior_kernel(
    dims,
    density, first_side, second_side, stay_all, weights_all, free, offsets, series, firsts, kinds,
    occupancy, q_edges, p_edges, acc_edges, sums,
    p, acc, q0, q1, stay, block, staged, sem_in, sem_late, weights, sem_edges, sem_out,
):
    block_first, block_second, _, _ = dims
    rows = block_second + 2 * HALO
    plane = 2 * rows
    chunk = 8
    chunks = block_first // chunk
    even = (lax.axis_index("gy") & 1) == 0
    lattice = Lattice(
        rows, 0, (offsets, series, firsts, kinds), weights, free, stay, p, acc, block_first
    )
    loads = [
        pltpu.make_async_copy(
            density.at[pl.ds(c * chunk, chunk)], block.at[pl.ds(c * chunk, chunk)], sem_in.at[c]
        )
        for c in range(chunks)
    ]
    copy_all(loads)
    late = [
        pltpu.make_async_copy(
            stay_all.at[pl.ds(HALO * plane, block_first * plane)], stay, sem_late.at[0]
        ),
        pltpu.make_async_copy(weights_all, weights, sem_late.at[1]),
    ]
    copy_all(late)
    spread = parity_matrix(False)
    for c in range(chunks):
        loads[c].wait()

        def layer(i, c=c):
            local = c * chunk + i
            first, second = first_side[local], second_side[local]
            below = jnp.where(even, second, first)
            above = jnp.where(even, first, second)
            values = jnp.concatenate([below, block[local], above], axis=0)
            lattice.ingest(
                q0, split_product(values, spread), local, local + HALO, local, local
            )

        in_groups(chunk, 8, layer)
    wait_all(late)

    edges = []

    def export(k):
        q = (q0, q1)[k % 2]
        for side in range(2):
            layer = 2 * k if side == 0 else block_first - 2 * k - 4
            for turn in (-1, 0, 1):
                edges.append(
                    pltpu.make_async_copy(
                        q.at[pl.ds(lattice.moved(turn, layer * plane), 4 * plane)],
                        q_edges.at[k, side, turn + 1],
                        sem_edges.at[(k * 2 + side) * 4 + turn + 1],
                    )
                )
                edges[-1].start()
            layer = 2 * k if side == 0 else block_first - 2 * k - 2
            edges.append(
                pltpu.make_async_copy(
                    p.at[pl.ds(layer * plane, 2 * plane)],
                    p_edges.at[k, side],
                    sem_edges.at[(k * 2 + side) * 4 + 3],
                )
            )
            edges[-1].start()

    def layout_of(low, unroll):
        def layout(b):
            local = low + b * unroll
            return [Segment(unroll, local, local + HALO, local, local, local)]

        return layout

    export(0)
    for k in range(1, STEPS):
        low, high = 2 * k, block_first - 2 * k
        unroll = largest_divisor(high - low, BODY_LAYERS)
        lattice.advance(
            k, (q0, q1)[(k - 1) % 2], (q0, q1)[k % 2], (high - low) // unroll, layout_of(low, unroll)
        )
        export(k)
    for side in range(2):
        layer = 0 if side == 0 else block_first - HALO
        edges.append(
            pltpu.make_async_copy(
                acc.at[pl.ds(layer * plane, HALO * plane)], acc_edges.at[side], sem_edges.at[32 + side]
            )
        )
        edges[-1].start()
    inner = block_first - 2 * HALO
    unroll = largest_divisor(inner, 8)
    mass, hit = lattice.finish((q0, q1)[(STEPS - 1) % 2], inner // unroll, layout_of(HALO, unroll))
    sums[pl.ds(0, ROWS), :] = mass
    sums[pl.ds(ROWS, ROWS), :] = hit
    gather = parity_matrix(True)
    outs = []
    part = largest_divisor(inner, 8)
    for c in range(inner // part):
        in_groups(
            part, 4, lambda i, c=c: lattice.restore(HALO + c * part + i, staged, c * part + i, gather)
        )
        outs.append(
            pltpu.make_async_copy(
                staged.at[pl.ds(c * part, part)],
                occupancy.at[pl.ds(HALO + c * part, part)],
                sem_out.at[c],
            )
        )
        outs[-1].start()
    wait_all(outs)
    wait_all(edges)


SIDE = 2 * HALO + 2
SIDE_MOVED = HALO + 4


def edges_kernel(
    dims, devices,
    first_halo, second_halo, first_corner, second_corner, stay_all, q_edges, p_edges, acc_edges, sums_in,
    weights_all, free, offsets, series, firsts, kinds, occupancy_in,
    occupancy, row_out,
    p, acc, q0, q1, q2, q3, stay, earlier, weights, staged, sem_q, sem_p, sem_other, sem_out,
):
    block_first, block_second, extents, _ = dims
    rows = block_second + 2 * HALO
    plane = 2 * rows
    q = (q0, q1, q2, q3)
    right_table = block_first - 2
    lattice = Lattice(
        rows, 1, (offsets, series, firsts, kinds), weights, free, stay, p, acc, 2 * SIDE_MOVED
    )
    early, late, imports = [], [], []
    p_imports = [[] for _ in range(STEPS)]
    for side in range(2):
        for i, (first, count) in enumerate(
            ((2, HALO), (2 + HALO, HALO - 2)) if side == 0 else ((HALO, HALO), (2, HALO - 2))
        ):
            (early if i == 0 else p_imports[1]).append(
                pltpu.make_async_copy(
                    stay_all.at[pl.ds(((0, right_table)[side] + first) * plane, count * plane)],
                    stay.at[pl.ds((side * SIDE + first) * plane, count * plane)],
                    sem_other.at[(0, 5)[i] + side],
                )
            )
        late.append(
            pltpu.make_async_copy(
                acc_edges.at[side],
                earlier.at[pl.ds(side * HALO * plane, HALO * plane)],
                sem_other.at[2 + side],
            )
        )
        for k in range(STEPS):
            layer = 2 * k + HALO if side == 0 else SIDE + 8 - 2 * k
            p_imports[k].append(
                pltpu.make_async_copy(
                    p_edges.at[k, side], p.at[pl.ds(layer * plane, 2 * plane)], sem_p.at[k * 2 + side]
                )
            )
    for k in range(STEPS):
        imports.append([])
        for side in range(2):
            layer = HALO if side == 0 else SIDE_MOVED
            for turn in (-1, 0, 1):
                imports[k].append(
                    pltpu.make_async_copy(
                        q_edges.at[k, side, turn + 1],
                        q[k].at[pl.ds(lattice.moved(turn, layer * plane), 4 * plane)],
                        sem_q.at[(k * 2 + side) * 3 + turn + 1],
                    )
                )
    early.append(pltpu.make_async_copy(weights_all, weights, sem_other.at[4]))
    copy_all(imports[0] + early + p_imports[0])
    spread = parity_matrix(False)
    even = (lax.axis_index("gx") & 1) == 0
    for side in range(2):

        def layer(i, side=side):
            take_first = even if side == 1 else ~even
            corner = jnp.where(take_first, first_corner[i], second_corner[i])
            main = jnp.where(take_first, first_halo[i], second_halo[i])
            values = jnp.concatenate([corner[:HALO], main, corner[HALO:]], axis=0)
            lattice.ingest(
                q0,
                split_product(values, spread),
                i if side == 0 else SIDE + 10 + i,
                i if side == 0 else block_first + HALO + i,
                i if side == 0 else SIDE_MOVED + 4 + i,
                None,
            )

        in_groups(HALO, 4, layer)
    wait_all(early)

    def layout_of(k):
        def layout(b):
            return [
                Segment(HALO, 2 * k, 2 * k, 2, 0, 2 * k - HALO),
                Segment(
                    HALO, SIDE + 10 - 2 * k, block_first + HALO - 2 * k,
                    SIDE_MOVED + 2, SIDE_MOVED + 4, 2 * HALO - 2 * k,
                ),
            ]

        return layout

    for k in range(1, STEPS):
        wait_all(imports[k - 1] + p_imports[k - 1])
        copy_all(imports[k] + p_imports[k])
        if k == STEPS - 1:
            copy_all(late)
        own = [
            None if u < HALO - 2 * k else "new" if u >= HALO - 2 else "add" for u in range(HALO)
        ]
        own += own[::-1]
        lattice.advance(k, q[k - 1], q[k], 1, layout_of(k), own)
    wait_all(imports[STEPS - 1] + p_imports[STEPS - 1] + late)
    fresh = [u >= HALO - 2 for u in range(HALO)]
    mass, hit = lattice.finish(q[STEPS - 1], 1, layout_of(STEPS), earlier, fresh + fresh[::-1])
    gather = parity_matrix(True)
    outs = []
    for side in range(2):
        in_groups(
            HALO,
            4,
            lambda i, side=side: lattice.restore(side * HALO + i, staged, side * HALO + i, gather),
        )
        outs.append(
            pltpu.make_async_copy(
                staged.at[pl.ds(side * HALO, HALO)],
                occupancy.at[pl.ds(0 if side == 0 else block_first - HALO, HALO)],
                sem_out.at[side],
            )
        )
        outs[-1].start()
    share = 1.0 / math.prod(extents)
    mass = jnp.sum(mass + sums_in[pl.ds(0, ROWS), :]) * share
    hit = jnp.sum(hit + sums_in[pl.ds(ROWS, ROWS), :]) * share
    lane = lax.broadcasted_iota(jnp.int32, (devices, LANES), 1)
    row_out[...] = jnp.where(lane == 0, hit, jnp.where(lane == 1, mass, 0.0))
    wait_all(outs)


def body(density, reaction_rates, state_changes, target_box, truncation):
    block_first, block_second, species_third = density.shape
    extents = (
        block_first * lax.axis_size("gx"),
        block_second * lax.axis_size("gy"),
        species_third,
    )
    count_first, count_second = lax.axis_size("gx"), lax.axis_size("gy")
    devices = count_first * count_second
    rows = block_second + 2 * HALO
    plane = 2 * rows
    layers = block_first + 2 * HALO
    dims = (block_first, block_second, extents, (block_first, 2 * SIDE_MOVED))

    def exchange(pieces, axis, count):
        received = []
        for start, piece in enumerate(pieces):
            pairs = [(i, i + 1) for i in range(start, count - 1, 2)]
            received.append(lax.ppermute(piece, axis, pairs + [(j, i) for i, j in pairs]))
        return received

    f32 = jnp.float32
    smem = pl.BlockSpec(memory_space=pltpu.SMEM)
    vmem = pl.BlockSpec(memory_space=pltpu.VMEM)
    hbm = pl.BlockSpec(memory_space=pl.ANY)
    params = pltpu.CompilerParams(vmem_limit_bytes=VMEM_LIMIT)
    heavy = pl.CostEstimate(flops=200_000_000_000, bytes_accessed=400_000_000, transcendentals=0)
    light = pl.CostEstimate(flops=1000, bytes_accessed=1000, transcendentals=0)
    side_shape = (block_first, HALO, species_third)
    halo_shape = (HALO, block_second, species_third)
    side_sends = pl.pallas_call(
        sends_kernel,
        out_shape=(jax.ShapeDtypeStruct(side_shape, f32),) * 2,
        in_specs=[hbm],
        out_specs=(hbm,) * 2,
        scratch_shapes=[pltpu.VMEM((2,) + side_shape, f32), pltpu.SemaphoreType.DMA((4,))],
        compiler_params=params,
        cost_estimate=light,
        name="sends",
    )(density)
    first_side, second_side = exchange(side_sends, "gy", count_second)

    table_lanes = -(-(layers + 2 * ABOVE) // LANES) * LANES
    stay, weights, free, *tables, first_send, second_send = pl.pallas_call(
        functools.partial(tables_kernel, dims),
        out_shape=(
            jax.ShapeDtypeStruct((layers * plane, LANES), f32),
            jax.ShapeDtypeStruct((12 * rows, LANES), f32),
            jax.ShapeDtypeStruct((6 * rows, LANES), f32),
            jax.ShapeDtypeStruct((24,), jnp.int32),
            jax.ShapeDtypeStruct((STEPS + 2,), f32),
            jax.ShapeDtypeStruct((8, table_lanes), f32),
            jax.ShapeDtypeStruct((8, table_lanes), jnp.int32),
            jax.ShapeDtypeStruct(halo_shape, f32),
            jax.ShapeDtypeStruct(halo_shape, f32),
        ),
        in_specs=[smem] * 4 + [hbm, hbm],
        out_specs=(hbm, vmem, vmem, smem, smem, vmem, vmem, hbm, hbm),
        scratch_shapes=[
            pltpu.VMEM((layers * plane, LANES), f32),
            pltpu.VMEM((2,) + halo_shape, f32),
            pltpu.SemaphoreType.DMA((layers // largest_divisor(layers, 8),)),
            pltpu.SemaphoreType.DMA((4,)),
        ],
        compiler_params=params,
        cost_estimate=light,
        name="tables",
    )(reaction_rates, state_changes.T, target_box, truncation, density, side_sends[0])
    first_halo, second_halo = exchange((first_send, second_send), "gx", count_first)
    offsets = tables[0]

    corner = jax.ShapeDtypeStruct((HALO, 2 * HALO, species_third), f32)
    odd = jnp.where(tables[0][0] < -(10**9), 0, lax.axis_index("gx") & 1)
    swapped = (lax.axis_index("gy") & 1) == 0
    lower = jnp.where(swapped, second_side, first_side)
    upper = jnp.where(swapped, first_side, second_side)
    corner_sends = [
        jnp.concatenate(
            [lax.dynamic_slice_in_dim(x, start, HALO, axis=0) for x in (lower, upper)], axis=1
        )
        for start in ((1 - odd) * (block_first - HALO), odd * (block_first - HALO))
    ]
    first_corner, second_corner = exchange(corner_sends, "gx", count_first)

    def scratch(own, totals, moved, steps):
        return (
            [pltpu.VMEM((own * plane, LANES), f32), pltpu.VMEM((totals * plane, LANES), f32)]
            + [pltpu.VMEM((3 * moved * plane + 2 * PAD, LANES), f32) for _ in range(steps)]
            + [pltpu.VMEM((own * plane, LANES), f32)]
        )

    chunks = block_first // 8
    occupancy, q_edges, p_edges, acc_edges, sums = pl.pallas_call(
        functools.partial(interior_kernel, dims),
        out_shape=(
            jax.ShapeDtypeStruct(density.shape, f32),
            jax.ShapeDtypeStruct((STEPS, 2, 3, 4 * plane, LANES), f32),
            jax.ShapeDtypeStruct((STEPS, 2, 2 * plane, LANES), f32),
            jax.ShapeDtypeStruct((2, HALO * plane, LANES), f32),
            jax.ShapeDtypeStruct((2 * ROWS, LANES), f32),
        ),
        in_specs=[hbm, vmem, vmem, hbm, hbm, vmem] + [smem] * 4,
        out_specs=(hbm, hbm, hbm, hbm, vmem),
        scratch_shapes=scratch(block_first, block_first, block_first, 2)
        + [
            pltpu.VMEM((block_first, block_second, species_third), f32),
            pltpu.VMEM((block_first - 2 * HALO, block_second, species_third), f32),
            pltpu.SemaphoreType.DMA((chunks,)),
            pltpu.SemaphoreType.DMA((2,)),
            pltpu.VMEM((12 * rows, LANES), f32),
            pltpu.SemaphoreType.DMA((34,)),
            pltpu.SemaphoreType.DMA((block_first // HALO,)),
        ],
        compiler_params=params,
        cost_estimate=heavy,
        name="interior",
    )(density, first_side, second_side, stay, weights, free, *tables)

    occupancy, row = pl.pallas_call(
        functools.partial(edges_kernel, dims, devices),
        out_shape=(
            jax.ShapeDtypeStruct(density.shape, f32),
            jax.ShapeDtypeStruct((devices, LANES), f32),
        ),
        in_specs=[vmem] * 4 + [hbm] * 4 + [vmem, hbm, vmem] + [smem] * 4 + [hbm],
        out_specs=(hbm, vmem),
        scratch_shapes=scratch(2 * SIDE, 2 * HALO, 2 * SIDE_MOVED, STEPS)
        + [
            pltpu.VMEM((2 * HALO * plane, LANES), f32),
            pltpu.VMEM((12 * rows, LANES), f32),
            pltpu.VMEM((2 * HALO, block_second, species_third), f32),
            pltpu.SemaphoreType.DMA((24,)),
            pltpu.SemaphoreType.DMA((8,)),
            pltpu.SemaphoreType.DMA((7,)),
            pltpu.SemaphoreType.DMA((2,)),
        ],
        input_output_aliases={15: 0},
        compiler_params=params,
        name="edges",
    )(
        first_halo, second_halo, first_corner, second_corner, stay, q_edges, p_edges, acc_edges, sums,
        weights, free, *tables, occupancy,
    )
    rows_in = lax.all_to_all(row, ("gx", "gy"), 0, 0, tiled=True)
    summary = jnp.sum(rows_in[:, :2], axis=0)
    return occupancy, summary


def solution(mesh):
    placed = (P("gx", "gy", None), P(), P(), P(), P())
    return jax.shard_map(
        body, mesh=mesh, in_specs=placed, out_specs=(P("gx", "gy", None), P()), check_vma=False
    )
```
